32 devices in a mesh: dp: 4 (over y, x), seq: 8 (over z, core).
Axes of the slice: x: 2, y: 2, z: 4, core: 2. Of those that a mesh axis runs over, the one named last changes fastest.
Arguments:
- frames_in: bfloat16 [8, 16, 144, 1152], P('dp', 'seq'), may hold values from -36 to 36
- modulation: float32 [8, 6, 1152], P('dp'), may hold values from -3 to 3
- spatial_qkv: bfloat16 [1152, 3456], replicated, may hold values from -0.8249579 to 0.8249579
- spatial_out: bfloat16 [1152, 1152], replicated, may hold values from -0.1875 to 0.1875
- temporal_qkv: bfloat16 [1152, 3456], replicated, may hold values from -0.8249579 to 0.8249579
- temporal_out: bfloat16 [1152, 1152], replicated, may hold values from -0.1875 to 0.1875
- cotangent: bfloat16 [8, 16, 144, 1152], P('dp', 'seq'), may hold values from -6 to 6
Outputs:
- block_out: bfloat16 [8, 16, 144, 1152], P('dp', 'seq')
- grad_input: bfloat16 [8, 16, 144, 1152], P('dp', 'seq')
- grad_spatial_qkv: bfloat16 [1152, 3456], P(('dp', 'seq'))
- grad_spatial_out: bfloat16 [1152, 1152], P(('dp', 'seq'))
- grad_temporal_qkv: bfloat16 [1152, 3456], P(('dp', 'seq'))
- grad_temporal_out: bfloat16 [1152, 1152], P(('dp', 'seq'))
The draws below stay inside these ranges and needn't reach their ends.
All inputs are finite; a program needn't handle non-finite values.
Results may differ from the reference program's by a relative error of at most 0.02.
Values may be sent and summed in bfloat16 or wider, within the bound.
No kernel may reach another device: no remote copies, remote signals or barrier semaphores. Data moves between devices by JAX's collectives and lax.ppermute only.
A program may use at most 192 MiB of HBM per device.

```python
import math
import jax
import jax.numpy as jnp
from jax import lax

HEADS = 16
D = 1152
FRAMES = 16
PATCHES = 144
VID_DEV = 2
VIDEOS = 8
TOKENS = 18432
N_DP = 4
N_SEQ = 8


def projection_draw(key, top_gain):
    query_key, noise_key, value_key, gain_key = jax.random.split(key, 4)
    base_query = jnp.clip(jax.random.normal(query_key, (D, D), jnp.float32), -4.0, 4.0)
    noise_part = jnp.clip(jax.random.normal(noise_key, (D, D), jnp.float32), -4.0, 4.0)
    base_value = jnp.clip(jax.random.normal(value_key, (D, D), jnp.float32), -4.0, 4.0)
    head_gain = jnp.exp(jax.random.uniform(gain_key, (HEADS,), jnp.float32, 0.0, math.log(top_gain)))
    column_gain = jnp.repeat(head_gain, D // HEADS)
    key_part = noise_part
    joined = jnp.concatenate([base_query * column_gain, key_part * column_gain, base_value], 1)
    return (joined * D ** (-0.5)).astype(jnp.bfloat16)


def draw_frames_in(key, part):
    key = jax.random.fold_in(key, 11)
    base_key, row_key, chan_key = jax.random.split(key, 3)
    shape_all = (VIDEOS, FRAMES, PATCHES, D)
    row_scale = jnp.exp(jax.random.uniform(row_key, (VIDEOS, FRAMES, PATCHES, 1), jnp.float32, -1.2, 1.1))
    chan_scale = jnp.exp(jax.random.uniform(chan_key, (D,), jnp.float32, -1.2, 1.1))
    base = jnp.clip(jax.random.normal(base_key, shape_all, jnp.float32), -4.0, 4.0)
    return (base * row_scale * chan_scale).astype(jnp.bfloat16)


def draw_spatial_qkv(key, part):
    key = jax.random.fold_in(key, 21)
    return projection_draw(key, 1.0)


def draw_temporal_qkv(key, part):
    key = jax.random.fold_in(key, 31)
    return projection_draw(key, 1.0)


def steps_of(rng, shape, cuts, low, high):
    gain = 1.0
    for position, blocks in cuts:
        steps = jax.random.uniform(jax.random.fold_in(jax.random.fold_in(rng, 6), position), (blocks,), jnp.float32, low / len(cuts), high / len(cuts))
        gain = gain * jnp.repeat(jnp.exp(steps), shape[position] // blocks).reshape((-1,) + (1,) * (len(shape) - 1 - position))
    return gain


def noise(rng, extent, deviation, bound, shards=(), held_as=jnp.bfloat16):
    drawn = deviation * jax.random.normal(rng, extent, jnp.float32)
    if shards:
        drawn = drawn * steps_of(rng, extent, shards, -0.22, 0.18)
    return jnp.clip(drawn, -bound, bound).astype(held_as)


def setup_inputs(seed: int = 0) -> dict:
    keys = jax.random.split(jax.random.key(seed), 8)
    frames_in = draw_frames_in(jax.random.fold_in(keys[7], 71), 0)
    modulation = noise(keys[1], (VIDEOS, 6, D), 0.5, 3.0, ((0, 4),), jnp.float32)
    spatial_qkv = draw_spatial_qkv(jax.random.fold_in(keys[7], 71), 0)
    spatial_out = noise(keys[3], (D, D), D ** -0.5, 0.1875)
    temporal_qkv = draw_temporal_qkv(jax.random.fold_in(keys[7], 71), 0)
    temporal_out = noise(keys[5], (D, D), D ** -0.5, 0.1875)
    cotangent = noise(keys[6], (VIDEOS, FRAMES, PATCHES, D), 1.0, 6.0, ((0, 4), (1, 8)))
    return {"frames_in": frames_in, "modulation": modulation, "spatial_qkv": spatial_qkv, "spatial_out": spatial_out, "temporal_qkv": temporal_qkv, "temporal_out": temporal_out, "cotangent": cotangent}


NORM_EPSILON = 1e-06

def heads_view(values):
    return values.reshape(values.shape[:-1] + (HEADS, values.shape[-1] // HEADS))

def attend(queries, key_in, value_in, attend_axis):
    factor = queries.shape[-1] ** (-0.5)
    if attend_axis == 'space':
        scores = jnp.einsum('vfpne,vfqne->vfnpq', queries.astype(jnp.float32), key_in.astype(jnp.float32)) * factor
    else:
        scores = jnp.einsum('vfpne,vgpne->vpnfg', queries.astype(jnp.float32), key_in.astype(jnp.float32)) * factor
    softmax_out = jax.nn.softmax(scores, axis=-1)
    weights = softmax_out.astype(jnp.bfloat16)
    if attend_axis == 'space':
        mixed_heads = jnp.einsum('vfnpq,vfqne->vfpne', weights.astype(jnp.float32), value_in.astype(jnp.float32))
    else:
        mixed_heads = jnp.einsum('vpnfg,vgpne->vfpne', weights.astype(jnp.float32), value_in.astype(jnp.float32))
    return (softmax_out, weights, mixed_heads)

def branch_forward(tokens_in, shift, scale, gate, w_qkv, w_out, attend_axis):
    values = tokens_in.astype(jnp.float32)
    row_mean = lax.optimization_barrier(jnp.mean(values, -1, keepdims=True))
    centred = values - row_mean
    inverse = lax.rsqrt(lax.optimization_barrier(jnp.mean(centred * centred, -1, keepdims=True)) + NORM_EPSILON)
    normed = centred * inverse
    modded = (normed * (1.0 + scale) + shift).astype(jnp.bfloat16)
    packed = jnp.dot(modded, w_qkv, preferred_element_type=jnp.float32).astype(jnp.bfloat16)
    model_width = w_out.shape[0]
    queries = heads_view(packed[..., :model_width])
    key_in = heads_view(packed[..., model_width:2 * model_width])
    value_in = heads_view(packed[..., 2 * model_width:])
    softmax_out, weights, mixed_heads = attend(queries, key_in, value_in, attend_axis)
    attended = mixed_heads.reshape(tokens_in.shape).astype(jnp.bfloat16)
    projected = jnp.dot(attended, w_out, preferred_element_type=jnp.float32)
    result = (values + gate * projected).astype(jnp.bfloat16)
    saved = (normed, inverse, modded, queries, key_in, value_in, softmax_out, weights, attended)
    return (result, saved)

def branch_backward(saved, scale, gate, w_qkv, w_out, attend_axis, upstream):
    normed, inverse, modded, queries, key_in, value_in, softmax_out, weights, attended = saved
    incoming = upstream.astype(jnp.float32)
    scaled_grad = (gate * incoming).astype(jnp.bfloat16)
    d_attended = jnp.dot(scaled_grad, w_out.T, preferred_element_type=jnp.float32).astype(jnp.bfloat16)
    d_heads = heads_view(d_attended).astype(jnp.float32)
    factor = queries.shape[-1] ** (-0.5)
    weights_wide = weights.astype(jnp.float32)
    query_wide = queries.astype(jnp.float32)
    key_wide = key_in.astype(jnp.float32)
    value_wide = value_in.astype(jnp.float32)
    if attend_axis == 'space':
        d_value = jnp.einsum('vfnpq,vfpne->vfqne', weights_wide, d_heads)
        d_probs = jnp.einsum('vfpne,vfqne->vfnpq', d_heads, value_wide)
    else:
        d_value = jnp.einsum('vpnfg,vfpne->vgpne', weights_wide, d_heads)
        d_probs = jnp.einsum('vfpne,vgpne->vpnfg', d_heads, value_wide)
    d_scores = (softmax_out * (d_probs - lax.optimization_barrier(jnp.sum(softmax_out * d_probs, -1, keepdims=True))) * factor).astype(jnp.bfloat16)
    d_scores_wide = d_scores.astype(jnp.float32)
    if attend_axis == 'space':
        d_query = jnp.einsum('vfnpq,vfqne->vfpne', d_scores_wide, key_wide)
        d_key = jnp.einsum('vfnpq,vfpne->vfqne', d_scores_wide, query_wide)
    else:
        d_query = jnp.einsum('vpnfg,vgpne->vfpne', d_scores_wide, key_wide)
        d_key = jnp.einsum('vpnfg,vfpne->vgpne', d_scores_wide, query_wide)
    shape_out = upstream.shape
    d_packed = jnp.concatenate([d_query.reshape(shape_out), d_key.reshape(shape_out), d_value.reshape(shape_out)], -1).astype(jnp.bfloat16)
    d_modded = jnp.dot(d_packed, w_qkv.T, preferred_element_type=jnp.float32)
    d_normed = d_modded * (1.0 + scale)
    d_tokens = inverse * (d_normed - lax.optimization_barrier(jnp.mean(d_normed, -1, keepdims=True)) - normed * lax.optimization_barrier(jnp.mean(d_normed * normed, -1, keepdims=True)))
    result = (incoming + d_tokens).astype(jnp.bfloat16)
    return (result, ((modded, d_packed), (attended, scaled_grad)))

def reference(frames_in, modulation, spatial_qkv, spatial_out, temporal_qkv, temporal_out, cotangent):
    grad_scale = TOKENS ** (-0.5)
    frame_rows = FRAMES // N_SEQ
    patch_rows = PATCHES // N_SEQ

    def grouped(left_rows, right_rows, dim, rows_each):

        def add_term(index_now, running):
            start = jnp.asarray(index_now * rows_each).astype(jnp.int32)
            left_part = lax.dynamic_slice_in_dim(left_rows, start, rows_each, dim)
            right_part = lax.dynamic_slice_in_dim(right_rows, start, rows_each, dim)
            one_term = jnp.einsum('vfpd,vfpc->dc', left_part.astype(jnp.float32), right_part.astype(jnp.float32)) * grad_scale
            rounded = lax.optimization_barrier(one_term.astype(jnp.bfloat16))
            return running + rounded.astype(jnp.float32)
        empty = jnp.zeros((left_rows.shape[-1], right_rows.shape[-1]), jnp.float32)
        return lax.fori_loop(0, N_SEQ, add_term, empty)

    def group_pass(running, inputs):
        block_in, mod_block, cot_block = inputs
        mod_rows = mod_block[:, :, None, None, :]
        middle, saved_space = branch_forward(block_in, mod_rows[:, 0], mod_rows[:, 1], mod_rows[:, 2], spatial_qkv, spatial_out, 'space')
        block_out, saved_time = branch_forward(middle, mod_rows[:, 3], mod_rows[:, 4], mod_rows[:, 5], temporal_qkv, temporal_out, 'time')
        d_middle, time_terms = branch_backward(saved_time, mod_rows[:, 4], mod_rows[:, 5], temporal_qkv, temporal_out, 'time', cot_block)
        grad_input, space_terms = branch_backward(saved_space, mod_rows[:, 1], mod_rows[:, 2], spatial_qkv, spatial_out, 'space', d_middle)
        added = (grouped(space_terms[0][0], space_terms[0][1], 1, frame_rows), grouped(space_terms[1][0], space_terms[1][1], 1, frame_rows), grouped(time_terms[0][0], time_terms[0][1], 2, patch_rows), grouped(time_terms[1][0], time_terms[1][1], 2, patch_rows))
        return (jax.tree.map(jnp.add, running, added), (block_out, grad_input))
    start_sums = (jnp.zeros((D, 3 * D), jnp.float32), jnp.zeros((D, D), jnp.float32), jnp.zeros((D, 3 * D), jnp.float32), jnp.zeros((D, D), jnp.float32))
    inputs = (frames_in.reshape(N_DP, VID_DEV, FRAMES, PATCHES, D), modulation.reshape(N_DP, VID_DEV, 6, D), cotangent.reshape(N_DP, VID_DEV, FRAMES, PATCHES, D))
    sums, outputs = lax.scan(group_pass, start_sums, inputs)
    block_out = outputs[0].reshape(VIDEOS, FRAMES, PATCHES, D)
    grad_input = outputs[1].reshape(VIDEOS, FRAMES, PATCHES, D)
    return (block_out, grad_input, sums[0].astype(jnp.bfloat16), sums[1].astype(jnp.bfloat16), sums[2].astype(jnp.bfloat16), sums[3].astype(jnp.bfloat16))
```

```python
import functools

import jax
import jax.numpy as jnp
import numpy as np
from jax import lax
from jax.experimental import pallas as pl
from jax.experimental.pallas import tpu as pltpu
from jax.sharding import PartitionSpec as P

HEADS = 16
NORM_EPSILON = 1e-06
MASKED = -1e30
VMEM_LIMIT = 60 * 1024 * 1024
F32 = jnp.float32
BF16 = jnp.bfloat16

NN = (((1,), (0,)), ((), ()))
NT = (((1,), (1,)), ((), ()))
TN = (((0,), (0,)), ((), ()))


def dot(left, right, dims=NN):
    return lax.dot_general(left, right, dims, preferred_element_type=F32)


def call(body, out_shape, n_in, scratch=(), smem=()):
    specs = [
        pl.BlockSpec(memory_space=pltpu.SMEM if i in smem else pltpu.VMEM) for i in range(n_in)
    ]
    return pl.pallas_call(
        body,
        out_shape=out_shape,
        in_specs=specs,
        out_specs=jax.tree.map(lambda _: pl.BlockSpec(memory_space=pltpu.VMEM), out_shape),
        scratch_shapes=list(scratch),
        compiler_params=pltpu.CompilerParams(vmem_limit_bytes=VMEM_LIMIT),
    )


def shaped(*shape, dtype=BF16):
    return jax.ShapeDtypeStruct(shape, dtype)


def norm_stats(values):
    mean = jnp.mean(values, -1, keepdims=True)
    centred = values - mean
    inverse = lax.rsqrt(jnp.mean(centred * centred, -1, keepdims=True) + NORM_EPSILON)
    return centred * inverse, inverse


def norm_backward(d_modded, normed, inverse, scale):
    e = d_modded * (1.0 + scale)
    return inverse * (
        e
        - jnp.mean(e, -1, keepdims=True)
        - normed * jnp.mean(e * normed, -1, keepdims=True)
    )


def windows(width):
    size = width // HEADS
    found = []
    for head in range(HEADS):
        start = head * size // 128 * 128
        offset = head * size - start
        found.append((start, 128 * pl.cdiv(offset + size, 128), offset))
    return found


def head_mask(rows, span, offset, size):
    lane = lax.broadcasted_iota(jnp.int32, (rows, span), 1)
    return (lane >= offset) & (lane < offset + size)


def probs_by_key(query, key, head, factor, keep):
    scores = dot(jnp.where(head, key, jnp.zeros_like(key)), query, NT) * factor
    if keep is not None:
        scores = jnp.where(keep, scores, MASKED)
    raised = jnp.exp(scores - jnp.max(scores, 0, keepdims=True))
    return raised * (1.0 / jnp.sum(raised, 0, keepdims=True))


def d_scores_by_key(probs, d_out, value, head, factor):
    d_probs = dot(jnp.where(head, value, jnp.zeros_like(value)), d_out, NT)
    total = jnp.sum(probs * d_probs, 0, keepdims=True)
    return (probs * (d_probs - total) * factor).astype(BF16)


def put(ref, rows, start, span, head, value):
    at = (pl.ds(rows, head.shape[0]), pl.ds(start, span))
    ref[at] = jnp.where(head, value.astype(BF16), ref[at])


def frame_rows(pieces):
    n, rows, width = pieces.shape
    return pieces.astype(F32).reshape(n * rows, width).astype(BF16)


def piece_rows(values, n):
    return values.reshape(n, values.shape[0] // n, values.shape[1]).astype(BF16)


def split_kernel(n, x_ref, scatter_ref, out_ref):
    out_ref[...] = piece_rows(dot(scatter_ref[...], x_ref[...]), n)


def join_kernel(in_ref, gather_ref, out_ref):
    out_ref[...] = dot(gather_ref[...], frame_rows(in_ref[...])).astype(BF16)


def space_forward_kernel(
    n, block, x_ref, mod_ref, wqkv_ref, wout_ref, scatter_ref, sent_ref, packed_ref, modded_ref,
    attended_ref,
):
    width = x_ref.shape[1]
    size = width // HEADS
    factor = size ** (-0.5)
    x = x_ref[...].astype(F32)
    normed, _ = norm_stats(x)
    modded_ref[...] = (normed * (1.0 + mod_ref[1:2, :]) + mod_ref[0:1, :]).astype(BF16)
    for part in range(3):
        at = pl.ds(part * width, width)
        packed_ref[:, at] = dot(modded_ref[...], wqkv_ref[:, at]).astype(BF16)

    def one_block(g, carry):
        rows = pl.multiple_of(g * block, 16)
        for start, span, offset in windows(width):
            head = head_mask(block, span, offset, size)
            at = pl.ds(rows, block)
            query = packed_ref[at, pl.ds(start, span)]
            key = packed_ref[at, pl.ds(width + start, span)]
            value = packed_ref[at, pl.ds(2 * width + start, span)]
            weights = probs_by_key(query, key, head, factor, None).astype(BF16)
            put(attended_ref, rows, start, span, head, dot(weights, value, TN))
        return carry

    lax.fori_loop(0, x_ref.shape[0] // block, one_block, 0)
    projected = dot(attended_ref[...], wout_ref[...])
    middle = (x_ref[...].astype(F32) + mod_ref[2:3, :] * projected).astype(BF16)
    sent_ref[...] = piece_rows(dot(scatter_ref[...], middle), n)


def write_units(core, width, modded_ref, attended_ref, grad_ref, d_packed_ref, own_ref, sent_ref):
    sent_ref[:, 0:width] = modded_ref[...]
    sent_ref[:, width : 2 * width] = attended_ref[...]

    @pl.when(core == 0)
    def _():
        own_ref[...] = d_packed_ref[:, 0 : 2 * width]
        sent_ref[:, 2 * width : 3 * width] = d_packed_ref[:, 2 * width :]
        sent_ref[:, 3 * width :] = grad_ref[...]

    @pl.when(core != 0)
    def _():
        own_ref[:, 0:width] = d_packed_ref[:, 2 * width :]
        own_ref[:, width:] = grad_ref[...]
        sent_ref[:, 2 * width :] = d_packed_ref[:, 0 : 2 * width]


def time_kernel(
    n, block, span_frames, core_ref, middle_ref, cot_ref, mod_ref, wqkv_ref, wout_ref, gather_ref,
    scatter_ref, block_out_ref, d_middle_ref, own_ref, sent_ref,
    x_ref, up_ref, modded_ref, packed_ref, d_out_ref, attended_ref, grad_ref, d_packed_ref,
):
    width = wout_ref.shape[0]
    size = width // HEADS
    factor = size ** (-0.5)
    x_ref[...] = dot(gather_ref[...], frame_rows(middle_ref[...]))
    up_ref[...] = dot(gather_ref[...], frame_rows(cot_ref[...]))
    normed, _ = norm_stats(x_ref[...])
    modded_ref[...] = (normed * (1.0 + mod_ref[4:5, :]) + mod_ref[3:4, :]).astype(BF16)
    for part in range(3):
        at = pl.ds(part * width, width)
        packed_ref[:, at] = dot(modded_ref[...], wqkv_ref[:, at]).astype(BF16)
    grad_ref[...] = (mod_ref[5:6, :] * up_ref[...]).astype(BF16)
    d_out_ref[...] = dot(grad_ref[...], wout_ref[...], NT).astype(BF16)

    def one_block(g, carry):
        rows = pl.multiple_of(g * block, 16)
        left = lax.broadcasted_iota(jnp.int32, (block, block), 0) // span_frames
        right = lax.broadcasted_iota(jnp.int32, (block, block), 1) // span_frames
        keep = left == right
        for start, span, offset in windows(width):
            head = head_mask(block, span, offset, size)
            at = pl.ds(rows, block)
            query = packed_ref[at, pl.ds(start, span)]
            key = packed_ref[at, pl.ds(width + start, span)]
            value = packed_ref[at, pl.ds(2 * width + start, span)]
            d_out = d_out_ref[at, pl.ds(start, span)]
            probs = probs_by_key(query, key, head, factor, keep)
            weights = probs.astype(BF16)
            put(attended_ref, rows, start, span, head, dot(weights, value, TN))
            d_scores = d_scores_by_key(probs, d_out, value, head, factor)
            put(d_packed_ref, rows, start, span, head, dot(d_scores, key, TN))
            put(d_packed_ref, rows, width + start, span, head, dot(d_scores, query))
            put(d_packed_ref, rows, 2 * width + start, span, head, dot(weights, d_out))
        return carry

    lax.fori_loop(0, x_ref.shape[0] // block, one_block, 0)
    projected = dot(attended_ref[...], wout_ref[...])
    out = (x_ref[...] + mod_ref[5:6, :] * projected).astype(BF16)
    block_out_ref[...] = piece_rows(dot(scatter_ref[...], out), n)
    d_modded = dot(d_packed_ref[...], wqkv_ref[...], NT)
    normed, inverse = norm_stats(x_ref[...])
    d_middle = up_ref[...] + norm_backward(d_modded, normed, inverse, mod_ref[4:5, :])
    d_middle_ref[...] = piece_rows(dot(scatter_ref[...], d_middle.astype(BF16)), n)
    write_units(
        core_ref[0], width, modded_ref, attended_ref, grad_ref, d_packed_ref, own_ref, sent_ref
    )


def space_backward_kernel(
    block, core_ref, up_ref, mod_ref, wout_ref, gather_ref, packed_ref, modded_ref, attended_ref,
    d_middle_ref, d_packed_ref, own_ref, sent_ref,
    d_out_ref, grad_ref,
):
    width = wout_ref.shape[0]
    size = width // HEADS
    factor = size ** (-0.5)
    up = dot(gather_ref[...], frame_rows(up_ref[...]))
    d_middle_ref[...] = up.astype(BF16)
    grad_ref[...] = (mod_ref[2:3, :] * up).astype(BF16)
    d_out_ref[...] = dot(grad_ref[...], wout_ref[...], NT).astype(BF16)

    def one_block(g, carry):
        rows = pl.multiple_of(g * block, 16)
        for start, span, offset in windows(width):
            head = head_mask(block, span, offset, size)
            at = pl.ds(rows, block)
            query = packed_ref[at, pl.ds(start, span)]
            key = packed_ref[at, pl.ds(width + start, span)]
            value = packed_ref[at, pl.ds(2 * width + start, span)]
            d_out = d_out_ref[at, pl.ds(start, span)]
            probs = probs_by_key(query, key, head, factor, None)
            weights = probs.astype(BF16)
            d_scores = d_scores_by_key(probs, d_out, value, head, factor)
            put(d_packed_ref, rows, start, span, head, dot(d_scores, key, TN))
            put(d_packed_ref, rows, width + start, span, head, dot(d_scores, query))
            put(d_packed_ref, rows, 2 * width + start, span, head, dot(weights, d_out))
        return carry

    lax.fori_loop(0, grad_ref.shape[0] // block, one_block, 0)
    write_units(
        core_ref[0], width, modded_ref, attended_ref, grad_ref, d_packed_ref, own_ref, sent_ref
    )


def grad_input_kernel(d_packed_ref, d_middle_ref, x_ref, mod_ref, wqkv_ref, out_ref):
    d_modded = dot(d_packed_ref[...], wqkv_ref[...], NT)
    normed, inverse = norm_stats(x_ref[...].astype(F32))
    d_tokens = norm_backward(d_modded, normed, inverse, mod_ref[1:2, :])
    out_ref[...] = (d_middle_ref[...].astype(F32) + d_tokens).astype(BF16)


def weight_kernel(videos, grad_scale, core_ref, *refs):
    own, sent, got = refs[:videos], refs[videos : 2 * videos], refs[2 * videos : 3 * videos]
    first_ref, second_ref = refs[3 * videos :]
    width = first_ref.shape[0]

    def total(left_at, own_at, got_at):
        parts = [dot(s[:, left_at], o[:, own_at], TN) for s, o in zip(sent, own)]
        parts += [dot(g[:, left_at], g[:, got_at], TN) for g in got]
        return (sum(parts[1:], parts[0]) * grad_scale).astype(BF16)

    first_ref[...] = total(
        slice(0, width), slice(0, width), slice(2 * width, 3 * width)
    )

    @pl.when(core_ref[0] == 0)
    def _():
        second_ref[...] = total(
            slice(0, width), slice(width, 2 * width), slice(3 * width, 4 * width)
        )

    @pl.when(core_ref[0] != 0)
    def _():
        second_ref[...] = total(
            slice(width, 2 * width), slice(width, 2 * width), slice(3 * width, 4 * width)
        )


def swap(x, axis, mask):
    size = lax.axis_size(axis)
    return lax.ppermute(x, axis, [(i, i ^ mask) for i in range(size)])


def halve(blocks, dim, axis, bit):
    mine = (lax.axis_index(axis) >> bit) & 1
    kept = lax.dynamic_index_in_dim(blocks, mine, dim, False)
    sent = lax.dynamic_index_in_dim(blocks, 1 - mine, dim, False)
    got = swap(sent, axis, 1 << bit)
    return (kept.astype(F32) + got.astype(F32)).astype(BF16)


def reduce_unit(unit, dp_bits_first):
    dp_bits = lax.axis_size("dp").bit_length() - 1
    seq_bits = lax.axis_size("seq").bit_length() - 1
    bits = [2] * (dp_bits + seq_bits - 1)
    blocks = unit.reshape(bits + [unit.shape[0] >> len(bits), unit.shape[1]])
    left = list(range(dp_bits - 1, -1, -1)) + [10 + b for b in range(seq_bits - 1, 0, -1)]
    for bit in dp_bits_first(range(dp_bits)):
        dim = left.index(bit)
        blocks = halve(blocks, dim, "dp", bit)
        left.pop(dim)
    for bit in range(1, seq_bits):
        dim = left.index(10 + bit)
        blocks = halve(blocks, dim, "seq", bit)
        left.pop(dim)
    return blocks


def reduce_units(first, second):
    core = lax.axis_index("seq") & 1
    one = reduce_unit(first, list)
    two = reduce_unit(second, lambda bits: list(bits)[::-1])
    rows = one.shape[0] // 2
    both = jnp.stack([one, two]).reshape(2, 2, rows, one.shape[1])
    kept = lax.dynamic_index_in_dim(both, core, 1, False)
    got = swap(lax.dynamic_index_in_dim(both, 1 - core, 1, False), "seq", 1)
    at_zero = core == 0
    low = jnp.where(at_zero, kept, got)
    high = jnp.where(at_zero, got, kept)
    return jnp.concatenate([low[0], low[1], high[0]], 1), high[1]


def shards(frames_in, modulation, spatial_qkv, spatial_out, temporal_qkv, temporal_out, cotangent):
    n = lax.axis_size("seq")
    videos, frames, patches, width = frames_in.shape
    all_frames = frames * n
    tokens = frames * patches
    block = patches
    own_patches = patches // n
    rows = frames * own_patches
    padded = -(-rows // 8) * 8
    core = (lax.axis_index("seq") & 1).astype(jnp.int32).reshape(1)

    to_pieces = np.zeros((n * padded, tokens), np.float32)
    for device in range(n):
        for f in range(frames):
            for p in range(own_patches):
                to_pieces[device * padded + f * own_patches + p, f * patches + device * own_patches + p] = 1
    by_patch = np.zeros((tokens, n * padded), np.float32)
    for device in range(n):
        for f in range(frames):
            for p in range(own_patches):
                by_patch[p * all_frames + device * frames + f, device * padded + f * own_patches + p] = 1
    to_pieces, from_pieces = jnp.asarray(to_pieces, BF16), jnp.asarray(to_pieces.T, BF16)
    by_patch, from_patch = jnp.asarray(by_patch, BF16), jnp.asarray(by_patch.T, BF16)

    def exchange(pieces):
        return lax.all_to_all(pieces, "seq", split_axis=0, concat_axis=0, tiled=True)

    piece = shaped(n, padded, width)
    row = shaped(tokens, width)
    three = shaped(tokens, 3 * width)
    unit_own, unit_sent = shaped(tokens, 2 * width), shaped(tokens, 4 * width)

    def vmem(*shape, dtype=BF16):
        return pltpu.VMEM(shape, dtype)

    x = [frames_in[v].reshape(tokens, width) for v in range(videos)]
    cot = [cotangent[v].reshape(tokens, width) for v in range(videos)]
    mod = [modulation[v] for v in range(videos)]

    split = call(functools.partial(split_kernel, n), piece, 2)
    join = call(join_kernel, row, 2)
    space_forward = call(
        functools.partial(space_forward_kernel, n, block), (piece, three, row, row), 5
    )
    time = call(
        functools.partial(time_kernel, n, block, all_frames),
        (piece, piece, unit_own, unit_sent),
        8,
        [
            vmem(tokens, width, dtype=F32), vmem(tokens, width, dtype=F32), vmem(tokens, width),
            vmem(tokens, 3 * width), vmem(tokens, width), vmem(tokens, width),
            vmem(tokens, width), vmem(tokens, 3 * width),
        ],
        smem=(0,),
    )
    space_backward = call(
        functools.partial(space_backward_kernel, block),
        (row, three, unit_own, unit_sent),
        8,
        [vmem(tokens, width), vmem(tokens, width)],
        smem=(0,),
    )
    grad_input_call = call(grad_input_kernel, row, 5)
    grad_scale = (videos * lax.axis_size("dp") * all_frames * patches) ** (-0.5)
    weight = call(
        functools.partial(weight_kernel, videos, grad_scale),
        (shaped(width, width), shaped(width, width)),
        1 + 3 * videos,
        smem=(0,),
    )

    cot_pieces = [exchange(split(cot[v], to_pieces)) for v in range(videos)]
    saved = []
    middle_pieces = []
    for v in range(videos):
        sent, packed, modded, attended = space_forward(
            x[v], mod[v], spatial_qkv, spatial_out, to_pieces
        )
        middle_pieces.append(exchange(sent))
        saved.append((packed, modded, attended))

    def units(results):
        own = [r[0] for r in results]
        sent = [r[1] for r in results]
        got = [swap(s, "seq", 1) for s in sent]
        return weight(core, *own, *sent, *got)

    d_pieces = []
    out_pieces = []
    time_units = []
    for v in range(videos):
        out, d_middle, own, sent = time(
            core, middle_pieces[v], cot_pieces[v], mod[v], temporal_qkv, temporal_out, by_patch,
            from_patch,
        )
        d_pieces.append(exchange(d_middle))
        out_pieces.append(exchange(out))
        time_units.append((own, sent))
    grad_time = reduce_units(*units(time_units))

    grad_input = []
    space_units = []
    for v in range(videos):
        d_middle, d_packed, own, sent = space_backward(
            core, d_pieces[v], mod[v], spatial_out, from_pieces, *saved[v]
        )
        space_units.append((own, sent))
        grad_input.append(grad_input_call(d_packed, d_middle, x[v], mod[v], spatial_qkv))
    grad_space = reduce_units(*units(space_units))
    block_out = [join(p, from_pieces) for p in out_pieces]

    def whole(parts):
        return jnp.stack(parts).reshape(frames_in.shape)

    return (whole(block_out), whole(grad_input), *grad_space, *grad_time)


def solution(mesh):
    return jax.shard_map(
        shards,
        mesh=mesh,
        in_specs=(
            P("dp", "seq", None, None),
            P("dp", None, None),
            P(),
            P(),
            P(),
            P(),
            P("dp", "seq", None, None),
        ),
        out_specs=(
            P("dp", "seq", None, None),
            P("dp", "seq", None, None),
            P(("dp", "seq"), None),
            P(("dp", "seq"), None),
            P(("dp", "seq"), None),
            P(("dp", "seq"), None),
        ),
        check_vma=False,
    )
```

```python
import functools

import jax
import jax.numpy as jnp
import numpy as np
from jax import lax
from jax.experimental import pallas as pl
from jax.experimental.pallas import tpu as pltpu
from jax.sharding import PartitionSpec as P

HEADS = 16
NORM_EPSILON = 1e-06
MASKED = -1e30
LOG2_E = 1.4426950408889634
MIB = 1024 * 1024
F32 = jnp.float32
BF16 = jnp.bfloat16

NN = (((1,), (0,)), ((), ()))
NT = (((1,), (1,)), ((), ()))
TN = (((0,), (0,)), ((), ()))


def dot(left, right, dims=NN):
    return lax.dot_general(left, right, dims, preferred_element_type=F32)


SPACES = {"v": pltpu.VMEM, "s": pltpu.SMEM, "a": pl.ANY}


def call(name, us, body, ins, out_shape, outs, scratch=()):
    def run(*operands, deps=()):
        return pl.pallas_call(
            body,
            out_shape=out_shape,
            in_specs=[pl.BlockSpec(memory_space=SPACES[s]) for s in ins + "a" * len(deps)],
            out_specs=(
                tuple(pl.BlockSpec(memory_space=SPACES[s]) for s in outs)
                if isinstance(out_shape, tuple)
                else pl.BlockSpec(memory_space=SPACES[outs])
            ),
            scratch_shapes=list(scratch),
            compiler_params=pltpu.CompilerParams(vmem_limit_bytes=(56 if us > 4 else 16) * MIB),
            cost_estimate=pl.CostEstimate(
                flops=int(us * 1e9), transcendentals=0, bytes_accessed=int(us * 1e6)
            ),
            name=name,
        )(*operands, *deps)

    return run


def shaped(*shape, dtype=BF16):
    return jax.ShapeDtypeStruct(shape, dtype)


def norm_stats(values):
    mean = jnp.mean(values, -1, keepdims=True)
    centred = values - mean
    inverse = lax.rsqrt(jnp.mean(centred * centred, -1, keepdims=True) + NORM_EPSILON)
    return centred * inverse, inverse


def norm_backward(d_modded, normed, inverse, scale):
    e = d_modded * (1.0 + scale)
    return inverse * (
        e
        - jnp.mean(e, -1, keepdims=True)
        - normed * jnp.mean(e * normed, -1, keepdims=True)
    )


def pair_windows(width):
    size = 2 * width // HEADS
    found = []
    for pair in range(HEADS // 2):
        start = pair * size // 128 * 128
        offset = pair * size - start
        found.append((start, 128 * pl.cdiv(offset + size, 128), offset))
    return found


def pair_masks(rows, span, offset, size):
    lane = lax.broadcasted_iota(jnp.int32, (rows, span), 1)
    first = (lane >= offset) & (lane < offset + size)
    both = (lane >= offset) & (lane < offset + 2 * size)
    return first, both


def two_heads(values, first, both):
    zero = jnp.zeros_like(values)
    return jnp.concatenate(
        [jnp.where(first, values, zero), jnp.where(both & ~first, values, zero)], 0
    )


def per_query(by_key, other, first):
    out = dot(by_key, other, TN)
    rows = out.shape[0] // 2
    return jnp.where(first, out[:rows], out[rows:])


def probs_by_key(queries, key, factor, keep):
    scores = dot(key, queries, NT)
    if keep is not None:
        scores = jnp.where(keep, scores, MASKED)
    raised = jnp.exp2((scores - jnp.max(scores, 0, keepdims=True)) * (factor * LOG2_E))
    return raised * (1.0 / jnp.sum(raised, 0, keepdims=True))


def put(ref, rows, start, both, value):
    at = (pl.ds(rows, both.shape[0]), pl.ds(start, both.shape[1]))
    ref[at] = jnp.where(both, value.astype(BF16), ref[at])


def frame_rows(pieces):
    n, rows, width = pieces.shape
    return pieces.astype(F32).reshape(n * rows, width).astype(BF16)


def piece_rows(values, n):
    return values.reshape(n, values.shape[0] // n, values.shape[1]).astype(BF16)


def same_video(rows, frames):
    left = lax.broadcasted_iota(jnp.int32, (rows, 2 * rows), 0) // frames
    column = lax.broadcasted_iota(jnp.int32, (rows, 2 * rows), 1)
    right = jnp.where(column >= rows, column - rows, column) // frames
    return left == right


class Copies:
    def __init__(self, sems):
        self.sems, self.used = sems, 0

    def start(self, source, target):
        copy = pltpu.make_async_copy(source, target, self.sems.at[self.used])
        self.used += 1
        copy.start()
        return copy


def qkv_loads(copies, wqkv_ref, wqkv, width):
    parts = [pl.ds(part * width, width) for part in range(3)]
    return [copies.start(wqkv_ref.at[:, at], wqkv.at[:, at]) for at in parts]


def project_qkv(modded, wqkv, loads, packed, width):
    for part, load in enumerate(loads):
        load.wait()
        at = pl.ds(part * width, width)
        packed[:, at] = dot(modded, wqkv[:, at]).astype(BF16)


def split_kernel(n, video, x_ref, scatter_ref, *refs):
    out_ref = refs[-1]
    out_ref[...] = piece_rows(dot(scatter_ref[...], x_ref[video]), n)


def join_kernel(videos, *refs):
    gather_ref, out_ref = refs[videos], refs[-1]
    for video in range(videos):
        out_ref[video] = dot(gather_ref[...], frame_rows(refs[video][...])).astype(BF16)


def space_forward_kernel(
    n, block, video, with_cot, x_ref, cot_ref, mod_ref, wqkv_ref, wout_ref, scatter_ref, *refs
):
    sent_ref, packed_out, modded_out, attended_out, weights_out = refs[-14:-9]
    x, cot, modded, packed, attended, weights, wqkv, wout, sems = refs[-9:]
    width = x.shape[1]
    size = width // HEADS
    factor = size ** (-0.5)
    copies = Copies(sems)
    load_x = copies.start(x_ref.at[video], x)
    load_qkv = qkv_loads(copies, wqkv_ref, wqkv, width)
    load_out = copies.start(wout_ref, wout)
    if with_cot:
        load_cot = copies.start(cot_ref.at[video], cot)
    load_x.wait()
    normed, _ = norm_stats(x[...].astype(F32))
    modded[...] = (normed * (1.0 + mod_ref[video, 1:2, :]) + mod_ref[video, 0:1, :]).astype(BF16)
    stores = [copies.start(modded, modded_out)]
    project_qkv(modded[...], wqkv, load_qkv, packed, width)
    stores.append(copies.start(packed, packed_out))
    pairs = pair_windows(width)

    def one_block(g, carry):
        rows = pl.multiple_of(g * block, 16)
        for pair, (start, span, offset) in enumerate(pairs):
            first, both = pair_masks(block, span, offset, size)
            at = pl.ds(rows, block)
            query = packed[at, pl.ds(start, span)]
            key = packed[at, pl.ds(width + start, span)]
            value = packed[at, pl.ds(2 * width + start, span)]
            probs = probs_by_key(two_heads(query, first, both), key, factor, None).astype(BF16)
            weights[g * len(pairs) + pair] = probs
            put(attended, rows, start, both, per_query(probs, value, first))
        return carry

    lax.fori_loop(0, x.shape[0] // block, one_block, 0)
    stores.append(copies.start(attended, attended_out))
    stores.append(copies.start(weights, weights_out))
    load_out.wait()
    projected = dot(attended[...], wout[...])
    middle = (x[...].astype(F32) + mod_ref[video, 2:3, :] * projected).astype(BF16)
    pieces = piece_rows(dot(scatter_ref[...], middle), n)
    if with_cot:
        load_cot.wait()
        padded = pieces.shape[1]
        sent_ref[:, :padded, :] = pieces
        sent_ref[:, padded:, :] = piece_rows(dot(scatter_ref[...], cot[...]), n)
    else:
        sent_ref[...] = pieces
    for store in stores:
        store.wait()


def unit_stores(copies, core, width, left, right, outs):
    *sent_outs, right_out = outs
    other = (1 - core) * (2 * width)
    sources = [left.at[:, pl.ds(unit * width, width)] for unit in range(2)]
    sources += [
        right.at[:, pl.ds(pl.multiple_of(other + unit * width, 128), width)] for unit in range(2)
    ]
    return [copies.start(source, out) for source, out in zip(sources, sent_outs)] + [
        copies.start(right, right_out)
    ]


def time_kernel(
    n, block, frames, video, merged, joint, core_ref, middle_ref, cot_ref, mod_ref, wqkv_ref,
    wout_ref, gather_ref, scatter_ref, *refs
):
    n_out = 6 if joint else 7
    outs, scratch = refs[-10 - n_out : -10], refs[-10:]
    normed, x, up, left, packed, d_out, right, wqkv, wout, sems = scratch
    width = x.shape[1]
    size = width // HEADS
    factor = size ** (-0.5)
    copies = Copies(sems)
    load_qkv = qkv_loads(copies, wqkv_ref, wqkv, width)
    load_out = copies.start(wout_ref, wout)
    gather = gather_ref[...]
    if merged:
        padded = middle_ref.shape[1] // 2
        middle, cot = middle_ref[:, :padded, :], middle_ref[:, padded:, :]
    else:
        middle, cot = middle_ref[...], cot_ref[...]
    x[...] = dot(gather, frame_rows(middle)).astype(BF16)
    up[...] = dot(gather, frame_rows(cot)).astype(BF16)
    normed_now, inverse = norm_stats(x[...].astype(F32))
    normed[...] = normed_now
    left[:, 0:width] = (
        normed_now * (1.0 + mod_ref[video, 4:5, :]) + mod_ref[video, 3:4, :]
    ).astype(BF16)
    right[:, 3 * width :] = (mod_ref[video, 5:6, :] * up[...].astype(F32)).astype(BF16)
    project_qkv(left[:, 0:width], wqkv, load_qkv, packed, width)
    load_out.wait()
    d_out[...] = dot(right[:, 3 * width :], wout[...], NT).astype(BF16)
    keep = same_video(block, frames)

    def one_block(g, carry):
        rows = pl.multiple_of(g * block, 16)
        for start, span, offset in pair_windows(width):
            first, both = pair_masks(block, span, offset, size)
            at = pl.ds(rows, block)
            query = two_heads(packed[at, pl.ds(start, span)], first, both)
            key = packed[at, pl.ds(width + start, span)]
            value = packed[at, pl.ds(2 * width + start, span)]
            d_rows = two_heads(d_out[at, pl.ds(start, span)], first, both)
            probs = probs_by_key(query, key, factor, keep)
            weights = probs.astype(BF16)
            put(left, rows, width + start, both, per_query(weights, value, first))
            d_probs = dot(value, d_rows, NT)
            total = jnp.sum(probs * d_probs, 0, keepdims=True)
            d_scores = (probs * (d_probs - total) * factor).astype(BF16)
            put(right, rows, start, both, per_query(d_scores, key, first))
            put(right, rows, width + start, both, dot(d_scores, query))
            put(right, rows, 2 * width + start, both, dot(weights, d_rows))
        return carry

    lax.fori_loop(0, x.shape[0] // block, one_block, 0)
    stores = unit_stores(copies, core_ref[1] & 1, width, left, right, outs[-5:])
    d_modded = dot(right[:, 0 : 3 * width], wqkv[...], NT)
    d_middle = up[...].astype(F32) + norm_backward(
        d_modded, normed[...], inverse, mod_ref[video, 4:5, :]
    )
    d_pieces = piece_rows(dot(scatter_ref[...], d_middle.astype(BF16)), n)
    projected = dot(left[:, width:], wout[...])
    out = (x[...].astype(F32) + mod_ref[video, 5:6, :] * projected).astype(BF16)
    if joint:
        padded = d_pieces.shape[1]
        outs[0][:, :padded, :] = d_pieces
        outs[0][:, padded:, :] = piece_rows(dot(scatter_ref[...], out), n)
    else:
        outs[0][...] = d_pieces
        outs[1][0] = out
    for store in stores:
        store.wait()


def space_backward_kernel(
    block, video, core_ref, up_ref, mod_ref, wout_ref, gather_ref, packed_ref, modded_ref,
    attended_ref, weights_ref, *refs
):
    d_middle_ref, *unit_outs = refs[-12:-6]
    d_out, left, right, packed, wout, sems = refs[-6:]
    width = wout.shape[0]
    size = width // HEADS
    factor = size ** (-0.5)
    copies = Copies(sems)
    load_out = copies.start(wout_ref, wout)
    load_packed = copies.start(packed_ref, packed)
    loads = [
        copies.start(modded_ref, left.at[:, pl.ds(0, width)]),
        copies.start(attended_ref, left.at[:, pl.ds(width, width)]),
    ]
    padded = gather_ref.shape[1] // up_ref.shape[0]
    up = dot(gather_ref[...], frame_rows(up_ref[:, :padded, :]))
    d_middle_ref[...] = up.astype(BF16)
    right[:, 3 * width :] = (mod_ref[video, 2:3, :] * up).astype(BF16)
    load_out.wait()
    d_out[...] = dot(right[:, 3 * width :], wout[...], NT).astype(BF16)
    load_packed.wait()
    pairs = pair_windows(width)

    def one_block(g, carry):
        rows = pl.multiple_of(g * block, 16)
        for pair, (start, span, offset) in enumerate(pairs):
            first, both = pair_masks(block, span, offset, size)
            at = pl.ds(rows, block)
            query = two_heads(packed[at, pl.ds(start, span)], first, both)
            key = packed[at, pl.ds(width + start, span)]
            value = packed[at, pl.ds(2 * width + start, span)]
            d_rows = two_heads(d_out[at, pl.ds(start, span)], first, both)
            weights = weights_ref[g * len(pairs) + pair]
            probs = weights.astype(F32)
            d_probs = dot(value, d_rows, NT)
            total = jnp.sum(probs * d_probs, 0, keepdims=True) / jnp.sum(probs, 0, keepdims=True)
            d_scores = (probs * (d_probs - total) * factor).astype(BF16)
            put(right, rows, start, both, per_query(d_scores, key, first))
            put(right, rows, width + start, both, dot(d_scores, query))
            put(right, rows, 2 * width + start, both, dot(weights, d_rows))
        return carry

    lax.fori_loop(0, d_out.shape[0] // block, one_block, 0)
    for load in loads:
        load.wait()
    for store in unit_stores(copies, core_ref[1] & 1, width, left, right, unit_outs):
        store.wait()


def grad_input_kernel(video, right_ref, d_middle_ref, x_ref, mod_ref, wqkv_ref, *refs):
    out_ref, d_packed, sems = refs[-3:]
    width = out_ref.shape[1]
    Copies(sems).start(right_ref.at[:, pl.ds(0, 3 * width)], d_packed).wait()
    d_modded = dot(d_packed[...], wqkv_ref[...], NT)
    normed, inverse = norm_stats(x_ref[video].astype(F32))
    d_tokens = norm_backward(d_modded, normed, inverse, mod_ref[video, 1:2, :])
    out_ref[...] = (d_middle_ref[...].astype(F32) + d_tokens).astype(BF16)


def bit_of(place_ref, axis, bit):
    return (place_ref[0 if axis == "dp" else 1] >> bit) & 1


def emit_halves(rows, inner, mine, kept_ref, sent_ref):
    for outer in range(kept_ref.shape[0]):
        low = rows[2 * outer * inner : (2 * outer + 1) * inner, :]
        high = rows[(2 * outer + 1) * inner : (2 * outer + 2) * inner, :]
        kept_ref[outer] = jnp.where(mine == 0, low, high).astype(BF16)
        sent_ref[outer] = jnp.where(mine == 0, high, low).astype(BF16)


def weight_kernel(videos, cuts, steps, grad_scale, place_ref, *refs):
    right, units = refs[:videos], refs[videos : 9 * videos]
    sent = [units[4 * v : 4 * v + 4] for v in range(videos)]
    got = [units[4 * v : 4 * v + 4] for v in range(videos, 2 * videos)]
    outs = refs[-4 - 2 * len(cuts) : -4]
    left_rows, right_rows, total, sems = refs[-4:]
    width = left_rows.shape[1] // 2
    tokens = right[0].shape[0]
    copies = Copies(sems)
    core = place_ref[1] & 1
    own = pl.multiple_of(core * (2 * width), 128)
    waits = []
    for unit in range(2):
        now = []
        for video in range(videos):
            for place, (left, mine) in enumerate(((sent[video], right[video]), (got[video], None))):
                rows = pl.ds((2 * video + place) * tokens, tokens)
                at = pl.ds(unit * width, width)
                now.append(copies.start(left[unit], left_rows.at[rows, at]))
                source = (
                    left[2 + unit]
                    if mine is None
                    else mine.at[:, pl.ds(pl.multiple_of(own + unit * width, 128), width)]
                )
                now.append(copies.start(source, right_rows.at[rows, at]))
        waits.append(now)
    done = 0
    for part, ((low, high), (axis, bit, inner)) in enumerate(zip(cuts, steps)):
        for unit in range(2):
            start, stop = max(low, unit * width), min(high, (unit + 1) * width)
            if start >= stop:
                continue
            while done <= unit:
                for wait in waits[done]:
                    wait.wait()
                done += 1
            column = pl.multiple_of(core * width, 128) if unit else 0
            left = left_rows[:, pl.ds(column, width)]
            total[:, start - low : stop - low] = (
                dot(left, right_rows[:, start:stop], TN) * grad_scale
            )
        emit_halves(
            total, inner, bit_of(place_ref, axis, bit), outs[2 * part], outs[2 * part + 1]
        )


def stage_kernel(steps, place_ref, *refs):
    count = len(steps)
    total, outs = refs[-1], refs[-1 - 2 * count : -1]
    for part, (axis, bit, inner) in enumerate(steps):
        kept, got = refs[part], refs[count + part]
        each = kept.shape[1]
        for outer in range(kept.shape[0]):
            total[outer * each : (outer + 1) * each, :] = kept[outer].astype(F32) + got[
                outer
            ].astype(F32)
        emit_halves(
            total, inner, bit_of(place_ref, axis, bit), outs[2 * part], outs[2 * part + 1]
        )


def core_stage_kernel(count, place_ref, *refs):
    kept_out, sent_out = refs[-2:]
    rows, columns = refs[0].shape[1:]
    core = place_ref[1] & 1
    for part in range(count):
        total = refs[part][0].astype(F32) + refs[count + part][0].astype(F32)
        low, high = total[: rows // 2], total[rows // 2 :]
        at = slice(part * columns, (part + 1) * columns)
        kept_out[:, at] = jnp.where(core == 0, low, high).astype(BF16)
        sent_out[:, at] = jnp.where(core == 0, high, low).astype(BF16)


def assemble_kernel(place_ref, kept_ref, got_ref, qkv_ref, out_ref):
    width = out_ref.shape[1]
    core = place_ref[1] & 1
    kept, got = kept_ref[...].astype(F32), got_ref[...].astype(F32)
    low = jnp.where(core == 0, kept, got).astype(BF16)
    high = jnp.where(core == 0, got, kept).astype(BF16)
    qkv_ref[:, : 2 * width] = low
    qkv_ref[:, 2 * width :] = high[:, :width]
    out_ref[...] = high[:, width:]


def swap(x, axis, mask):
    size = lax.axis_size(axis)
    return lax.ppermute(x, axis, [(i, i ^ mask) for i in range(size)])


class Reduction:
    def __init__(self, place, width):
        dp_bits = [("dp", bit) for bit in range(lax.axis_size("dp").bit_length() - 1)]
        seq_bits = [("seq", bit) for bit in range(1, lax.axis_size("seq").bit_length() - 1)]
        self.place, self.width, self.columns = place, width, 2 * width // 3
        self.cuts = tuple((part * self.columns, (part + 1) * self.columns) for part in range(3))
        self.orders = (
            dp_bits + seq_bits,
            dp_bits[-1:] + seq_bits[:1] + dp_bits[:-1] + seq_bits[1:],
            seq_bits[:1] + dp_bits + seq_bits[1:],
        )
        self.bits = dp_bits[::-1] + seq_bits[::-1]
        self.step = 0

    def next_steps(self):
        least = self.width >> len(self.bits)
        steps, shapes = [], []
        for order in self.orders:
            left = [bit for bit in self.bits if bit not in order[: self.step]]
            above = left.index(order[self.step])
            inner = least << (len(left) - above - 1)
            steps.append((*order[self.step], inner))
            shapes += 2 * [shaped(1 << above, inner, self.columns)]
        return tuple(steps), tuple(shapes)

    def send(self, halves):
        self.kept = halves[0::2]
        self.got = [
            swap(half, order[self.step][0], 1 << order[self.step][1])
            for half, order in zip(halves[1::2], self.orders)
        ]
        self.step += 1

    def stage(self, deps=()):
        steps, shapes = self.next_steps()
        halves = call(
            "stage", 2, functools.partial(stage_kernel, steps), "s" + "v" * 6, shapes, "v" * 6,
            [pltpu.VMEM((self.width >> self.step, self.columns), F32)],
        )(self.place, *self.kept, *self.got, deps=deps)
        self.send(halves)
        return halves[0]

    def finish(self):
        while self.step < len(self.bits):
            self.stage()
        rows = self.width >> (len(self.bits) + 1)
        half = shaped(rows, 2 * self.width)
        kept, sent = call(
            "core_stage", 1, functools.partial(core_stage_kernel, 3), "s" + "v" * 6, (half, half),
            "vv",
        )(self.place, *self.kept, *self.got)
        return call(
            "assemble", 1, assemble_kernel, "svv",
            (shaped(rows, 3 * self.width), shaped(rows, self.width)), "vv",
        )(self.place, kept, swap(sent, "seq", 1))


def shards(frames_in, modulation, spatial_qkv, spatial_out, temporal_qkv, temporal_out, cotangent):
    n = lax.axis_size("seq")
    videos, frames, patches, width = frames_in.shape
    all_frames = frames * n
    tokens = frames * patches
    own_patches = patches // n
    rows = frames * own_patches
    padded = -(-rows // 8) * 8
    time_block = 6 * all_frames if own_patches % 6 == 0 else 3 * all_frames
    core = jnp.stack([lax.axis_index("dp"), lax.axis_index("seq")]).astype(jnp.int32)

    to_pieces = np.zeros((n * padded, tokens), np.float32)
    by_patch = np.zeros((tokens, n * padded), np.float32)
    for device in range(n):
        for f in range(frames):
            for p in range(own_patches):
                place = device * padded + f * own_patches + p
                to_pieces[place, f * patches + device * own_patches + p] = 1
                by_patch[p * all_frames + device * frames + f, place] = 1
    to_pieces, from_pieces = jnp.asarray(to_pieces, BF16), jnp.asarray(to_pieces.T, BF16)
    by_patch, from_patch = jnp.asarray(by_patch, BF16), jnp.asarray(by_patch.T, BF16)

    def exchange(pieces):
        return lax.all_to_all(pieces, "seq", split_axis=0, concat_axis=0, tiled=True)

    piece = shaped(n, padded, width)
    piece_pair = shaped(n, 2 * padded, width)
    row = shaped(tokens, width)
    three, four = shaped(tokens, 3 * width), shaped(tokens, 4 * width)
    all_rows = shaped(videos, tokens, width)
    weights_shape = (frames * (HEADS // 2), patches, 2 * patches)

    def vmem(*shape, dtype=BF16):
        return pltpu.VMEM(shape, dtype)

    def sems(count):
        return pltpu.SemaphoreType.DMA((count,))

    weight_refs = [vmem(width, 3 * width), vmem(width, width)]
    x = frames_in.reshape(videos, tokens, width)
    cot = cotangent.reshape(videos, tokens, width)

    def split(values, video, matrix, deps=()):
        return call("split", 3, functools.partial(split_kernel, n, video), "vv", piece, "v")(
            values, matrix, deps=deps
        )

    cot_first = split(cot, 0, to_pieces)
    deps = [cot_first]
    saved, arrived = [], []
    for v in range(videos):
        sent, *keep = call(
            "space_forward", 14,
            functools.partial(space_forward_kernel, n, patches, v, v > 0),
            "aavaav",
            (piece_pair if v > 0 else piece, three, row, row, shaped(*weights_shape)),
            "vaaaa",
            [
                vmem(tokens, width), vmem(tokens, width), vmem(tokens, width),
                vmem(tokens, 3 * width), vmem(tokens, width), vmem(*weights_shape),
                *weight_refs, sems(10),
            ],
        )(x, cot, modulation, spatial_qkv, spatial_out, to_pieces, deps=deps)
        if v == 0:
            cot_pieces = exchange(cot_first)
            deps = [cot_pieces]
        else:
            deps = [sent]
        arrived.append(exchange(sent))
        saved.append(keep)

    def exchange_units(sent):
        return [swap(unit, "seq", 1) for unit in sent]

    returned, time_units = [], []
    last = videos - 1
    for v in range(videos):
        joint = v != last
        outs = call(
            "time", 25,
            functools.partial(time_kernel, n, time_block, all_frames, v, v > 0, joint),
            "svvvaavv",
            ((piece_pair,) if joint else (piece, shaped(1, tokens, width))) + 4 * (row,) + (four,),
            ("v" if joint else "vv") + "aaaaa",
            [
                vmem(tokens, width, dtype=F32), vmem(tokens, width), vmem(tokens, width),
                vmem(tokens, 2 * width), vmem(tokens, 3 * width), vmem(tokens, width),
                vmem(tokens, 4 * width), *weight_refs, sems(9),
            ],
        )(
            core, arrived[v], cot_pieces if v == 0 else core, modulation, temporal_qkv,
            temporal_out, by_patch, from_patch, deps=deps,
        )
        deps = [outs[-1]]
        returned.append(exchange(outs[0]))
        time_units.append((list(outs[-5:-1]), outs[-1], exchange_units(outs[-5:-1])))
    last_out = outs[1]

    grad_scale = (videos * lax.axis_size("dp") * all_frames * patches) ** (-0.5)

    def weights(units, deps=()):
        reduction = Reduction(core, width)
        steps, shapes = reduction.next_steps()
        sent, right, got = zip(*units)
        halves = call(
            "weights", 10,
            functools.partial(weight_kernel, videos, reduction.cuts, steps, grad_scale),
            "s" + "a" * (9 * videos), shapes, "v" * 6,
            [
                vmem(2 * videos * tokens, 2 * width), vmem(2 * videos * tokens, 2 * width),
                vmem(width, reduction.columns, dtype=F32), sems(8 * videos),
            ],
        )(core, *right, *sum(sent, []), *sum(got, []), deps=deps)
        reduction.send(halves)
        return reduction, halves[0]

    def grad_of(video, units, d_middle, deps=()):
        return call(
            "grad_input", 8, functools.partial(grad_input_kernel, video), "avvvv", row, "v",
            [vmem(tokens, 3 * width), sems(1)],
        )(units[1], d_middle, x, modulation, spatial_qkv, deps=deps)

    d_middles, space_units, grad_input = [], [], []
    for v in range(videos):
        d_middle, *sent, right = call(
            "space_backward", 15, functools.partial(space_backward_kernel, patches, v),
            "svvavaaav",
            (row,) + 4 * (row,) + (four,),
            "vaaaaa",
            [
                vmem(tokens, width), vmem(tokens, 2 * width), vmem(tokens, 4 * width),
                vmem(tokens, 3 * width), vmem(width, width), sems(9),
            ],
        )(
            core, returned[v], modulation, spatial_out, from_pieces, *saved[v], deps=deps
        )
        if v == 0:
            last_pieces = split(last_out, 0, from_patch, deps=[right])
            time_sum, began = weights(time_units, deps=[last_pieces])
            deps = [began]
            last_back = exchange(last_pieces)
        d_middles.append(d_middle)
        space_units.append((sent, right, exchange_units(sent)))
    began = time_sum.stage(deps=[right])
    space_sum, began = weights(space_units, deps=[began, last_back])
    began = time_sum.stage(deps=[began])
    for v in range(videos):
        grad_input.append(grad_of(v, space_units[v], d_middles[v], deps=[began]))
        began = grad_input[-1]
    began = space_sum.stage(deps=[began])
    out_pieces = [r[:, padded:, :] for r in returned[:-1]] + [last_back]
    block_out = call(
        "join", 4, functools.partial(join_kernel, videos), "v" * (videos + 1), all_rows, "v"
    )(*out_pieces, from_pieces, deps=[began])
    grad_input = jnp.stack(grad_input)
    grad_time, grad_space = time_sum.finish(), space_sum.finish()
    return (
        block_out.reshape(frames_in.shape), grad_input.reshape(frames_in.shape),
        *grad_space, *grad_time,
    )


def solution(mesh):
    return jax.shard_map(
        shards,
        mesh=mesh,
        in_specs=(
            P("dp", "seq", None, None),
            P("dp", None, None),
            P(),
            P(),
            P(),
            P(),
            P("dp", "seq", None, None),
        ),
        out_specs=(
            P("dp", "seq", None, None),
            P("dp", "seq", None, None),
            P(("dp", "seq"), None),
            P(("dp", "seq"), None),
            P(("dp", "seq"), None),
            P(("dp", "seq"), None),
        ),
        check_vma=False,
    )
```

```python
import functools

import jax
import jax.numpy as jnp
import numpy as np
from jax import lax
from jax.experimental import pallas as pl
from jax.experimental.pallas import tpu as pltpu
from jax.sharding import PartitionSpec as P

HEADS = 16
NORM_EPSILON = 1e-06
MASKED = -1e30
LOG2_E = 1.4426950408889634
MIB = 1024 * 1024
F32 = jnp.float32
BF16 = jnp.bfloat16

NN = (((1,), (0,)), ((), ()))
NT = (((1,), (1,)), ((), ()))
TN = (((0,), (0,)), ((), ()))


def dot(left, right, dims=NN):
    return lax.dot_general(left, right, dims, preferred_element_type=F32)


SPACES = {"v": pltpu.VMEM, "s": pltpu.SMEM, "a": pl.ANY}


def call(name, us, body, ins, out_shape, outs, scratch=()):
    def run(*operands, deps=()):
        return pl.pallas_call(
            body,
            out_shape=out_shape,
            in_specs=[pl.BlockSpec(memory_space=SPACES[s]) for s in ins + "a" * len(deps)],
            out_specs=(
                tuple(pl.BlockSpec(memory_space=SPACES[s]) for s in outs)
                if isinstance(out_shape, tuple)
                else pl.BlockSpec(memory_space=SPACES[outs])
            ),
            scratch_shapes=list(scratch),
            compiler_params=pltpu.CompilerParams(vmem_limit_bytes=(16 if us < 3 else 56) * MIB),
            cost_estimate=pl.CostEstimate(
                flops=int(us * 1e9), transcendentals=0, bytes_accessed=int(us * 1e6)
            ),
            name=name,
        )(*operands, *deps)

    return run


def shaped(*shape, dtype=BF16):
    return jax.ShapeDtypeStruct(shape, dtype)


def norm_stats(values):
    mean = jnp.mean(values, -1, keepdims=True)
    centred = values - mean
    inverse = lax.rsqrt(jnp.mean(centred * centred, -1, keepdims=True) + NORM_EPSILON)
    return centred * inverse, inverse


def norm_backward(d_modded, normed, inverse, scale):
    e = d_modded * (1.0 + scale)
    return inverse * (
        e
        - jnp.mean(e, -1, keepdims=True)
        - normed * jnp.mean(e * normed, -1, keepdims=True)
    )


def pair_windows(width):
    size = 2 * width // HEADS
    found = []
    for pair in range(HEADS // 2):
        start = pair * size // 128 * 128
        offset = pair * size - start
        found.append((start, 128 * pl.cdiv(offset + size, 128), offset))
    return found


def pair_masks(rows, span, offset, size):
    lane = lax.broadcasted_iota(jnp.int32, (rows, span), 1)
    first = (lane >= offset) & (lane < offset + size)
    both = (lane >= offset) & (lane < offset + 2 * size)
    return first, both


def two_heads(values, first, both):
    zero = jnp.zeros_like(values)
    return jnp.concatenate(
        [jnp.where(first, values, zero), jnp.where(both & ~first, values, zero)], 0
    )


def per_query(by_key, other, first):
    out = dot(by_key, other, TN)
    rows = out.shape[0] // 2
    return jnp.where(first, out[:rows], out[rows:])


def probs_by_key(queries, key, factor, keep):
    scores = dot(key, queries, NT)
    if keep is not None:
        scores = jnp.where(keep, scores, MASKED)
    raised = jnp.exp2((scores - jnp.max(scores, 0, keepdims=True)) * (factor * LOG2_E))
    return raised * (1.0 / jnp.sum(raised, 0, keepdims=True))


def put(ref, rows, start, both, value):
    at = (pl.ds(rows, both.shape[0]), pl.ds(start, both.shape[1]))
    ref[at] = jnp.where(both, value.astype(BF16), ref[at])


def frame_rows(pieces):
    n, rows, width = pieces.shape
    return pieces.astype(F32).reshape(n * rows, width).astype(BF16)


def piece_rows(values, n):
    return values.reshape(n, values.shape[0] // n, values.shape[1]).astype(BF16)


def same_video(rows, frames):
    left = lax.broadcasted_iota(jnp.int32, (rows, 2 * rows), 0) // frames
    column = lax.broadcasted_iota(jnp.int32, (rows, 2 * rows), 1)
    right = jnp.where(column >= rows, column - rows, column) // frames
    return left == right


class Copies:
    def __init__(self, sems):
        self.sems, self.used = sems, 0

    def start(self, source, target):
        copy = pltpu.make_async_copy(source, target, self.sems.at[self.used])
        self.used += 1
        copy.start()
        return copy


def qkv_loads(copies, wqkv_ref, wqkv, width):
    parts = [pl.ds(part * width, width) for part in range(3)]
    return [copies.start(wqkv_ref.at[:, at], wqkv.at[:, at]) for at in parts]


def project_qkv(modded, wqkv, loads, packed, width):
    for part, load in enumerate(loads):
        load.wait()
        at = pl.ds(part * width, width)
        packed[:, at] = dot(modded, wqkv[:, at]).astype(BF16)


def split_kernel(n, x_ref, scatter_ref, *refs):
    out_ref = refs[-1]
    rows = x_ref[...].reshape(scatter_ref.shape[1], x_ref.shape[-1])
    out_ref[...] = piece_rows(dot(scatter_ref[...], rows), n)


def split_rows_kernel(n, *refs):
    *row_refs, scatter_ref = refs[: len(refs) - 2]
    out_ref = refs[-1]
    rows = jnp.concatenate([ref[...] for ref in row_refs], 0)
    out_ref[...] = piece_rows(dot(scatter_ref[...], rows), n)


def join_kernel(pieces_ref, gather_ref, *refs):
    out_ref = refs[-1]
    rows = dot(gather_ref[...], frame_rows(pieces_ref[...])).astype(BF16)
    out_ref[...] = rows.reshape(out_ref.shape)


def space_forward_kernel(
    n, block, video, x_ref, mod_ref, wqkv_ref, wout_ref, scatter_ref, *refs
):
    sent_ref, packed_out, modded_out, attended_out, weights_out = refs[-13:-8]
    x, modded, packed, attended, weights, wqkv, wout, sems = refs[-8:]
    width = x.shape[1]
    size = width // HEADS
    factor = size ** (-0.5)
    copies = Copies(sems)
    load_x = copies.start(x_ref.at[video], x)
    load_qkv = qkv_loads(copies, wqkv_ref, wqkv, width)
    load_out = copies.start(wout_ref, wout)
    load_x.wait()
    normed, _ = norm_stats(x[...].astype(F32))
    modded[...] = (normed * (1.0 + mod_ref[video, 1:2, :]) + mod_ref[video, 0:1, :]).astype(BF16)
    stores = [copies.start(modded, modded_out)]
    project_qkv(modded[...], wqkv, load_qkv, packed, width)
    stores.append(copies.start(packed, packed_out))
    pairs = pair_windows(width)

    def one_block(g, carry):
        rows = pl.multiple_of(g * block, 16)
        for pair, (start, span, offset) in enumerate(pairs):
            first, both = pair_masks(block, span, offset, size)
            at = pl.ds(rows, block)
            query = packed[at, pl.ds(start, span)]
            key = packed[at, pl.ds(width + start, span)]
            value = packed[at, pl.ds(2 * width + start, span)]
            probs = probs_by_key(two_heads(query, first, both), key, factor, None).astype(BF16)
            weights[g * len(pairs) + pair] = probs
            put(attended, rows, start, both, per_query(probs, value, first))
        return carry

    lax.fori_loop(0, x.shape[0] // block, one_block, 0)
    stores.append(copies.start(attended, attended_out))
    stores.append(copies.start(weights, weights_out))
    load_out.wait()
    projected = dot(attended[...], wout[...])
    middle = (x[...].astype(F32) + mod_ref[video, 2:3, :] * projected).astype(BF16)
    sent_ref[...] = piece_rows(dot(scatter_ref[...], middle), n)
    for store in stores:
        store.wait()


def unit_stores(copies, core, width, left, right, outs):
    *sent_outs, right_out = outs
    other = (1 - core) * (2 * width)
    sources = [left.at[:, pl.ds(unit * width, width)] for unit in range(2)]
    sources += [
        right.at[:, pl.ds(pl.multiple_of(other + unit * width, 128), width)] for unit in range(2)
    ]
    return [copies.start(source, out) for source, out in zip(sources, sent_outs)] + [
        copies.start(right, right_out)
    ]


def time_kernel(
    n, block, frames, video, core_ref, middle_ref, cot_ref, mod_ref, wqkv_ref, wout_ref,
    gather_ref, gather_cot_ref, scatter_ref, *refs
):
    (d_middle_ref, block_out_ref, *unit_outs), scratch = refs[-17:-10], refs[-10:]
    normed, x, up, left, packed, d_out, right, wqkv, wout, sems = scratch
    width = x.shape[1]
    size = width // HEADS
    factor = size ** (-0.5)
    copies = Copies(sems)
    load_qkv = qkv_loads(copies, wqkv_ref, wqkv, width)
    load_out = copies.start(wout_ref, wout)
    x[...] = dot(gather_ref[...], frame_rows(middle_ref[...])).astype(BF16)
    up[...] = dot(gather_cot_ref[...], frame_rows(cot_ref[...])).astype(BF16)
    normed_now, inverse = norm_stats(x[...].astype(F32))
    normed[...] = normed_now
    left[:, 0:width] = (
        normed_now * (1.0 + mod_ref[video, 4:5, :]) + mod_ref[video, 3:4, :]
    ).astype(BF16)
    right[:, 3 * width :] = (mod_ref[video, 5:6, :] * up[...].astype(F32)).astype(BF16)
    project_qkv(left[:, 0:width], wqkv, load_qkv, packed, width)
    load_out.wait()
    d_out[...] = dot(right[:, 3 * width :], wout[...], NT).astype(BF16)
    keep = same_video(block, frames)

    def one_block(g, carry):
        rows = pl.multiple_of(g * block, 16)
        for start, span, offset in pair_windows(width):
            first, both = pair_masks(block, span, offset, size)
            at = pl.ds(rows, block)
            query = two_heads(packed[at, pl.ds(start, span)], first, both)
            key = packed[at, pl.ds(width + start, span)]
            value = packed[at, pl.ds(2 * width + start, span)]
            d_rows = two_heads(d_out[at, pl.ds(start, span)], first, both)
            probs = probs_by_key(query, key, factor, keep)
            weights = probs.astype(BF16)
            put(left, rows, width + start, both, per_query(weights, value, first))
            d_probs = dot(value, d_rows, NT)
            total = jnp.sum(probs * d_probs, 0, keepdims=True)
            d_scores = (probs * (d_probs - total) * factor).astype(BF16)
            put(right, rows, start, both, per_query(d_scores, key, first))
            put(right, rows, width + start, both, dot(d_scores, query))
            put(right, rows, 2 * width + start, both, dot(weights, d_rows))
        return carry

    lax.fori_loop(0, x.shape[0] // block, one_block, 0)
    stores = unit_stores(copies, core_ref[1] & 1, width, left, right, unit_outs)
    d_modded = dot(right[:, 0 : 3 * width], wqkv[...], NT)
    d_middle = up[...].astype(F32) + norm_backward(
        d_modded, normed[...], inverse, mod_ref[video, 4:5, :]
    )
    d_middle_ref[...] = piece_rows(dot(scatter_ref[...], d_middle.astype(BF16)), n)
    projected = dot(left[:, width:], wout[...])
    out = (x[...].astype(F32) + mod_ref[video, 5:6, :] * projected).astype(BF16)
    block_out_ref[...] = out
    for store in stores:
        store.wait()


def space_backward_kernel(
    block, video, core_ref, up_ref, mod_ref, wout_ref, gather_ref, packed_ref, modded_ref,
    attended_ref, weights_ref, *refs
):
    d_middle_ref, *unit_outs = refs[-12:-6]
    d_out, left, right, packed, wout, sems = refs[-6:]
    width = wout.shape[0]
    size = width // HEADS
    factor = size ** (-0.5)
    copies = Copies(sems)
    load_out = copies.start(wout_ref, wout)
    load_packed = copies.start(packed_ref, packed)
    loads = [
        copies.start(modded_ref, left.at[:, pl.ds(0, width)]),
        copies.start(attended_ref, left.at[:, pl.ds(width, width)]),
    ]
    up = dot(gather_ref[...], frame_rows(up_ref[...]))
    d_middle_ref[...] = up.astype(BF16)
    right[:, 3 * width :] = (mod_ref[video, 2:3, :] * up).astype(BF16)
    load_out.wait()
    d_out[...] = dot(right[:, 3 * width :], wout[...], NT).astype(BF16)
    load_packed.wait()
    pairs = pair_windows(width)

    def one_block(g, carry):
        rows = pl.multiple_of(g * block, 16)
        for pair, (start, span, offset) in enumerate(pairs):
            first, both = pair_masks(block, span, offset, size)
            at = pl.ds(rows, block)
            query = two_heads(packed[at, pl.ds(start, span)], first, both)
            key = packed[at, pl.ds(width + start, span)]
            value = packed[at, pl.ds(2 * width + start, span)]
            d_rows = two_heads(d_out[at, pl.ds(start, span)], first, both)
            weights = weights_ref[g * len(pairs) + pair]
            probs = weights.astype(F32)
            d_probs = dot(value, d_rows, NT)
            total = jnp.sum(probs * d_probs, 0, keepdims=True) / jnp.sum(probs, 0, keepdims=True)
            d_scores = (probs * (d_probs - total) * factor).astype(BF16)
            put(right, rows, start, both, per_query(d_scores, key, first))
            put(right, rows, width + start, both, dot(d_scores, query))
            put(right, rows, 2 * width + start, both, dot(weights, d_rows))
        return carry

    lax.fori_loop(0, d_out.shape[0] // block, one_block, 0)
    for load in loads:
        load.wait()
    for store in unit_stores(copies, core_ref[1] & 1, width, left, right, unit_outs):
        store.wait()


def grad_input_kernel(video, right_ref, d_middle_ref, x_ref, mod_ref, wqkv_ref, *refs):
    out_ref, d_packed, sems = refs[-3:]
    width = out_ref.shape[1]
    Copies(sems).start(right_ref.at[:, pl.ds(0, 3 * width)], d_packed).wait()
    d_modded = dot(d_packed[...], wqkv_ref[...], NT)
    normed, inverse = norm_stats(x_ref[video].astype(F32))
    d_tokens = norm_backward(d_modded, normed, inverse, mod_ref[video, 1:2, :])
    out_ref[...] = (d_middle_ref[...].astype(F32) + d_tokens).astype(BF16)


def bit_of(place_ref, axis, bit):
    return (place_ref[0 if axis == "dp" else 1] >> bit) & 1


def emit_halves(rows, inner, mine, kept_ref, sent_ref):
    for outer in range(kept_ref.shape[0]):
        low = rows[2 * outer * inner : (2 * outer + 1) * inner, :]
        high = rows[(2 * outer + 1) * inner : (2 * outer + 2) * inner, :]
        kept_ref[outer] = jnp.where(mine == 0, low, high).astype(BF16)
        sent_ref[outer] = jnp.where(mine == 0, high, low).astype(BF16)


def weight_kernel(videos, cuts, steps, grad_scale, place_ref, *refs):
    right, units = refs[:videos], refs[videos : 9 * videos]
    sent = [units[4 * v : 4 * v + 4] for v in range(videos)]
    got = [units[4 * v : 4 * v + 4] for v in range(videos, 2 * videos)]
    outs = refs[-4 - 2 * len(cuts) : -4]
    left_rows, right_rows, total, sems = refs[-4:]
    width = left_rows.shape[1] // 2
    tokens = right[0].shape[0]
    copies = Copies(sems)
    core = place_ref[1] & 1
    own = pl.multiple_of(core * (2 * width), 128)
    waits = []
    for unit in range(2):
        now = []
        for video in range(videos):
            for place, (left, mine) in enumerate(((sent[video], right[video]), (got[video], None))):
                rows = pl.ds((2 * video + place) * tokens, tokens)
                at = pl.ds(unit * width, width)
                now.append(copies.start(left[unit], left_rows.at[rows, at]))
                source = (
                    left[2 + unit]
                    if mine is None
                    else mine.at[:, pl.ds(pl.multiple_of(own + unit * width, 128), width)]
                )
                now.append(copies.start(source, right_rows.at[rows, at]))
        waits.append(now)
    done = 0
    for part, ((low, high), (axis, bit, inner)) in enumerate(zip(cuts, steps)):
        for unit in range(2):
            start, stop = max(low, unit * width), min(high, (unit + 1) * width)
            if start >= stop:
                continue
            while done <= unit:
                for wait in waits[done]:
                    wait.wait()
                done += 1
            column = pl.multiple_of(core * width, 128) if unit else 0
            left = left_rows[:, pl.ds(column, width)]
            total[:, start - low : stop - low] = (
                dot(left, right_rows[:, start:stop], TN) * grad_scale
            )
        emit_halves(
            total, inner, bit_of(place_ref, axis, bit), outs[2 * part], outs[2 * part + 1]
        )


def stage_kernel(steps, place_ref, *refs):
    count = len(steps)
    total, outs = refs[-1], refs[-1 - 2 * count : -1]
    for part, (axis, bit, inner) in enumerate(steps):
        kept, got = refs[part], refs[count + part]
        each = kept.shape[1]
        for outer in range(kept.shape[0]):
            total[outer * each : (outer + 1) * each, :] = kept[outer].astype(F32) + got[
                outer
            ].astype(F32)
        emit_halves(
            total, inner, bit_of(place_ref, axis, bit), outs[2 * part], outs[2 * part + 1]
        )


def core_stage_kernel(count, place_ref, *refs):
    kept_out, sent_out = refs[-2:]
    rows, columns = refs[0].shape[1:]
    core = place_ref[1] & 1
    for part in range(count):
        total = refs[part][0].astype(F32) + refs[count + part][0].astype(F32)
        low, high = total[: rows // 2], total[rows // 2 :]
        at = slice(part * columns, (part + 1) * columns)
        kept_out[:, at] = jnp.where(core == 0, low, high).astype(BF16)
        sent_out[:, at] = jnp.where(core == 0, high, low).astype(BF16)


def assemble_kernel(place_ref, kept_ref, got_ref, qkv_ref, out_ref):
    width = out_ref.shape[1]
    core = place_ref[1] & 1
    kept, got = kept_ref[...].astype(F32), got_ref[...].astype(F32)
    low = jnp.where(core == 0, kept, got).astype(BF16)
    high = jnp.where(core == 0, got, kept).astype(BF16)
    qkv_ref[:, : 2 * width] = low
    qkv_ref[:, 2 * width :] = high[:, :width]
    out_ref[...] = high[:, width:]


def swap(x, axis, mask):
    size = lax.axis_size(axis)
    return lax.ppermute(x, axis, [(i, i ^ mask) for i in range(size)])


class Reduction:
    def __init__(self, place, width, late):
        dp_bits = [("dp", bit) for bit in range(lax.axis_size("dp").bit_length() - 1)]
        seq_bits = [("seq", bit) for bit in range(1, lax.axis_size("seq").bit_length() - 1)]
        if late:
            self.orders = (
                dp_bits + seq_bits,
                dp_bits[-1:] + seq_bits[:1] + dp_bits[:-1] + seq_bits[1:],
                seq_bits[:1] + dp_bits + seq_bits[1:],
            )
        else:
            self.orders = (dp_bits + seq_bits, dp_bits[::-1] + seq_bits)
        self.parts = len(self.orders)
        self.place, self.width, self.columns = place, width, 2 * width // self.parts
        self.cuts = tuple(
            (part * self.columns, (part + 1) * self.columns) for part in range(self.parts)
        )
        self.bits = dp_bits[::-1] + seq_bits[::-1]
        self.step = 0

    def next_steps(self):
        least = self.width >> len(self.bits)
        steps, shapes = [], []
        for order in self.orders:
            left = [bit for bit in self.bits if bit not in order[: self.step]]
            above = left.index(order[self.step])
            inner = least << (len(left) - above - 1)
            steps.append((*order[self.step], inner))
            shapes += 2 * [shaped(1 << above, inner, self.columns)]
        return tuple(steps), tuple(shapes)

    def send(self, halves):
        self.kept = halves[0::2]
        self.got = [
            swap(half, order[self.step][0], 1 << order[self.step][1])
            for half, order in zip(halves[1::2], self.orders)
        ]
        self.step += 1

    def stage(self, deps=()):
        steps, shapes = self.next_steps()
        halves = call(
            "stage", 2, functools.partial(stage_kernel, steps), "s" + "v" * len(shapes), shapes,
            "v" * len(shapes),
            [pltpu.VMEM((self.width >> self.step, self.columns), F32)],
        )(self.place, *self.kept, *self.got, deps=deps)
        self.send(halves)
        return halves[0]

    def finish(self):
        while self.step < len(self.bits):
            self.stage()
        rows = self.width >> (len(self.bits) + 1)
        half = shaped(rows, 2 * self.width)
        kept, sent = call(
            "core_stage", 1, functools.partial(core_stage_kernel, self.parts),
            "s" + "v" * (2 * self.parts), (half, half), "vv",
        )(self.place, *self.kept, *self.got)
        return call(
            "assemble", 1, assemble_kernel, "svv",
            (shaped(rows, 3 * self.width), shaped(rows, self.width)), "vv",
        )(self.place, kept, swap(sent, "seq", 1))


def shards(frames_in, modulation, spatial_qkv, spatial_out, temporal_qkv, temporal_out, cotangent):
    n = lax.axis_size("seq")
    videos, frames, patches, width = frames_in.shape
    all_frames = frames * n
    tokens = frames * patches
    own_patches = patches // n
    rows = frames * own_patches
    padded = -(-rows // 8) * 8
    time_block = 6 * all_frames if own_patches % 6 == 0 else 3 * all_frames
    core = jnp.stack([lax.axis_index("dp"), lax.axis_index("seq")]).astype(jnp.int32)

    joint_padded = -(-videos * rows // 8) * 8
    to_pieces = np.zeros((n * padded, tokens), np.float32)
    to_joint = np.zeros((n * joint_padded, videos * tokens), np.float32)
    by_patch = np.zeros((tokens, n * padded), np.float32)
    joint_by_patch = np.zeros((videos, tokens, n * joint_padded), np.float32)
    for device in range(n):
        for f in range(frames):
            for p in range(own_patches):
                inside = f * own_patches + p
                before = f * patches + device * own_patches + p
                after = p * all_frames + device * frames + f
                to_pieces[device * padded + inside, before] = 1
                by_patch[after, device * padded + inside] = 1
                for v in range(videos):
                    place = device * joint_padded + v * rows + inside
                    to_joint[place, v * tokens + before] = 1
                    joint_by_patch[v, after, place] = 1
    joint_from_patch = np.concatenate(list(joint_by_patch), 0).T
    to_pieces, from_pieces = jnp.asarray(to_pieces, BF16), jnp.asarray(to_pieces.T, BF16)
    to_joint, from_joint = jnp.asarray(to_joint, BF16), jnp.asarray(to_joint.T, BF16)
    by_patch, from_patch = jnp.asarray(by_patch, BF16), jnp.asarray(by_patch.T, BF16)
    joint_by_patch = [jnp.asarray(m, BF16) for m in joint_by_patch]
    joint_from_patch = jnp.asarray(joint_from_patch, BF16)

    def exchange(pieces):
        return lax.all_to_all(pieces, "seq", split_axis=0, concat_axis=0, tiled=True)

    piece = shaped(n, padded, width)
    joint_piece = shaped(n, joint_padded, width)
    row = shaped(tokens, width)
    three, four = shaped(tokens, 3 * width), shaped(tokens, 4 * width)
    all_rows = shaped(videos, tokens, width)
    weights_shape = (frames * (HEADS // 2), patches, 2 * patches)

    def vmem(*shape, dtype=BF16):
        return pltpu.VMEM(shape, dtype)

    def sems(count):
        return pltpu.SemaphoreType.DMA((count,))

    weight_refs = [vmem(width, 3 * width), vmem(width, width)]
    x = frames_in.reshape(videos, tokens, width)
    cot = cotangent.reshape(videos, tokens, width)

    cot_sent = call("split", 3, functools.partial(split_kernel, n), "vv", joint_piece, "v")(
        cot, to_joint
    )
    cot_pieces = exchange(cot_sent)
    deps = [cot_sent]
    saved, arrived = [], []
    for v in range(videos):
        sent, *keep = call(
            "space_forward", 14, functools.partial(space_forward_kernel, n, patches, v),
            "avaav",
            (piece, three, row, row, shaped(*weights_shape)),
            "vaaaa",
            [
                vmem(tokens, width), vmem(tokens, width), vmem(tokens, 3 * width),
                vmem(tokens, width), vmem(*weights_shape), *weight_refs, sems(9),
            ],
        )(x, modulation, spatial_qkv, spatial_out, to_pieces, deps=deps)
        deps = [keep[0], cot_pieces]
        arrived.append(exchange(sent))
        saved.append(keep)

    def exchange_units(sent):
        return [swap(unit, "seq", 1) for unit in sent]

    returned, time_units, outs = [], [], []
    for v in range(videos):
        d_middle, out, *sent, right = call(
            "time", 25, functools.partial(time_kernel, n, time_block, all_frames, v),
            "svvvaavvv",
            (piece, row) + 4 * (row,) + (four,),
            "vvaaaaa",
            [
                vmem(tokens, width, dtype=F32), vmem(tokens, width), vmem(tokens, width),
                vmem(tokens, 2 * width), vmem(tokens, 3 * width), vmem(tokens, width),
                vmem(tokens, 4 * width), *weight_refs, sems(9),
            ],
        )(
            core, arrived[v], cot_pieces, modulation, temporal_qkv, temporal_out, by_patch,
            joint_by_patch[v], from_patch, deps=deps,
        )
        deps = [right]
        outs.append(out)
        returned.append(exchange(d_middle))
        time_units.append((sent, right, exchange_units(sent)))

    grad_scale = (videos * lax.axis_size("dp") * all_frames * patches) ** (-0.5)

    def weights(units, late, deps=()):
        reduction = Reduction(core, width, late)
        steps, shapes = reduction.next_steps()
        sent, right, got = zip(*units)
        halves = call(
            "weights", 10,
            functools.partial(weight_kernel, videos, reduction.cuts, steps, grad_scale),
            "s" + "a" * (9 * videos), shapes, "v" * len(shapes),
            [
                vmem(2 * videos * tokens, 2 * width), vmem(2 * videos * tokens, 2 * width),
                vmem(width, reduction.columns, dtype=F32), sems(8 * videos),
            ],
        )(core, *right, *sum(sent, []), *sum(got, []), deps=deps)
        reduction.send(halves)
        return reduction, halves[0]

    def grad_of(video, units, d_middle, deps=()):
        return call(
            "grad_input", 8, functools.partial(grad_input_kernel, video), "avvvv", row, "v",
            [vmem(tokens, 3 * width), sems(1)],
        )(units[1], d_middle, x, modulation, spatial_qkv, deps=deps)

    d_middles, space_units, grad_input = [], [], []
    for v in range(videos):
        d_middle, *sent, right = call(
            "space_backward", 15, functools.partial(space_backward_kernel, patches, v),
            "svvavaaav",
            (row,) + 4 * (row,) + (four,),
            "vaaaaa",
            [
                vmem(tokens, width), vmem(tokens, 2 * width), vmem(tokens, 4 * width),
                vmem(tokens, 3 * width), vmem(width, width), sems(9),
            ],
        )(
            core, returned[v], modulation, spatial_out, from_pieces, *saved[v], deps=deps
        )
        if v == 0:
            time_sum, began = weights(time_units, False, deps=[right])
            out_sent = call(
                "split", 3, functools.partial(split_rows_kernel, n), "v" * (videos + 1),
                joint_piece, "v",
            )(*outs, joint_from_patch, deps=[began])
            deps = [out_sent]
            out_back = exchange(out_sent)
        d_middles.append(d_middle)
        space_units.append((sent, right, exchange_units(sent)))
    began = time_sum.stage(deps=[right])
    space_sum, began = weights(space_units, True, deps=[began])
    began = time_sum.stage(deps=[began, out_back])
    for v in range(videos):
        grad_input.append(grad_of(v, space_units[v], d_middles[v], deps=[began]))
        began = grad_input[-1]
    began = space_sum.stage(deps=[began])
    block_out = call("join", 4, join_kernel, "vv", all_rows, "v")(
        out_back, from_joint, deps=[began]
    )
    grad_input = jnp.stack(grad_input)
    grad_time, grad_space = time_sum.finish(), space_sum.finish()
    return (
        block_out.reshape(frames_in.shape), grad_input.reshape(frames_in.shape),
        *grad_space, *grad_time,
    )


def solution(mesh):
    return jax.shard_map(
        shards,
        mesh=mesh,
        in_specs=(
            P("dp", "seq", None, None),
            P("dp", None, None),
            P(),
            P(),
            P(),
            P(),
            P("dp", "seq", None, None),
        ),
        out_specs=(
            P("dp", "seq", None, None),
            P("dp", "seq", None, None),
            P(("dp", "seq"), None),
            P(("dp", "seq"), None),
            P(("dp", "seq"), None),
            P(("dp", "seq"), None),
        ),
        check_vma=False,
    )
```

```python
import functools

import jax
import jax.numpy as jnp
import numpy as np
from jax import lax
from jax.experimental import pallas as pl
from jax.experimental.pallas import tpu as pltpu
from jax.sharding import PartitionSpec as P

HEADS = 16
NORM_EPSILON = 1e-06
MASKED = -1e30
LOG2_E = 1.4426950408889634
MIB = 1024 * 1024
F32 = jnp.float32
BF16 = jnp.bfloat16

NN = (((1,), (0,)), ((), ()))
NT = (((1,), (1,)), ((), ()))
TN = (((0,), (0,)), ((), ()))


def dot(left, right, dims=NN):
    return lax.dot_general(left, right, dims, preferred_element_type=F32)


ROOM = {
    "split": 56, "space_forward": 56, "time": 56, "weights": 56, "space_backward": 56,
    "grad_input": 56, "stage": 16, "core_stage": 16, "assemble": 16, "join": 56,
}
SPACES = {"v": pltpu.VMEM, "s": pltpu.SMEM, "a": pl.ANY}


def call(name, us, body, ins, out_shape, outs, scratch=()):
    def run(*operands, deps=()):
        return pl.pallas_call(
            body,
            out_shape=out_shape,
            in_specs=[pl.BlockSpec(memory_space=SPACES[s]) for s in ins + "a" * len(deps)],
            out_specs=(
                tuple(pl.BlockSpec(memory_space=SPACES[s]) for s in outs)
                if isinstance(out_shape, tuple)
                else pl.BlockSpec(memory_space=SPACES[outs])
            ),
            scratch_shapes=list(scratch),
            compiler_params=pltpu.CompilerParams(vmem_limit_bytes=ROOM[name] * MIB),
            cost_estimate=pl.CostEstimate(
                flops=int(us * 1e9), transcendentals=0, bytes_accessed=int(us * 1e6)
            ),
            name=name,
        )(*operands, *deps)

    return run


def shaped(*shape, dtype=BF16):
    return jax.ShapeDtypeStruct(shape, dtype)


def norm_stats(values):
    mean = jnp.mean(values, -1, keepdims=True)
    centred = values - mean
    inverse = lax.rsqrt(jnp.mean(centred * centred, -1, keepdims=True) + NORM_EPSILON)
    return centred * inverse, inverse


def norm_backward(d_modded, normed, inverse, scale):
    e = d_modded * (1.0 + scale)
    return inverse * (
        e
        - jnp.mean(e, -1, keepdims=True)
        - normed * jnp.mean(e * normed, -1, keepdims=True)
    )


def pair_windows(width):
    size = 2 * width // HEADS
    found = []
    for pair in range(HEADS // 2):
        start = pair * size // 128 * 128
        offset = pair * size - start
        found.append((start, 128 * pl.cdiv(offset + size, 128), offset))
    return found


def pair_masks(rows, span, offset, size):
    lane = lax.broadcasted_iota(jnp.int32, (rows, span), 1)
    first = (lane >= offset) & (lane < offset + size)
    both = (lane >= offset) & (lane < offset + 2 * size)
    return first, both


def two_heads(values, first, both):
    zero = jnp.zeros_like(values)
    return jnp.concatenate(
        [jnp.where(first, values, zero), jnp.where(both & ~first, values, zero)], 0
    )


def per_query(by_key, other, first):
    out = dot(by_key, other, TN)
    rows = out.shape[0] // 2
    return jnp.where(first, out[:rows], out[rows:])


def probs_by_key(queries, key, factor, keep):
    scores = dot(key, queries, NT)
    if keep is not None:
        scores = jnp.where(keep, scores, MASKED)
    raised = jnp.exp2((scores - jnp.max(scores, 0, keepdims=True)) * (factor * LOG2_E))
    return raised * (1.0 / jnp.sum(raised, 0, keepdims=True))


def put(ref, rows, start, both, value):
    at = (pl.ds(rows, both.shape[0]), pl.ds(start, both.shape[1]))
    ref[at] = jnp.where(both, value.astype(BF16), ref[at])


def frame_rows(pieces):
    n, rows, width = pieces.shape
    return pieces.astype(F32).reshape(n * rows, width).astype(BF16)


def piece_rows(values, n):
    return values.reshape(n, values.shape[0] // n, values.shape[1]).astype(BF16)


def same_video(rows, frames):
    left = lax.broadcasted_iota(jnp.int32, (rows, 2 * rows), 0) // frames
    column = lax.broadcasted_iota(jnp.int32, (rows, 2 * rows), 1)
    right = jnp.where(column >= rows, column - rows, column) // frames
    return left == right


class Copies:
    def __init__(self, sems):
        self.sems, self.used = sems, 0

    def start(self, source, target):
        copy = pltpu.make_async_copy(source, target, self.sems.at[self.used])
        self.used += 1
        copy.start()
        return copy


def qkv_loads(copies, wqkv_ref, wqkv, width):
    parts = [pl.ds(part * width, width) for part in range(3)]
    return [copies.start(wqkv_ref.at[:, at], wqkv.at[:, at]) for at in parts]


def project_qkv(modded, wqkv, loads, packed, width):
    for part, load in enumerate(loads):
        load.wait()
        at = pl.ds(part * width, width)
        packed[:, at] = dot(modded, wqkv[:, at]).astype(BF16)


def split_kernel(n, x_ref, scatter_ref, out_ref):
    out_ref[...] = piece_rows(dot(scatter_ref[...], x_ref[0]), n)


def join_kernel(pieces_ref, gather_ref, *refs):
    out_ref = refs[-1]
    rows = dot(gather_ref[...], frame_rows(pieces_ref[...])).astype(BF16)
    out_ref[...] = rows.reshape(out_ref.shape)


def space_forward_kernel(
    n, block, video, x_ref, cot_ref, mod_ref, wqkv_ref, wout_ref, scatter_ref, scatter_cot_ref, *refs
):
    sent_ref, packed_out, modded_out, attended_out, weights_out = refs[-14:-9]
    x, cot, modded, packed, attended, weights, wqkv, wout, sems = refs[-9:]
    width = x.shape[1]
    size = width // HEADS
    factor = size ** (-0.5)
    copies = Copies(sems)
    load_x = copies.start(x_ref.at[video], x)
    load_qkv = qkv_loads(copies, wqkv_ref, wqkv, width)
    load_out = copies.start(wout_ref, wout)
    if video:
        load_cot = copies.start(cot_ref.at[video], cot)
    load_x.wait()
    normed, _ = norm_stats(x[...].astype(F32))
    modded[...] = (normed * (1.0 + mod_ref[video, 1:2, :]) + mod_ref[video, 0:1, :]).astype(BF16)
    stores = [copies.start(modded, modded_out)]
    project_qkv(modded[...], wqkv, load_qkv, packed, width)
    stores.append(copies.start(packed, packed_out))
    pairs = pair_windows(width)

    def one_block(g, carry):
        rows = pl.multiple_of(g * block, 16)
        for pair, (start, span, offset) in enumerate(pairs):
            first, both = pair_masks(block, span, offset, size)
            at = pl.ds(rows, block)
            query = packed[at, pl.ds(start, span)]
            key = packed[at, pl.ds(width + start, span)]
            value = packed[at, pl.ds(2 * width + start, span)]
            probs = probs_by_key(two_heads(query, first, both), key, factor, None).astype(BF16)
            weights[g * len(pairs) + pair] = probs
            put(attended, rows, start, both, per_query(probs, value, first))
        return carry

    lax.fori_loop(0, x.shape[0] // block, one_block, 0)
    stores.append(copies.start(attended, attended_out))
    stores.append(copies.start(weights, weights_out))
    load_out.wait()
    projected = dot(attended[...], wout[...])
    middle = (x[...].astype(F32) + mod_ref[video, 2:3, :] * projected).astype(BF16)
    pieces = dot(scatter_ref[...], middle)
    if video:
        load_cot.wait()
        pieces += dot(scatter_cot_ref[...], cot[...])
    sent_ref[...] = piece_rows(pieces, n)
    for store in stores:
        store.wait()


def unit_stores(copies, core, width, left, right, outs):
    *sent_outs, right_out = outs
    other = (1 - core) * (2 * width)
    sources = [left.at[:, pl.ds(unit * width, width)] for unit in range(2)]
    sources += [
        right.at[:, pl.ds(pl.multiple_of(other + unit * width, 128), width)] for unit in range(2)
    ]
    return [copies.start(source, out) for source, out in zip(sources, sent_outs)] + [
        copies.start(right, right_out)
    ]


def time_kernel(
    n, block, frames, video, core_ref, middle_ref, cot_ref, mod_ref, wqkv_ref, wout_ref,
    gather_ref, gather_cot_ref, scatter_ref, scatter_out_ref, others_ref, *refs
):
    (d_middle_ref, block_out_ref, *unit_outs), scratch = refs[-17:-10], refs[-10:]
    normed, x, up, left, packed, d_out, right, wqkv, wout, sems = scratch
    width = x.shape[1]
    size = width // HEADS
    factor = size ** (-0.5)
    copies = Copies(sems)
    load_qkv = qkv_loads(copies, wqkv_ref, wqkv, width)
    load_out = copies.start(wout_ref, wout)
    x[...] = dot(gather_ref[...], frame_rows(middle_ref[...])).astype(BF16)
    up[...] = dot(gather_cot_ref[...], frame_rows(cot_ref[...])).astype(BF16)
    normed_now, inverse = norm_stats(x[...].astype(F32))
    normed[...] = normed_now
    left[:, 0:width] = (
        normed_now * (1.0 + mod_ref[video, 4:5, :]) + mod_ref[video, 3:4, :]
    ).astype(BF16)
    right[:, 3 * width :] = (mod_ref[video, 5:6, :] * up[...].astype(F32)).astype(BF16)
    project_qkv(left[:, 0:width], wqkv, load_qkv, packed, width)
    load_out.wait()
    d_out[...] = dot(right[:, 3 * width :], wout[...], NT).astype(BF16)
    keep = same_video(block, frames)

    def one_block(g, carry):
        rows = pl.multiple_of(g * block, 16)
        for start, span, offset in pair_windows(width):
            first, both = pair_masks(block, span, offset, size)
            at = pl.ds(rows, block)
            query = two_heads(packed[at, pl.ds(start, span)], first, both)
            key = packed[at, pl.ds(width + start, span)]
            value = packed[at, pl.ds(2 * width + start, span)]
            d_rows = two_heads(d_out[at, pl.ds(start, span)], first, both)
            probs = probs_by_key(query, key, factor, keep)
            weights = probs.astype(BF16)
            put(left, rows, width + start, both, per_query(weights, value, first))
            d_probs = dot(value, d_rows, NT)
            total = jnp.sum(probs * d_probs, 0, keepdims=True)
            d_scores = (probs * (d_probs - total) * factor).astype(BF16)
            put(right, rows, start, both, per_query(d_scores, key, first))
            put(right, rows, width + start, both, dot(d_scores, query))
            put(right, rows, 2 * width + start, both, dot(weights, d_rows))
        return carry

    lax.fori_loop(0, x.shape[0] // block, one_block, 0)
    stores = unit_stores(copies, core_ref[1] & 1, width, left, right, unit_outs)
    d_modded = dot(right[:, 0 : 3 * width], wqkv[...], NT)
    d_middle = up[...].astype(F32) + norm_backward(
        d_modded, normed[...], inverse, mod_ref[video, 4:5, :]
    )
    d_middle_ref[...] = piece_rows(dot(scatter_ref[...], d_middle.astype(BF16)), n)
    projected = dot(left[:, width:], wout[...])
    out = (x[...].astype(F32) + mod_ref[video, 5:6, :] * projected).astype(BF16)
    pieces = dot(scatter_out_ref[...], out)
    if video:
        pieces += others_ref[...].astype(F32).reshape(pieces.shape)
    block_out_ref[...] = piece_rows(pieces, n)
    for store in stores:
        store.wait()


def space_backward_kernel(
    block, video, core_ref, up_ref, mod_ref, wout_ref, gather_ref, packed_ref, modded_ref,
    attended_ref, weights_ref, *refs
):
    d_middle_ref, *unit_outs = refs[-12:-6]
    d_out, left, right, packed, wout, sems = refs[-6:]
    width = wout.shape[0]
    size = width // HEADS
    factor = size ** (-0.5)
    copies = Copies(sems)
    load_out = copies.start(wout_ref, wout)
    load_packed = copies.start(packed_ref, packed)
    loads = [
        copies.start(modded_ref, left.at[:, pl.ds(0, width)]),
        copies.start(attended_ref, left.at[:, pl.ds(width, width)]),
    ]
    up = dot(gather_ref[...], frame_rows(up_ref[...]))
    d_middle_ref[...] = up.astype(BF16)
    right[:, 3 * width :] = (mod_ref[video, 2:3, :] * up).astype(BF16)
    load_out.wait()
    d_out[...] = dot(right[:, 3 * width :], wout[...], NT).astype(BF16)
    load_packed.wait()
    pairs = pair_windows(width)

    def one_block(g, carry):
        rows = pl.multiple_of(g * block, 16)
        for pair, (start, span, offset) in enumerate(pairs):
            first, both = pair_masks(block, span, offset, size)
            at = pl.ds(rows, block)
            query = two_heads(packed[at, pl.ds(start, span)], first, both)
            key = packed[at, pl.ds(width + start, span)]
            value = packed[at, pl.ds(2 * width + start, span)]
            d_rows = two_heads(d_out[at, pl.ds(start, span)], first, both)
            weights = weights_ref[g * len(pairs) + pair]
            probs = weights.astype(F32)
            d_probs = dot(value, d_rows, NT)
            total = jnp.sum(probs * d_probs, 0, keepdims=True) / jnp.sum(probs, 0, keepdims=True)
            d_scores = (probs * (d_probs - total) * factor).astype(BF16)
            put(right, rows, start, both, per_query(d_scores, key, first))
            put(right, rows, width + start, both, dot(d_scores, query))
            put(right, rows, 2 * width + start, both, dot(weights, d_rows))
        return carry

    lax.fori_loop(0, d_out.shape[0] // block, one_block, 0)
    for load in loads:
        load.wait()
    for store in unit_stores(copies, core_ref[1] & 1, width, left, right, unit_outs):
        store.wait()


def grad_input_kernel(video, right_ref, d_middle_ref, x_ref, mod_ref, wqkv_ref, *refs):
    out_ref, d_packed, wqkv, sems = refs[-4:]
    width = out_ref.shape[1]
    copies = Copies(sems)
    parts = [pl.ds(part * width, width) for part in range(3)]
    loads = [
        (copies.start(right_ref.at[:, at], d_packed.at[:, at]),
         copies.start(wqkv_ref.at[:, at], wqkv.at[:, at]))
        for at in parts
    ]
    normed, inverse = norm_stats(x_ref[video].astype(F32))
    d_modded = 0.0
    for at, load in zip(parts, loads):
        for one in load:
            one.wait()
        d_modded += dot(d_packed[:, at], wqkv[:, at], NT)
    d_tokens = norm_backward(d_modded, normed, inverse, mod_ref[video, 1:2, :])
    out_ref[...] = (d_middle_ref[...].astype(F32) + d_tokens).astype(BF16)


def bit_of(place_ref, axis, bit):
    return (place_ref[0 if axis == "dp" else 1] >> bit) & 1


def emit_halves(rows, inner, mine, kept_ref, sent_ref):
    for outer in range(kept_ref.shape[0]):
        low = rows[2 * outer * inner : (2 * outer + 1) * inner, :]
        high = rows[(2 * outer + 1) * inner : (2 * outer + 2) * inner, :]
        kept_ref[outer] = jnp.where(mine == 0, low, high).astype(BF16)
        sent_ref[outer] = jnp.where(mine == 0, high, low).astype(BF16)


def weight_kernel(videos, cuts, steps, grad_scale, place_ref, *refs):
    right, units = refs[:videos], refs[videos : 9 * videos]
    sent = [units[4 * v : 4 * v + 4] for v in range(videos)]
    got = [units[4 * v : 4 * v + 4] for v in range(videos, 2 * videos)]
    count = 2 * len(cuts)
    outs, scratch = refs[-4 - 2 * count : -4 - count], refs[-4 - count : -4]
    left_rows, right_rows, total, sems = refs[-4:]
    width = left_rows.shape[1] // 2
    tokens = right[0].shape[0]
    copies = Copies(sems)
    core = place_ref[1] & 1
    own = pl.multiple_of(core * (2 * width), 128)
    waits = []
    for unit in range(2):
        now = []
        for video in range(videos):
            for place, (left, mine) in enumerate(((sent[video], right[video]), (got[video], None))):
                rows = pl.ds((2 * video + place) * tokens, tokens)
                at = pl.ds(unit * width, width)
                now.append(copies.start(left[unit], left_rows.at[rows, at]))
                source = (
                    left[2 + unit]
                    if mine is None
                    else mine.at[:, pl.ds(pl.multiple_of(own + unit * width, 128), width)]
                )
                now.append(copies.start(source, right_rows.at[rows, at]))
        waits.append(now)
    done, stores = 0, []
    for part, ((low, high), (axis, bit, inner)) in enumerate(zip(cuts, steps)):
        for unit in range(2):
            start, stop = max(low, unit * width), min(high, (unit + 1) * width)
            if start >= stop:
                continue
            while done <= unit:
                for wait in waits[done]:
                    wait.wait()
                done += 1
            column = pl.multiple_of(core * width, 128) if unit else 0
            left = left_rows[:, pl.ds(column, width)]
            total[:, start - low : stop - low] = (
                dot(left, right_rows[:, start:stop], TN) * grad_scale
            )
        pair = slice(2 * part, 2 * part + 2)
        emit_halves(total, inner, bit_of(place_ref, axis, bit), *scratch[pair])
        stores += [copies.start(a, b) for a, b in zip(scratch[pair], outs[pair])]
    for store in stores:
        store.wait()


def stage_kernel(steps, place_ref, *refs):
    count = len(steps)
    total, outs = refs[-1], refs[-1 - 2 * count : -1]
    for part, (axis, bit, inner) in enumerate(steps):
        kept, got = refs[part], refs[count + part]
        each = kept.shape[1]
        for outer in range(kept.shape[0]):
            total[outer * each : (outer + 1) * each, :] = kept[outer].astype(F32) + got[
                outer
            ].astype(F32)
        emit_halves(
            total, inner, bit_of(place_ref, axis, bit), outs[2 * part], outs[2 * part + 1]
        )


def core_stage_kernel(count, place_ref, *refs):
    kept_out, sent_out = refs[-2:]
    rows, columns = refs[0].shape[1:]
    core = place_ref[1] & 1
    for part in range(count):
        total = refs[part][0].astype(F32) + refs[count + part][0].astype(F32)
        low, high = total[: rows // 2], total[rows // 2 :]
        at = slice(part * columns, (part + 1) * columns)
        kept_out[:, at] = jnp.where(core == 0, low, high).astype(BF16)
        sent_out[:, at] = jnp.where(core == 0, high, low).astype(BF16)


def assemble_kernel(place_ref, kept_ref, got_ref, qkv_ref, out_ref):
    width = out_ref.shape[1]
    core = place_ref[1] & 1
    kept, got = kept_ref[...].astype(F32), got_ref[...].astype(F32)
    low = jnp.where(core == 0, kept, got).astype(BF16)
    high = jnp.where(core == 0, got, kept).astype(BF16)
    qkv_ref[:, : 2 * width] = low
    qkv_ref[:, 2 * width :] = high[:, :width]
    out_ref[...] = high[:, width:]


def swap(x, axis, mask):
    size = lax.axis_size(axis)
    return lax.ppermute(x, axis, [(i, i ^ mask) for i in range(size)])


class Reduction:
    def __init__(self, place, width, late):
        dp_bits = [("dp", bit) for bit in range(lax.axis_size("dp").bit_length() - 1)]
        seq_bits = [("seq", bit) for bit in range(1, lax.axis_size("seq").bit_length() - 1)]
        if late:
            self.orders = (
                dp_bits + seq_bits,
                dp_bits[-1:] + seq_bits[:1] + dp_bits[:-1] + seq_bits[1:],
                seq_bits[:1] + dp_bits + seq_bits[1:],
            )
        else:
            self.orders = (dp_bits + seq_bits, dp_bits[::-1] + seq_bits)
        self.parts = len(self.orders)
        self.place, self.width, self.columns = place, width, 2 * width // self.parts
        self.cuts = tuple(
            (part * self.columns, (part + 1) * self.columns) for part in range(self.parts)
        )
        self.bits = dp_bits[::-1] + seq_bits[::-1]
        self.step = 0

    def next_steps(self):
        least = self.width >> len(self.bits)
        steps, shapes = [], []
        for order in self.orders:
            left = [bit for bit in self.bits if bit not in order[: self.step]]
            above = left.index(order[self.step])
            inner = least << (len(left) - above - 1)
            steps.append((*order[self.step], inner))
            shapes += 2 * [shaped(1 << above, inner, self.columns)]
        return tuple(steps), tuple(shapes)

    def send(self, halves):
        self.kept = halves[0::2]
        self.got = [
            swap(half, order[self.step][0], 1 << order[self.step][1])
            for half, order in zip(halves[1::2], self.orders)
        ]
        self.step += 1

    def stage(self, deps=()):
        steps, shapes = self.next_steps()
        halves = call(
            "stage", 2, functools.partial(stage_kernel, steps), "s" + "v" * len(shapes), shapes,
            "v" * len(shapes),
            [pltpu.VMEM((self.width >> self.step, self.columns), F32)],
        )(self.place, *self.kept, *self.got, deps=deps)
        self.send(halves)
        return halves[0]

    def core_stage(self, deps=()):
        while self.step < len(self.bits):
            self.stage()
        rows = self.width >> (len(self.bits) + 1)
        half = shaped(rows, 2 * self.width)
        self.mine, sent = call(
            "core_stage", 1, functools.partial(core_stage_kernel, self.parts),
            "s" + "v" * (2 * self.parts), (half, half), "vv",
        )(self.place, *self.kept, *self.got, deps=deps)
        self.other = swap(sent, "seq", 1)
        return self.mine

    def finish(self):
        rows = self.mine.shape[0]
        return call(
            "assemble", 1, assemble_kernel, "svv",
            (shaped(rows, 3 * self.width), shaped(rows, self.width)), "vv",
        )(self.place, self.mine, self.other)


def shards(frames_in, modulation, spatial_qkv, spatial_out, temporal_qkv, temporal_out, cotangent):
    n = lax.axis_size("seq")
    videos, frames, patches, width = frames_in.shape
    all_frames = frames * n
    tokens = frames * patches
    own_patches = patches // n
    rows = frames * own_patches
    padded = -(-rows // 8) * 8
    time_block = 6 * all_frames if own_patches % 6 == 0 else 3 * all_frames
    core = jnp.stack([lax.axis_index("dp"), lax.axis_index("seq")]).astype(jnp.int32)

    joint_padded = -(-videos * rows // 8) * 8
    to_pieces = np.zeros((n * padded, tokens), np.float32)
    to_joint = np.zeros((videos, n * joint_padded, tokens), np.float32)
    by_patch = np.zeros((tokens, n * padded), np.float32)
    joint_by_patch = np.zeros((videos, tokens, n * joint_padded), np.float32)
    for device in range(n):
        for f in range(frames):
            for p in range(own_patches):
                inside = f * own_patches + p
                before = f * patches + device * own_patches + p
                after = p * all_frames + device * frames + f
                to_pieces[device * padded + inside, before] = 1
                by_patch[after, device * padded + inside] = 1
                for v in range(videos):
                    place = device * joint_padded + v * rows + inside
                    to_joint[v, place, before] = 1
                    joint_by_patch[v, after, place] = 1
    from_joint = jnp.asarray(np.concatenate(list(to_joint), 1).T, BF16)
    to_pieces, from_pieces = jnp.asarray(to_pieces, BF16), jnp.asarray(to_pieces.T, BF16)
    to_joint = [jnp.asarray(m, BF16) for m in to_joint]
    by_patch, from_patch = jnp.asarray(by_patch, BF16), jnp.asarray(by_patch.T, BF16)
    joint_from_patch = [jnp.asarray(m.T, BF16) for m in joint_by_patch]
    joint_by_patch = [jnp.asarray(m, BF16) for m in joint_by_patch]

    def exchange(pieces):
        return lax.all_to_all(pieces, "seq", split_axis=0, concat_axis=0, tiled=True)

    piece = shaped(n, padded, width)
    joint_piece = shaped(n, joint_padded, width)
    row = shaped(tokens, width)
    three, four = shaped(tokens, 3 * width), shaped(tokens, 4 * width)
    all_rows = shaped(videos, tokens, width)
    weights_shape = (frames * (HEADS // 2), patches, 2 * patches)

    def vmem(*shape, dtype=BF16):
        return pltpu.VMEM(shape, dtype)

    def sems(count):
        return pltpu.SemaphoreType.DMA((count,))

    weight_refs = [vmem(width, 3 * width), vmem(width, width)]
    x = frames_in.reshape(videos, tokens, width)
    cot = cotangent.reshape(videos, tokens, width)

    cot_sent = call("split", 3, functools.partial(split_kernel, n), "vv", piece, "v")(
        cot, to_pieces
    )
    cot_pieces = exchange(cot_sent)
    deps = [cot_sent]
    saved, arrived = [], []
    for v in range(videos):
        sent, *keep = call(
            "space_forward", 14, functools.partial(space_forward_kernel, n, patches, v),
            "aavaavv",
            (joint_piece if v else piece, three, row, row, shaped(*weights_shape)),
            "vaaaa",
            [
                vmem(tokens, width), vmem(tokens, width), vmem(tokens, width),
                vmem(tokens, 3 * width), vmem(tokens, width), vmem(*weights_shape),
                *weight_refs, sems(10),
            ],
        )(
            x, cot, modulation, spatial_qkv, spatial_out, to_joint[0] if v else to_pieces,
            to_joint[1], deps=deps,
        )
        deps = [keep[0], cot_pieces]
        arrived.append(exchange(sent))
        saved.append(keep)

    def exchange_units(sent):
        return [swap(unit, "seq", 1) for unit in sent]

    returned, time_units, out_sent = [], [], core
    for v in range(videos):
        d_middle, out_sent, *sent, right = call(
            "time", 25, functools.partial(time_kernel, n, time_block, all_frames, v),
            "svvvaavvvv" + ("v" if v else "a"),
            (piece, joint_piece) + 4 * (row,) + (four,),
            "vvaaaaa",
            [
                vmem(tokens, width, dtype=F32), vmem(tokens, width), vmem(tokens, width),
                vmem(tokens, 2 * width), vmem(tokens, 3 * width), vmem(tokens, width),
                vmem(tokens, 4 * width), *weight_refs, sems(9),
            ],
        )(
            core, arrived[v], arrived[v] if v else cot_pieces, modulation, temporal_qkv,
            temporal_out, joint_by_patch[0] if v else by_patch,
            joint_by_patch[1] if v else by_patch, from_patch, joint_from_patch[v], out_sent,
            deps=deps,
        )
        deps = [right]
        returned.append(exchange(d_middle))
        time_units.append((sent, right, exchange_units(sent)))

    grad_scale = (videos * lax.axis_size("dp") * all_frames * patches) ** (-0.5)

    def weights(units, late, deps=()):
        reduction = Reduction(core, width, late)
        steps, shapes = reduction.next_steps()
        sent, right, got = zip(*units)
        halves = call(
            "weights", 10,
            functools.partial(weight_kernel, videos, reduction.cuts, steps, grad_scale),
            "s" + "a" * (9 * videos), shapes, "a" * len(shapes),
            [vmem(*half.shape) for half in shapes] + [
                vmem(2 * videos * tokens, 2 * width), vmem(2 * videos * tokens, 2 * width),
                vmem(width, reduction.columns, dtype=F32), sems(8 * videos + len(shapes)),
            ],
        )(core, *right, *sum(sent, []), *sum(got, []), deps=deps)
        reduction.send(halves)
        return reduction, halves[0]

    def grad_of(video, units, d_middle, deps=()):
        return call(
            "grad_input", 8, functools.partial(grad_input_kernel, video), "avvva", row, "v",
            [vmem(tokens, 3 * width), vmem(width, 3 * width), sems(6)],
        )(units[1], d_middle, x, modulation, spatial_qkv, deps=deps)

    d_middles, space_units, grad_input = [], [], []
    for v in range(videos):
        d_middle, *sent, right = call(
            "space_backward", 15, functools.partial(space_backward_kernel, patches, v),
            "svvavaaav",
            (row,) + 4 * (row,) + (four,),
            "vaaaaa",
            [
                vmem(tokens, width), vmem(tokens, 2 * width), vmem(tokens, 4 * width),
                vmem(tokens, 3 * width), vmem(width, width), sems(9),
            ],
        )(
            core, returned[v], modulation, spatial_out, from_pieces, *saved[v], deps=deps
        )
        if v == 0:
            time_sum, began = weights(time_units, False, deps=[right])
            deps = [began]
            out_back = exchange(out_sent)
        d_middles.append(d_middle)
        space_units.append((sent, right, exchange_units(sent)))
    grad_input.append(grad_of(0, space_units[0], d_middles[0], deps=[right]))
    began = time_sum.stage(deps=grad_input)
    space_sum, began = weights(space_units, True, deps=[began])
    began = time_sum.stage(deps=[began, out_back])
    for v in range(1, videos):
        grad_input.append(grad_of(v, space_units[v], d_middles[v], deps=[began]))
    began = time_sum.stage(deps=[grad_input[-1]])
    began = space_sum.stage(deps=[began])
    block_out = call("join", 4, join_kernel, "vv", all_rows, "v")(
        out_back, from_joint, deps=[began]
    )
    space_sum.stage(deps=[block_out, time_sum.core_stage(deps=[began])])
    space_sum.core_stage()
    grad_input = jnp.stack(grad_input)
    grad_time, grad_space = time_sum.finish(), space_sum.finish()
    return (
        block_out.reshape(frames_in.shape), grad_input.reshape(frames_in.shape),
        *grad_space, *grad_time,
    )


def solution(mesh):
    return jax.shard_map(
        shards,
        mesh=mesh,
        in_specs=(
            P("dp", "seq", None, None),
            P("dp", None, None),
            P(),
            P(),
            P(),
            P(),
            P("dp", "seq", None, None),
        ),
        out_specs=(
            P("dp", "seq", None, None),
            P("dp", "seq", None, None),
            P(("dp", "seq"), None),
            P(("dp", "seq"), None),
            P(("dp", "seq"), None),
            P(("dp", "seq"), None),
        ),
        check_vma=False,
    )
```

```python
import functools

import jax
import jax.numpy as jnp
import numpy as np
from jax import lax
from jax.experimental import pallas as pl
from jax.experimental.pallas import tpu as pltpu
from jax.sharding import PartitionSpec as P

HEADS = 16
NORM_EPSILON = 1e-06
MASKED = -1e30
LOG2_E = 1.4426950408889634
MIB = 1024 * 1024
F32 = jnp.float32
BF16 = jnp.bfloat16

NN = (((1,), (0,)), ((), ()))
NT = (((1,), (1,)), ((), ()))
TN = (((0,), (0,)), ((), ()))


def dot(left, right, dims=NN):
    return lax.dot_general(left, right, dims, preferred_element_type=F32)


ROOM = {
    "split": 56, "space_forward": 56, "time": 56, "weights": 56, "space_backward": 56,
    "grad_input": 56, "stage": 16, "core_stage": 16, "assemble": 16, "join": 56,
}
SPACES = {"v": pltpu.VMEM, "s": pltpu.SMEM, "a": pl.ANY}


def call(name, us, body, ins, out_shape, outs, scratch=()):
    def run(*operands, deps=()):
        return pl.pallas_call(
            body,
            out_shape=out_shape,
            in_specs=[pl.BlockSpec(memory_space=SPACES[s]) for s in ins + "a" * len(deps)],
            out_specs=(
                tuple(pl.BlockSpec(memory_space=SPACES[s]) for s in outs)
                if isinstance(out_shape, tuple)
                else pl.BlockSpec(memory_space=SPACES[outs])
            ),
            scratch_shapes=list(scratch),
            compiler_params=pltpu.CompilerParams(vmem_limit_bytes=ROOM[name] * MIB),
            cost_estimate=pl.CostEstimate(
                flops=int(us * 1e9), transcendentals=0, bytes_accessed=int(us * 1e6)
            ),
            name=name,
        )(*operands, *deps)

    return run


def shaped(*shape, dtype=BF16):
    return jax.ShapeDtypeStruct(shape, dtype)


def norm_stats(values):
    mean = jnp.mean(values, -1, keepdims=True)
    centred = values - mean
    inverse = lax.rsqrt(jnp.mean(centred * centred, -1, keepdims=True) + NORM_EPSILON)
    return centred * inverse, inverse


def norm_backward(d_modded, normed, inverse, scale):
    e = d_modded * (1.0 + scale)
    return inverse * (
        e
        - jnp.mean(e, -1, keepdims=True)
        - normed * jnp.mean(e * normed, -1, keepdims=True)
    )


def pair_windows(width):
    size = 2 * width // HEADS
    found = []
    for pair in range(HEADS // 2):
        start = pair * size // 128 * 128
        offset = pair * size - start
        found.append((start, 128 * pl.cdiv(offset + size, 128), offset))
    return found


def pair_masks(rows, span, offset, size):
    lane = lax.broadcasted_iota(jnp.int32, (rows, span), 1)
    first = (lane >= offset) & (lane < offset + size)
    both = (lane >= offset) & (lane < offset + 2 * size)
    return first, both


def two_heads(values, first, both):
    zero = jnp.zeros_like(values)
    return jnp.concatenate(
        [jnp.where(first, values, zero), jnp.where(both & ~first, values, zero)], 0
    )


def per_query(by_key, other, first):
    out = dot(by_key, other, TN)
    rows = out.shape[0] // 2
    return jnp.where(first, out[:rows], out[rows:])


def softmax_by_key(scores, factor, keep):
    if keep is not None:
        scores = jnp.where(keep, scores, MASKED)
    raised = jnp.exp2((scores - jnp.max(scores, 0, keepdims=True)) * (factor * LOG2_E))
    return raised * (1.0 / jnp.sum(raised, 0, keepdims=True))


def put(ref, rows, start, both, value):
    at = (pl.ds(rows, both.shape[0]), pl.ds(start, both.shape[1]))
    ref[at] = jnp.where(both, value.astype(BF16), ref[at])


def frame_rows(pieces):
    n, rows, width = pieces.shape
    return pieces.astype(F32).reshape(n * rows, width).astype(BF16)


def piece_rows(values, n):
    return values.reshape(n, values.shape[0] // n, values.shape[1]).astype(BF16)


def same_video(rows, frames):
    left = lax.broadcasted_iota(jnp.int32, (rows, 2 * rows), 0) // frames
    column = lax.broadcasted_iota(jnp.int32, (rows, 2 * rows), 1)
    right = jnp.where(column >= rows, column - rows, column) // frames
    return left == right


class Copies:
    def __init__(self, sems):
        self.sems, self.used = sems, 0

    def start(self, source, target):
        copy = pltpu.make_async_copy(source, target, self.sems.at[self.used])
        self.used += 1
        copy.start()
        return copy


def qkv_loads(copies, wqkv_ref, wqkv, width):
    parts = [pl.ds(part * width, width) for part in range(3)]
    return [copies.start(wqkv_ref.at[:, at], wqkv.at[:, at]) for at in parts]


def project_qkv(modded, wqkv, loads, packed, width):
    for part, load in enumerate(loads):
        load.wait()
        at = pl.ds(part * width, width)
        packed[:, at] = dot(modded, wqkv[:, at]).astype(BF16)


def split_kernel(n, x_ref, scatter_ref, out_ref):
    out_ref[...] = piece_rows(dot(scatter_ref[...], x_ref[0]), n)


def join_kernel(pieces_ref, gather_ref, *refs):
    out_ref = refs[-1]
    rows = dot(gather_ref[...], frame_rows(pieces_ref[...])).astype(BF16)
    out_ref[...] = rows.reshape(out_ref.shape)


def space_forward_kernel(
    n, block, video, x_ref, cot_ref, mod_ref, wqkv_ref, wout_ref, scatter_ref, scatter_cot_ref, *refs
):
    sent_ref, packed_out, left_out, weights_out = refs[-13:-9]
    x, cot, left, packed, weights, wqkv, wout, scores_ref, sems = refs[-9:]
    width = x.shape[1]
    size = width // HEADS
    factor = size ** (-0.5)
    copies = Copies(sems)
    load_x = copies.start(x_ref.at[video], x)
    load_qkv = qkv_loads(copies, wqkv_ref, wqkv, width)
    load_out = copies.start(wout_ref, wout)
    if video:
        load_cot = copies.start(cot_ref.at[video], cot)
    load_x.wait()
    normed, _ = norm_stats(x[...].astype(F32))
    left[:, 0:width] = (
        normed * (1.0 + mod_ref[video, 1:2, :]) + mod_ref[video, 0:1, :]
    ).astype(BF16)
    project_qkv(left[:, 0:width], wqkv, load_qkv, packed, width)
    stores = [copies.start(packed, packed_out)]
    pairs = pair_windows(width)

    def one_block(g, carry):
        rows = pl.multiple_of(g * block, 16)
        at = pl.ds(rows, block)
        for pair, (start, span, offset) in enumerate(pairs):
            first, both = pair_masks(block, span, offset, size)
            query = two_heads(packed[at, pl.ds(start, span)], first, both)
            scores_ref[pair] = dot(packed[at, pl.ds(width + start, span)], query, NT)
        for pair in range(len(pairs)):
            probs = softmax_by_key(scores_ref[pair], factor, None)
            weights[g * len(pairs) + pair] = probs.astype(BF16)
        for pair, (start, span, offset) in enumerate(pairs):
            first, both = pair_masks(block, span, offset, size)
            value = packed[at, pl.ds(2 * width + start, span)]
            attended = per_query(weights[g * len(pairs) + pair], value, first)
            put(left, rows, width + start, both, attended)
        return carry

    lax.fori_loop(0, x.shape[0] // block, one_block, 0)
    stores.append(copies.start(left, left_out))
    stores.append(copies.start(weights, weights_out))
    load_out.wait()
    projected = dot(left[:, width:], wout[...])
    middle = (x[...].astype(F32) + mod_ref[video, 2:3, :] * projected).astype(BF16)
    pieces = dot(scatter_ref[...], middle)
    if video:
        load_cot.wait()
        pieces += dot(scatter_cot_ref[...], cot[...])
    sent_ref[...] = piece_rows(pieces, n)
    for store in stores:
        store.wait()


def unit_stores(copies, core, width, right, outs):
    sent_out, right_out = outs
    other = pl.multiple_of((1 - core) * (2 * width), 128)
    return [
        copies.start(right.at[:, pl.ds(other, 2 * width)], sent_out), copies.start(right, right_out)
    ]


def time_kernel(
    n, block, frames, video, core_ref, middle_ref, cot_ref, mod_ref, wqkv_ref, wout_ref,
    gather_ref, gather_cot_ref, scatter_ref, scatter_out_ref, others_ref, *refs
):
    (d_middle_ref, block_out_ref, left_out, *unit_outs), scratch = refs[-19:-14], refs[-14:]
    normed, x, up, left, packed, d_out, right, wqkv, wout = scratch[:9]
    scores_ref, d_probs_ref, weights_ref, d_scores_ref, sems = scratch[9:]
    width = x.shape[1]
    size = width // HEADS
    factor = size ** (-0.5)
    copies = Copies(sems)
    load_qkv = qkv_loads(copies, wqkv_ref, wqkv, width)
    load_out = copies.start(wout_ref, wout)
    x[...] = dot(gather_ref[...], frame_rows(middle_ref[...])).astype(BF16)
    up[...] = dot(gather_cot_ref[...], frame_rows(cot_ref[...])).astype(BF16)
    normed_now, inverse = norm_stats(x[...].astype(F32))
    normed[...] = normed_now
    left[:, 0:width] = (
        normed_now * (1.0 + mod_ref[video, 4:5, :]) + mod_ref[video, 3:4, :]
    ).astype(BF16)
    right[:, 3 * width :] = (mod_ref[video, 5:6, :] * up[...].astype(F32)).astype(BF16)
    project_qkv(left[:, 0:width], wqkv, load_qkv, packed, width)
    load_out.wait()
    d_out[...] = dot(right[:, 3 * width :], wout[...], NT).astype(BF16)
    keep = same_video(block, frames)

    pairs = pair_windows(width)

    def one_block(g, carry):
        rows = pl.multiple_of(g * block, 16)
        at = pl.ds(rows, block)

        def parts(pair):
            start, span, offset = pairs[pair]
            first, both = pair_masks(block, span, offset, size)
            query = two_heads(packed[at, pl.ds(start, span)], first, both)
            key = packed[at, pl.ds(width + start, span)]
            value = packed[at, pl.ds(2 * width + start, span)]
            d_rows = two_heads(d_out[at, pl.ds(start, span)], first, both)
            return start, first, both, query, key, value, d_rows

        for pair in range(len(pairs)):
            _, _, _, query, key, value, d_rows = parts(pair)
            scores_ref[pair] = dot(key, query, NT)
            d_probs_ref[pair] = dot(value, d_rows, NT)
        for pair in range(len(pairs)):
            probs = softmax_by_key(scores_ref[pair], factor, keep)
            d_probs = d_probs_ref[pair]
            total = jnp.sum(probs * d_probs, 0, keepdims=True)
            weights_ref[pair] = probs.astype(BF16)
            d_scores_ref[pair] = (probs * (d_probs - total) * factor).astype(BF16)
        for pair in range(len(pairs)):
            start, first, both, query, key, value, d_rows = parts(pair)
            weights, d_scores = weights_ref[pair], d_scores_ref[pair]
            put(left, rows, width + start, both, per_query(weights, value, first))
            put(right, rows, start, both, per_query(d_scores, key, first))
            put(right, rows, width + start, both, dot(d_scores, query))
            put(right, rows, 2 * width + start, both, dot(weights, d_rows))
        return carry

    lax.fori_loop(0, x.shape[0] // block, one_block, 0)
    stores = [copies.start(left, left_out)]
    stores += unit_stores(copies, core_ref[1] & 1, width, right, unit_outs)
    d_modded = dot(right[:, 0 : 3 * width], wqkv[...], NT)
    d_middle = up[...].astype(F32) + norm_backward(
        d_modded, normed[...], inverse, mod_ref[video, 4:5, :]
    )
    d_middle_ref[...] = piece_rows(dot(scatter_ref[...], d_middle.astype(BF16)), n)
    projected = dot(left[:, width:], wout[...])
    out = (x[...].astype(F32) + mod_ref[video, 5:6, :] * projected).astype(BF16)
    pieces = dot(scatter_out_ref[...], out)
    if video:
        pieces += others_ref[...].astype(F32).reshape(pieces.shape)
    block_out_ref[...] = piece_rows(pieces, n)
    for store in stores:
        store.wait()


def space_backward_kernel(
    block, video, core_ref, up_ref, mod_ref, wout_ref, gather_ref, packed_ref, weights_ref, *refs
):
    d_middle_ref, *unit_outs = refs[-10:-7]
    d_out, right, packed, wout, d_probs_ref, d_scores_ref, sems = refs[-7:]
    width = wout.shape[0]
    size = width // HEADS
    factor = size ** (-0.5)
    copies = Copies(sems)
    load_out = copies.start(wout_ref, wout)
    load_packed = copies.start(packed_ref, packed)
    up = dot(gather_ref[...], frame_rows(up_ref[...]))
    d_middle_ref[...] = up.astype(BF16)
    right[:, 3 * width :] = (mod_ref[video, 2:3, :] * up).astype(BF16)
    load_out.wait()
    d_out[...] = dot(right[:, 3 * width :], wout[...], NT).astype(BF16)
    load_packed.wait()
    pairs = pair_windows(width)

    def one_block(g, carry):
        rows = pl.multiple_of(g * block, 16)
        at = pl.ds(rows, block)
        for pair, (start, span, offset) in enumerate(pairs):
            first, both = pair_masks(block, span, offset, size)
            d_rows = two_heads(d_out[at, pl.ds(start, span)], first, both)
            d_probs_ref[pair] = dot(packed[at, pl.ds(2 * width + start, span)], d_rows, NT)
        for pair in range(len(pairs)):
            probs = weights_ref[g * len(pairs) + pair].astype(F32)
            d_probs = d_probs_ref[pair]
            total = jnp.sum(probs * d_probs, 0, keepdims=True) / jnp.sum(probs, 0, keepdims=True)
            d_scores_ref[pair] = (probs * (d_probs - total) * factor).astype(BF16)
        for pair, (start, span, offset) in enumerate(pairs):
            first, both = pair_masks(block, span, offset, size)
            query = two_heads(packed[at, pl.ds(start, span)], first, both)
            key = packed[at, pl.ds(width + start, span)]
            d_rows = two_heads(d_out[at, pl.ds(start, span)], first, both)
            weights, d_scores = weights_ref[g * len(pairs) + pair], d_scores_ref[pair]
            put(right, rows, start, both, per_query(d_scores, key, first))
            put(right, rows, width + start, both, dot(d_scores, query))
            put(right, rows, 2 * width + start, both, dot(weights, d_rows))
        return carry

    lax.fori_loop(0, d_out.shape[0] // block, one_block, 0)
    for store in unit_stores(copies, core_ref[1] & 1, width, right, unit_outs):
        store.wait()


def grad_input_kernel(video, right_ref, d_middle_ref, x_ref, mod_ref, wqkv_ref, *refs):
    out_ref, d_packed, wqkv, sems = refs[-4:]
    width = out_ref.shape[1]
    copies = Copies(sems)
    parts = [pl.ds(part * width, width) for part in range(3)]
    loads = [
        (copies.start(right_ref.at[:, at], d_packed.at[:, at]),
         copies.start(wqkv_ref.at[:, at], wqkv.at[:, at]))
        for at in parts
    ]
    normed, inverse = norm_stats(x_ref[video].astype(F32))
    d_modded = 0.0
    for at, load in zip(parts, loads):
        for one in load:
            one.wait()
        d_modded += dot(d_packed[:, at], wqkv[:, at], NT)
    d_tokens = norm_backward(d_modded, normed, inverse, mod_ref[video, 1:2, :])
    out_ref[...] = (d_middle_ref[...].astype(F32) + d_tokens).astype(BF16)


def bit_of(place_ref, axis, bit):
    return (place_ref[0 if axis == "dp" else 1] >> bit) & 1


def emit_halves(rows, inner, mine, kept_ref, sent_ref):
    columns = kept_ref.shape[2]
    for outer in range(kept_ref.shape[0]):
        low = rows[2 * outer * inner : (2 * outer + 1) * inner, :columns]
        high = rows[(2 * outer + 1) * inner : (2 * outer + 2) * inner, :columns]
        kept_ref[outer] = jnp.where(mine == 0, low, high).astype(BF16)
        sent_ref[outer] = jnp.where(mine == 0, high, low).astype(BF16)


def weight_kernel(videos, cuts, steps, grad_scale, place_ref, *refs):
    left_own, left_got, right_own, right_got = [
        refs[at * videos : (at + 1) * videos] for at in range(4)
    ]
    count = 2 * len(cuts)
    outs, scratch = refs[-4 - 2 * count : -4 - count], refs[-4 - count : -4]
    left_rows, right_rows, total, sems = refs[-4:]
    width = left_rows.shape[1] // 2
    tokens = left_own[0].shape[0]
    copies = Copies(sems)
    core = place_ref[1] & 1
    own = pl.multiple_of(core * (2 * width), 128)
    waits = []
    for unit in range(2):
        now = []
        at = pl.ds(unit * width, width)
        mine = pl.ds(pl.multiple_of(own + unit * width, 128), width)
        for video in range(videos):
            for place, (left, right, columns) in enumerate(
                (
                    (left_own[video], right_own[video], mine),
                    (left_got[video], right_got[video], at),
                )
            ):
                rows = pl.ds((2 * video + place) * tokens, tokens)
                now.append(copies.start(left.at[:, at], left_rows.at[rows, at]))
                now.append(copies.start(right.at[:, columns], right_rows.at[rows, at]))
        waits.append(now)
    done, stores = 0, []
    for part, ((low, high), (axis, bit, inner)) in enumerate(zip(cuts, steps)):
        for unit in range(2):
            start, stop = max(low, unit * width), min(high, (unit + 1) * width)
            if start >= stop:
                continue
            while done <= unit:
                for wait in waits[done]:
                    wait.wait()
                done += 1
            column = pl.multiple_of(core * width, 128) if unit else 0
            left = left_rows[:, pl.ds(column, width)]
            total[:, start - low : stop - low] = (
                dot(left, right_rows[:, start:stop], TN) * grad_scale
            )
        pair = slice(2 * part, 2 * part + 2)
        emit_halves(total, inner, bit_of(place_ref, axis, bit), *scratch[pair])
        stores += [copies.start(a, b) for a, b in zip(scratch[pair], outs[pair])]
    for store in stores:
        store.wait()


def stage_kernel(steps, place_ref, *refs):
    count = len(steps)
    total, outs = refs[-1], refs[-1 - 2 * count : -1]
    for part, (axis, bit, inner) in enumerate(steps):
        kept, got = refs[part], refs[count + part]
        each = kept.shape[1]
        for outer in range(kept.shape[0]):
            total[outer * each : (outer + 1) * each, : kept.shape[2]] = kept[outer].astype(
                F32
            ) + got[outer].astype(F32)
        emit_halves(
            total, inner, bit_of(place_ref, axis, bit), outs[2 * part], outs[2 * part + 1]
        )


def core_stage_kernel(cuts, place_ref, *refs):
    kept_out, sent_out = refs[-2:]
    core = place_ref[1] & 1
    for part, (start, stop) in enumerate(cuts):
        total = refs[part][0].astype(F32) + refs[len(cuts) + part][0].astype(F32)
        rows = total.shape[0] // 2
        low, high = total[:rows], total[rows:]
        kept_out[:, start:stop] = jnp.where(core == 0, low, high).astype(BF16)
        sent_out[:, start:stop] = jnp.where(core == 0, high, low).astype(BF16)


def assemble_kernel(place_ref, kept_ref, got_ref, qkv_ref, out_ref):
    width = out_ref.shape[1]
    core = place_ref[1] & 1
    kept, got = kept_ref[...].astype(F32), got_ref[...].astype(F32)
    low = jnp.where(core == 0, kept, got).astype(BF16)
    high = jnp.where(core == 0, got, kept).astype(BF16)
    qkv_ref[:, : 2 * width] = low
    qkv_ref[:, 2 * width :] = high[:, :width]
    out_ref[...] = high[:, width:]


def swap(x, axis, mask):
    size = lax.axis_size(axis)
    return lax.ppermute(x, axis, [(i, i ^ mask) for i in range(size)])


class Reduction:
    def __init__(self, place, width, late):
        dp_bits = [("dp", bit) for bit in range(lax.axis_size("dp").bit_length() - 1)]
        seq_bits = [("seq", bit) for bit in range(1, lax.axis_size("seq").bit_length() - 1)]
        if late:
            self.orders = (
                dp_bits + seq_bits,
                dp_bits[-1:] + seq_bits[:1] + dp_bits[:-1] + seq_bits[1:],
                seq_bits[:1] + dp_bits + seq_bits[1:],
            )
        else:
            self.orders = (dp_bits + seq_bits, dp_bits[::-1] + seq_bits)
        tiles = 2 * width // 128
        ends = [0, (tiles - tiles // 6) * 64, (tiles - tiles // 6) * 128] if late else [0, width]
        self.cuts = tuple(zip(ends, ends[1:] + [2 * width]))
        self.parts = len(self.orders)
        self.place, self.width = place, width
        self.columns = max(stop - start for start, stop in self.cuts)
        self.bits = dp_bits[::-1] + seq_bits[::-1]
        self.step = 0

    def next_steps(self):
        least = self.width >> len(self.bits)
        steps, shapes = [], []
        for order, (start, stop) in zip(self.orders, self.cuts):
            left = [bit for bit in self.bits if bit not in order[: self.step]]
            above = left.index(order[self.step])
            inner = least << (len(left) - above - 1)
            steps.append((*order[self.step], inner))
            shapes += 2 * [shaped(1 << above, inner, stop - start)]
        return tuple(steps), tuple(shapes)

    def send(self, halves):
        self.kept = halves[0::2]
        self.got = [
            swap(half, order[self.step][0], 1 << order[self.step][1])
            for half, order in zip(halves[1::2], self.orders)
        ]
        self.step += 1

    def stage(self, deps=()):
        steps, shapes = self.next_steps()
        halves = call(
            "stage", 2, functools.partial(stage_kernel, steps), "s" + "v" * len(shapes), shapes,
            "v" * len(shapes),
            [pltpu.VMEM((self.width >> self.step, self.columns), F32)],
        )(self.place, *self.kept, *self.got, deps=deps)
        self.send(halves)
        return halves[0]

    def core_stage(self, deps=()):
        while self.step < len(self.bits):
            self.stage()
        rows = self.width >> (len(self.bits) + 1)
        half = shaped(rows, 2 * self.width)
        self.mine, sent = call(
            "core_stage", 1, functools.partial(core_stage_kernel, self.cuts),
            "s" + "v" * (2 * self.parts), (half, half), "vv",
        )(self.place, *self.kept, *self.got, deps=deps)
        self.other = swap(sent, "seq", 1)
        return self.mine

    def finish(self):
        rows = self.mine.shape[0]
        return call(
            "assemble", 1, assemble_kernel, "svv",
            (shaped(rows, 3 * self.width), shaped(rows, self.width)), "vv",
        )(self.place, self.mine, self.other)


def shards(frames_in, modulation, spatial_qkv, spatial_out, temporal_qkv, temporal_out, cotangent):
    n = lax.axis_size("seq")
    videos, frames, patches, width = frames_in.shape
    all_frames = frames * n
    tokens = frames * patches
    own_patches = patches // n
    rows = frames * own_patches
    padded = -(-rows // 8) * 8
    time_block = 6 * all_frames if own_patches % 6 == 0 else 3 * all_frames
    core = jnp.stack([lax.axis_index("dp"), lax.axis_index("seq")]).astype(jnp.int32)

    joint_padded = -(-videos * rows // 8) * 8
    to_pieces = np.zeros((n * padded, tokens), np.float32)
    to_joint = np.zeros((videos, n * joint_padded, tokens), np.float32)
    by_patch = np.zeros((tokens, n * padded), np.float32)
    joint_by_patch = np.zeros((videos, tokens, n * joint_padded), np.float32)
    for device in range(n):
        for f in range(frames):
            for p in range(own_patches):
                inside = f * own_patches + p
                before = f * patches + device * own_patches + p
                after = p * all_frames + device * frames + f
                to_pieces[device * padded + inside, before] = 1
                by_patch[after, device * padded + inside] = 1
                for v in range(videos):
                    place = device * joint_padded + v * rows + inside
                    to_joint[v, place, before] = 1
                    joint_by_patch[v, after, place] = 1
    from_joint = jnp.asarray(np.concatenate(list(to_joint), 1).T, BF16)
    to_pieces, from_pieces = jnp.asarray(to_pieces, BF16), jnp.asarray(to_pieces.T, BF16)
    to_joint = [jnp.asarray(m, BF16) for m in to_joint]
    by_patch, from_patch = jnp.asarray(by_patch, BF16), jnp.asarray(by_patch.T, BF16)
    joint_from_patch = [jnp.asarray(m.T, BF16) for m in joint_by_patch]
    joint_by_patch = [jnp.asarray(m, BF16) for m in joint_by_patch]

    def exchange(pieces):
        return lax.all_to_all(pieces, "seq", split_axis=0, concat_axis=0, tiled=True)

    piece = shaped(n, padded, width)
    joint_piece = shaped(n, joint_padded, width)
    row = shaped(tokens, width)
    two, three, four = [shaped(tokens, count * width) for count in (2, 3, 4)]
    all_rows = shaped(videos, tokens, width)
    weights_shape = (frames * (HEADS // 2), patches, 2 * patches)

    def vmem(*shape, dtype=BF16):
        return pltpu.VMEM(shape, dtype)

    def sems(count):
        return pltpu.SemaphoreType.DMA((count,))

    weight_refs = [vmem(width, 3 * width), vmem(width, width)]
    x = frames_in.reshape(videos, tokens, width)
    cot = cotangent.reshape(videos, tokens, width)

    def exchange_units(units):
        return swap(units, "seq", 1)

    cot_sent = call("split", 3, functools.partial(split_kernel, n), "vv", piece, "v")(
        cot, to_pieces
    )
    cot_pieces = exchange(cot_sent)
    deps = [cot_sent]
    saved, arrived = [], []
    for v in range(videos):
        sent, *keep = call(
            "space_forward", 14, functools.partial(space_forward_kernel, n, patches, v),
            "aavaavv",
            (joint_piece if v else piece, three, two, shaped(*weights_shape)),
            "vaaa",
            [
                vmem(tokens, width), vmem(tokens, width), vmem(tokens, 2 * width),
                vmem(tokens, 3 * width), vmem(*weights_shape), *weight_refs,
                vmem(HEADS // 2, patches, 2 * patches, dtype=F32), sems(9),
            ],
        )(
            x, cot, modulation, spatial_qkv, spatial_out, to_joint[0] if v else to_pieces,
            to_joint[1], deps=deps,
        )
        deps = [keep[0], cot_pieces]
        arrived.append(exchange(sent))
        saved.append((*keep, exchange_units(keep[1])))

    returned, time_units, out_sent = [], [], core
    for v in range(videos):
        d_middle, out_sent, left, sent, right = call(
            "time", 25, functools.partial(time_kernel, n, time_block, all_frames, v),
            "svvvaavvvv" + ("v" if v else "a"),
            (piece, joint_piece, two, two, four),
            "vvaaa",
            [
                vmem(tokens, width, dtype=F32), vmem(tokens, width), vmem(tokens, width),
                vmem(tokens, 2 * width), vmem(tokens, 3 * width), vmem(tokens, width),
                vmem(tokens, 4 * width), *weight_refs,
                *[vmem(HEADS // 2, time_block, 2 * time_block, dtype=d) for d in (F32, F32, BF16, BF16)],
                sems(9),
            ],
        )(
            core, arrived[v], arrived[v] if v else cot_pieces, modulation, temporal_qkv,
            temporal_out, joint_by_patch[0] if v else by_patch,
            joint_by_patch[1] if v else by_patch, from_patch, joint_from_patch[v], out_sent,
            deps=deps,
        )
        deps = [right]
        returned.append(exchange(d_middle))
        time_units.append((left, exchange_units(left), right, exchange_units(sent)))

    grad_scale = (videos * lax.axis_size("dp") * all_frames * patches) ** (-0.5)

    def weights(units, late, deps=()):
        reduction = Reduction(core, width, late)
        steps, shapes = reduction.next_steps()
        operands = [one for kind in zip(*units) for one in kind]
        halves = call(
            "weights", 10,
            functools.partial(weight_kernel, videos, reduction.cuts, steps, grad_scale),
            "s" + "a" * (4 * videos), shapes, "a" * len(shapes),
            [vmem(*half.shape) for half in shapes] + [
                vmem(2 * videos * tokens, 2 * width), vmem(2 * videos * tokens, 2 * width),
                vmem(width, reduction.columns, dtype=F32), sems(8 * videos + len(shapes)),
            ],
        )(core, *operands, deps=deps)
        reduction.send(halves)
        return reduction, halves[0]

    def grad_of(video, units, d_middle, deps=()):
        return call(
            "grad_input", 8, functools.partial(grad_input_kernel, video), "avvva", row, "v",
            [vmem(tokens, 3 * width), vmem(width, 3 * width), sems(6)],
        )(units[2], d_middle, x, modulation, spatial_qkv, deps=deps)

    d_middles, space_units, grad_input = [], [], []
    for v in range(videos):
        packed, left, weights_saved, left_got = saved[v]
        d_middle, sent, right = call(
            "space_backward", 15, functools.partial(space_backward_kernel, patches, v),
            "svvavav",
            (row, two, four),
            "vaa",
            [
                vmem(tokens, width), vmem(tokens, 4 * width), vmem(tokens, 3 * width),
                vmem(width, width),
                *[vmem(HEADS // 2, patches, 2 * patches, dtype=d) for d in (F32, BF16)], sems(4),
            ],
        )(
            core, returned[v], modulation, spatial_out, from_pieces, packed, weights_saved,
            deps=[*deps, left_got],
        )
        if v == 0:
            time_sum, began = weights(time_units, False, deps=[right])
            deps = [began]
            out_back = exchange(out_sent)
        d_middles.append(d_middle)
        space_units.append((left, left_got, right, exchange_units(sent)))
    grad_input.append(grad_of(0, space_units[0], d_middles[0], deps=[right]))
    began = time_sum.stage(deps=grad_input)
    space_sum, began = weights(space_units, True, deps=[began])
    began = time_sum.stage(deps=[began, out_back])
    for v in range(1, videos):
        grad_input.append(grad_of(v, space_units[v], d_middles[v], deps=[began]))
    began = time_sum.stage(deps=[grad_input[-1]])
    began = space_sum.stage(deps=[began])
    block_out = call("join", 4, join_kernel, "vv", all_rows, "v")(
        out_back, from_joint, deps=[began]
    )
    space_sum.stage(deps=[block_out, time_sum.core_stage(deps=[began])])
    space_sum.core_stage()
    grad_input = jnp.stack(grad_input)
    grad_time, grad_space = time_sum.finish(), space_sum.finish()
    return (
        block_out.reshape(frames_in.shape), grad_input.reshape(frames_in.shape),
        *grad_space, *grad_time,
    )


def solution(mesh):
    return jax.shard_map(
        shards,
        mesh=mesh,
        in_specs=(
            P("dp", "seq", None, None),
            P("dp", None, None),
            P(),
            P(),
            P(),
            P(),
            P("dp", "seq", None, None),
        ),
        out_specs=(
            P("dp", "seq", None, None),
            P("dp", "seq", None, None),
            P(("dp", "seq"), None),
            P(("dp", "seq"), None),
            P(("dp", "seq"), None),
            P(("dp", "seq"), None),
        ),
        check_vma=False,
    )
```

```python
import functools

import jax
import jax.numpy as jnp
import numpy as np
from jax import lax
from jax.experimental import pallas as pl
from jax.experimental.pallas import tpu as pltpu
from jax.sharding import PartitionSpec as P

HEADS = 16
NORM_EPSILON = 1e-06
MASKED = -1e30
TOKEN = jax.ShapeDtypeStruct((8, 128), jnp.float32)
LOG2_E = 1.4426950408889634
MIB = 1024 * 1024
F32 = jnp.float32
BF16 = jnp.bfloat16

NN = (((1,), (0,)), ((), ()))
NT = (((1,), (1,)), ((), ()))
TN = (((0,), (0,)), ((), ()))


def dot(left, right, dims=NN):
    return lax.dot_general(left, right, dims, preferred_element_type=F32)


ROOM = {
    "split": 56, "space_forward": 56, "time": 56, "weights": 56, "space_backward": 56,
    "grad_input": 56, "stage": 24, "last_stage": 16, "assemble": 16, "join": 56,
}
SPACES = {"v": pltpu.VMEM, "s": pltpu.SMEM, "a": pl.ANY, "h": pltpu.HBM}


def call(name, us, body, ins, out_shape, outs, scratch=()):
    def run(*operands, deps=()):
        before = len(operands) + len(deps) + len(out_shape)

        def with_token(*refs):
            refs[before][...] = jnp.zeros(TOKEN.shape, TOKEN.dtype)
            body(*refs[:before], *refs[before + 1 :])

        return pl.pallas_call(
            with_token,
            out_shape=(*out_shape, TOKEN),
            in_specs=[pl.BlockSpec(memory_space=SPACES[s]) for s in ins + "a" * len(deps)],
            out_specs=tuple(pl.BlockSpec(memory_space=SPACES[s]) for s in outs + "v"),
            scratch_shapes=list(scratch),
            compiler_params=pltpu.CompilerParams(vmem_limit_bytes=ROOM[name] * MIB),
            cost_estimate=pl.CostEstimate(
                flops=int(us * 1e9), transcendentals=0, bytes_accessed=int(us * 1e6)
            ),
            name=name,
        )(*operands, *deps)

    return run


def shaped(*shape, dtype=BF16):
    return jax.ShapeDtypeStruct(shape, dtype)


def norm_stats(values):
    mean = jnp.mean(values, -1, keepdims=True)
    centred = values - mean
    inverse = lax.rsqrt(jnp.mean(centred * centred, -1, keepdims=True) + NORM_EPSILON)
    return centred * inverse, inverse


def norm_backward(d_modded, normed, inverse, scale):
    e = d_modded * (1.0 + scale)
    return inverse * (
        e
        - jnp.mean(e, -1, keepdims=True)
        - normed * jnp.mean(e * normed, -1, keepdims=True)
    )


def pair_windows(width):
    size = 2 * width // HEADS
    found = []
    for pair in range(HEADS // 2):
        start = pair * size // 128 * 128
        offset = pair * size - start
        found.append((start, 128 * pl.cdiv(offset + size, 128), offset))
    return found


def pair_masks(rows, span, offset, size):
    lane = lax.broadcasted_iota(jnp.int32, (rows, span), 1)
    first = (lane >= offset) & (lane < offset + size)
    both = (lane >= offset) & (lane < offset + 2 * size)
    return first, both


def two_heads(values, first, both):
    zero = jnp.zeros_like(values)
    return jnp.concatenate(
        [jnp.where(first, values, zero), jnp.where(both & ~first, values, zero)], 0
    )


def per_query(by_key, other, first):
    out = dot(by_key, other, TN)
    rows = out.shape[0] // 2
    return jnp.where(first, out[:rows], out[rows:])


def softmax_by_key(scores, factor, keep):
    if keep is not None:
        scores = jnp.where(keep, scores, MASKED)
    raised = jnp.exp2((scores - jnp.max(scores, 0, keepdims=True)) * (factor * LOG2_E))
    return raised * (1.0 / jnp.sum(raised, 0, keepdims=True))


def put(ref, rows, start, both, value):
    at = (pl.ds(rows, both.shape[0]), pl.ds(start, both.shape[1]))
    ref[at] = jnp.where(both, value.astype(BF16), ref[at])


def frame_rows(pieces):
    n, rows, width = pieces.shape
    return pieces.astype(F32).reshape(n * rows, width).astype(BF16)


def piece_rows(values, n):
    return values.reshape(n, values.shape[0] // n, values.shape[1]).astype(BF16)


def same_video(rows, frames):
    left = lax.broadcasted_iota(jnp.int32, (rows, 2 * rows), 0) // frames
    column = lax.broadcasted_iota(jnp.int32, (rows, 2 * rows), 1)
    right = jnp.where(column >= rows, column - rows, column) // frames
    return left == right


class Copies:
    def __init__(self, sems):
        self.sems, self.used = sems, 0

    def start(self, source, target):
        copy = pltpu.make_async_copy(source, target, self.sems.at[self.used])
        self.used += 1
        copy.start()
        return copy


def qkv_loads(copies, wqkv_ref, wqkv, width):
    parts = [pl.ds(part * width, width) for part in range(3)]
    return [copies.start(wqkv_ref.at[:, at], wqkv.at[:, at]) for at in parts]


def project_qkv(modded, wqkv, loads, packed, width):
    for part, load in enumerate(loads):
        load.wait()
        at = pl.ds(part * width, width)
        packed[:, at] = dot(modded, wqkv[:, at]).astype(BF16)


def split_kernel(n, x_ref, scatter_ref, out_ref):
    out_ref[...] = piece_rows(dot(scatter_ref[...], x_ref[0]), n)


def join_kernel(pieces_ref, gather_ref, *refs):
    *grads, out_ref, grad_out, sems = refs
    copies = Copies(sems)
    stores = [copies.start(grads[v], grad_out.at[v]) for v in range(grad_out.shape[0])]
    rows = dot(gather_ref[...], frame_rows(pieces_ref[...])).astype(BF16)
    out_ref[...] = rows.reshape(out_ref.shape)
    for store in stores:
        store.wait()


def space_forward_kernel(
    n, block, video, x_ref, cot_ref, mod_ref, wqkv_ref, wout_ref, scatter_ref, scatter_cot_ref, *refs
):
    sent_ref, packed_out, left_out, weights_out = refs[-13:-9]
    x, cot, left, packed, weights, wqkv, wout, scores_ref, sems = refs[-9:]
    width = x.shape[1]
    size = width // HEADS
    factor = size ** (-0.5)
    copies = Copies(sems)
    load_x = copies.start(x_ref.at[video], x)
    load_qkv = qkv_loads(copies, wqkv_ref, wqkv, width)
    load_out = copies.start(wout_ref, wout)
    if video:
        load_cot = copies.start(cot_ref.at[video], cot)
    load_x.wait()
    normed, _ = norm_stats(x[...].astype(F32))
    left[:, 0:width] = (
        normed * (1.0 + mod_ref[video, 1:2, :]) + mod_ref[video, 0:1, :]
    ).astype(BF16)
    project_qkv(left[:, 0:width], wqkv, load_qkv, packed, width)
    stores = [copies.start(packed, packed_out)]
    pairs = pair_windows(width)

    def one_block(g, carry):
        rows = pl.multiple_of(g * block, 16)
        at = pl.ds(rows, block)
        for pair, (start, span, offset) in enumerate(pairs):
            first, both = pair_masks(block, span, offset, size)
            query = two_heads(packed[at, pl.ds(start, span)], first, both)
            scores_ref[pair] = dot(packed[at, pl.ds(width + start, span)], query, NT)
        for pair in range(len(pairs)):
            probs = softmax_by_key(scores_ref[pair], factor, None)
            weights[g * len(pairs) + pair] = probs.astype(BF16)
        for pair, (start, span, offset) in enumerate(pairs):
            first, both = pair_masks(block, span, offset, size)
            value = packed[at, pl.ds(2 * width + start, span)]
            attended = per_query(weights[g * len(pairs) + pair], value, first)
            put(left, rows, width + start, both, attended)
        return carry

    lax.fori_loop(0, x.shape[0] // block, one_block, 0)
    stores.append(copies.start(left, left_out))
    stores.append(copies.start(weights, weights_out))
    load_out.wait()
    projected = dot(left[:, width:], wout[...])
    middle = (x[...].astype(F32) + mod_ref[video, 2:3, :] * projected).astype(BF16)
    pieces = dot(scatter_ref[...], middle)
    if video:
        load_cot.wait()
        pieces += dot(scatter_cot_ref[...], cot[...])
    sent_ref[...] = piece_rows(pieces, n)
    for store in stores:
        store.wait()


def unit_stores(copies, core, width, right, outs):
    sent_out, right_out = outs
    other = pl.multiple_of((1 - core) * (2 * width), 128)
    return [
        copies.start(right.at[:, pl.ds(other, 2 * width)], sent_out), copies.start(right, right_out)
    ]


def time_kernel(
    n, block, frames, video, core_ref, middle_ref, cot_ref, mod_ref, wqkv_ref, wout_ref,
    gather_ref, gather_cot_ref, scatter_ref, scatter_out_ref, others_ref, *refs
):
    (d_middle_ref, block_out_ref, left_out, *unit_outs), scratch = refs[-19:-14], refs[-14:]
    normed, x, up, left, packed, d_out, right, wqkv, wout = scratch[:9]
    scores_ref, d_probs_ref, weights_ref, d_scores_ref, sems = scratch[9:]
    width = x.shape[1]
    size = width // HEADS
    factor = size ** (-0.5)
    copies = Copies(sems)
    load_qkv = qkv_loads(copies, wqkv_ref, wqkv, width)
    load_out = copies.start(wout_ref, wout)
    x[...] = dot(gather_ref[...], frame_rows(middle_ref[...])).astype(BF16)
    up[...] = dot(gather_cot_ref[...], frame_rows(cot_ref[...])).astype(BF16)
    normed_now, inverse = norm_stats(x[...].astype(F32))
    normed[...] = normed_now
    left[:, 0:width] = (
        normed_now * (1.0 + mod_ref[video, 4:5, :]) + mod_ref[video, 3:4, :]
    ).astype(BF16)
    right[:, 3 * width :] = (mod_ref[video, 5:6, :] * up[...].astype(F32)).astype(BF16)
    project_qkv(left[:, 0:width], wqkv, load_qkv, packed, width)
    load_out.wait()
    d_out[...] = dot(right[:, 3 * width :], wout[...], NT).astype(BF16)
    keep = same_video(block, frames)

    pairs = pair_windows(width)

    def one_block(g, carry):
        rows = pl.multiple_of(g * block, 16)
        at = pl.ds(rows, block)

        def parts(pair):
            start, span, offset = pairs[pair]
            first, both = pair_masks(block, span, offset, size)
            query = two_heads(packed[at, pl.ds(start, span)], first, both)
            key = packed[at, pl.ds(width + start, span)]
            value = packed[at, pl.ds(2 * width + start, span)]
            d_rows = two_heads(d_out[at, pl.ds(start, span)], first, both)
            return start, first, both, query, key, value, d_rows

        for pair in range(len(pairs)):
            _, _, _, query, key, value, d_rows = parts(pair)
            scores_ref[pair] = dot(key, query, NT)
            d_probs_ref[pair] = dot(value, d_rows, NT)
        for pair in range(len(pairs)):
            probs = softmax_by_key(scores_ref[pair], factor, keep)
            d_probs = d_probs_ref[pair]
            total = jnp.sum(probs * d_probs, 0, keepdims=True)
            weights_ref[pair] = probs.astype(BF16)
            d_scores_ref[pair] = (probs * (d_probs - total) * factor).astype(BF16)
        for pair in range(len(pairs)):
            start, first, both, query, key, value, d_rows = parts(pair)
            weights, d_scores = weights_ref[pair], d_scores_ref[pair]
            put(left, rows, width + start, both, per_query(weights, value, first))
            put(right, rows, start, both, per_query(d_scores, key, first))
            put(right, rows, width + start, both, dot(d_scores, query))
            put(right, rows, 2 * width + start, both, dot(weights, d_rows))
        return carry

    lax.fori_loop(0, x.shape[0] // block, one_block, 0)
    stores = [copies.start(left, left_out)]
    stores += unit_stores(copies, core_ref[1] & 1, width, right, unit_outs)
    d_modded = dot(right[:, 0 : 3 * width], wqkv[...], NT)
    d_middle = up[...].astype(F32) + norm_backward(
        d_modded, normed[...], inverse, mod_ref[video, 4:5, :]
    )
    d_middle_ref[...] = piece_rows(dot(scatter_ref[...], d_middle.astype(BF16)), n)
    projected = dot(left[:, width:], wout[...])
    out = (x[...].astype(F32) + mod_ref[video, 5:6, :] * projected).astype(BF16)
    pieces = dot(scatter_out_ref[...], out)
    if video:
        pieces += others_ref[...].astype(F32).reshape(pieces.shape)
    block_out_ref[...] = piece_rows(pieces, n)
    for store in stores:
        store.wait()


def space_backward_kernel(
    block, video, core_ref, up_ref, mod_ref, wout_ref, gather_ref, packed_ref, weights_ref, *refs
):
    d_middle_ref, *unit_outs = refs[-10:-7]
    d_out, right, packed, wout, d_probs_ref, d_scores_ref, sems = refs[-7:]
    width = wout.shape[0]
    size = width // HEADS
    factor = size ** (-0.5)
    copies = Copies(sems)
    load_out = copies.start(wout_ref, wout)
    load_packed = copies.start(packed_ref, packed)
    up = dot(gather_ref[...], frame_rows(up_ref[...]))
    d_middle_ref[...] = up.astype(BF16)
    right[:, 3 * width :] = (mod_ref[video, 2:3, :] * up).astype(BF16)
    load_out.wait()
    d_out[...] = dot(right[:, 3 * width :], wout[...], NT).astype(BF16)
    load_packed.wait()
    pairs = pair_windows(width)

    def one_block(g, carry):
        rows = pl.multiple_of(g * block, 16)
        at = pl.ds(rows, block)
        for pair, (start, span, offset) in enumerate(pairs):
            first, both = pair_masks(block, span, offset, size)
            d_rows = two_heads(d_out[at, pl.ds(start, span)], first, both)
            d_probs_ref[pair] = dot(packed[at, pl.ds(2 * width + start, span)], d_rows, NT)
        for pair in range(len(pairs)):
            probs = weights_ref[g * len(pairs) + pair].astype(F32)
            d_probs = d_probs_ref[pair]
            total = jnp.sum(probs * d_probs, 0, keepdims=True) / jnp.sum(probs, 0, keepdims=True)
            d_scores_ref[pair] = (probs * (d_probs - total) * factor).astype(BF16)
        for pair, (start, span, offset) in enumerate(pairs):
            first, both = pair_masks(block, span, offset, size)
            query = two_heads(packed[at, pl.ds(start, span)], first, both)
            key = packed[at, pl.ds(width + start, span)]
            d_rows = two_heads(d_out[at, pl.ds(start, span)], first, both)
            weights, d_scores = weights_ref[g * len(pairs) + pair], d_scores_ref[pair]
            put(right, rows, start, both, per_query(d_scores, key, first))
            put(right, rows, width + start, both, dot(d_scores, query))
            put(right, rows, 2 * width + start, both, dot(weights, d_rows))
        return carry

    lax.fori_loop(0, d_out.shape[0] // block, one_block, 0)
    for store in unit_stores(copies, core_ref[1] & 1, width, right, unit_outs):
        store.wait()


def grad_input_kernel(video, right_ref, d_middle_ref, x_ref, mod_ref, wqkv_ref, *refs):
    out_ref, d_packed, wqkv, sems = refs[-4:]
    width = out_ref.shape[1]
    copies = Copies(sems)
    parts = [pl.ds(part * width, width) for part in range(3)]
    loads = [
        (copies.start(right_ref.at[:, at], d_packed.at[:, at]),
         copies.start(wqkv_ref.at[:, at], wqkv.at[:, at]))
        for at in parts
    ]
    normed, inverse = norm_stats(x_ref[video].astype(F32))
    d_modded = 0.0
    for at, load in zip(parts, loads):
        for one in load:
            one.wait()
        d_modded += dot(d_packed[:, at], wqkv[:, at], NT)
    d_tokens = norm_backward(d_modded, normed, inverse, mod_ref[video, 1:2, :])
    out_ref[...] = (d_middle_ref[...].astype(F32) + d_tokens).astype(BF16)


def bit_of(place_ref, axis, bit):
    return (place_ref[0 if axis == "dp" else 1] >> bit) & 1


def emit_halves(rows, inner, mine, kept_ref, sent_ref):
    columns = kept_ref.shape[2]
    for outer in range(kept_ref.shape[0]):
        low = rows[2 * outer * inner : (2 * outer + 1) * inner, :columns]
        high = rows[(2 * outer + 1) * inner : (2 * outer + 2) * inner, :columns]
        kept_ref[outer] = jnp.where(mine == 0, low, high).astype(BF16)
        sent_ref[outer] = jnp.where(mine == 0, high, low).astype(BF16)


def weight_kernel(videos, cuts, steps, grad_scale, place_ref, *refs):
    left_own, left_got, right_own, right_got = [
        refs[at * videos : (at + 1) * videos] for at in range(4)
    ]
    count = 2 * len(cuts)
    outs, scratch = refs[-4 - 2 * count : -4 - count], refs[-4 - count : -4]
    left_rows, right_rows, total, sems = refs[-4:]
    width = left_rows.shape[1] // 2
    tokens = left_own[0].shape[0]
    copies = Copies(sems)
    core = place_ref[1] & 1
    own = pl.multiple_of(core * (2 * width), 128)

    def load(unit):
        now = []
        at = pl.ds(unit * width, width)
        mine = pl.ds(pl.multiple_of(own + unit * width, 128), width)
        for video in range(videos):
            for place, (left, right, columns) in enumerate(
                (
                    (left_own[video], right_own[video], mine),
                    (left_got[video], right_got[video], at),
                )
            ):
                rows = pl.ds((2 * video + place) * tokens, tokens)
                now.append(copies.start(left.at[:, at], left_rows.at[rows, at]))
                now.append(copies.start(right.at[:, columns], right_rows.at[rows, at]))
        return now

    waits = [load(0)]
    done, stores = 0, []
    for part, ((low, high), (axis, bit, inner)) in enumerate(zip(cuts, steps)):
        for unit in range(2):
            start, stop = max(low, unit * width), min(high, (unit + 1) * width)
            if start >= stop:
                continue
            while done <= unit:
                for wait in waits[done]:
                    wait.wait()
                done += 1
                if done == 1:
                    waits.append(load(1))
            column = pl.multiple_of(core * width, 128) if unit else 0
            left = left_rows[:, pl.ds(column, width)]
            total[:, start - low : stop - low] = (
                dot(left, right_rows[:, start:stop], TN) * grad_scale
            )
        pair = slice(2 * part, 2 * part + 2)
        emit_halves(total, inner, bit_of(place_ref, axis, bit), *scratch[pair])
        stores += [copies.start(a, b) for a, b in zip(scratch[pair], outs[pair])]
    for store in stores:
        store.wait()


def add_got(total, kept, got):
    each, columns = kept.shape[1:]
    for outer in range(kept.shape[0]):
        total[outer * each : (outer + 1) * each, :columns] = kept[outer].astype(F32) + got[
            outer
        ].astype(F32)


def stage_kernel(steps, loaded, place_ref, *refs):
    count = len(steps)
    scratch = count + 2 if loaded else 1
    outs, total = refs[-scratch - 2 * count : -scratch], refs[-scratch]
    kept = refs[:count]
    if loaded:
        copies = Copies(refs[-1])
        loads = [copies.start(a, b) for a, b in zip(kept, refs[-count - 1 : -1])]
        kept = refs[-count - 1 : -1]
    for part, (axis, bit, inner) in enumerate(steps):
        if loaded:
            loads[part].wait()
        add_got(total, kept[part], refs[count + part])
        emit_halves(
            total, inner, bit_of(place_ref, axis, bit), outs[2 * part], outs[2 * part + 1]
        )


def last_stage_kernel(bit, cuts, place_ref, *refs):
    count = len(cuts)
    outs, total = refs[-5:-1], refs[-1]
    rows = outs[0].shape[0]
    mine, core = bit_of(place_ref, "seq", bit) == 0, (place_ref[1] & 1) == 0
    for part, (start, stop) in enumerate(cuts):
        add_got(total, refs[part], refs[count + part])
        low, high = total[: 2 * rows, : stop - start], total[2 * rows : 4 * rows, : stop - start]
        near, far = jnp.where(mine, low, high), jnp.where(mine, high, low)
        for place, half in enumerate((near, far)):
            first, second = half[:rows], half[rows:]
            same, other = jnp.where(core, first, second), jnp.where(core, second, first)
            outs[2 * place][:, start:stop] = same.astype(BF16)
            outs[2 * place + 1][:, start:stop] = other.astype(BF16)


def assemble_kernel(place_ref, *refs):
    near, far, near_other, far_other = [ref[...].astype(F32) for ref in refs[:4]]
    qkv_ref, out_ref = refs[-2:]
    width = out_ref.shape[1]
    core = (place_ref[1] & 1) == 0
    mine, others = near + far, near_other + far_other
    low = jnp.where(core, mine, others).astype(BF16)
    high = jnp.where(core, others, mine).astype(BF16)
    qkv_ref[:, : 2 * width] = low
    qkv_ref[:, 2 * width :] = high[:, :width]
    out_ref[...] = high[:, width:]


def swap(x, axis, mask):
    size = lax.axis_size(axis)
    return lax.ppermute(x, axis, [(i, i ^ mask) for i in range(size)])


class Reduction:
    def __init__(self, place, width, late):
        dp_bits = [("dp", bit) for bit in range(lax.axis_size("dp").bit_length() - 1)]
        seq_bits = [("seq", bit) for bit in range(1, lax.axis_size("seq").bit_length() - 1)]
        if late:
            self.orders = (
                dp_bits + seq_bits,
                dp_bits[-1:] + seq_bits[:1] + dp_bits[:-1] + seq_bits[1:],
                seq_bits[:1] + dp_bits + seq_bits[1:],
            )
        else:
            self.orders = (dp_bits + seq_bits, dp_bits[::-1] + seq_bits)
        tiles = 2 * width // 128
        ends = [0, (tiles - tiles // 6) * 64, (tiles - tiles // 6) * 128] if late else [0, width]
        self.cuts = tuple(zip(ends, ends[1:] + [2 * width]))
        self.parts = len(self.orders)
        self.place, self.width = place, width
        self.columns = max(stop - start for start, stop in self.cuts)
        self.bits = dp_bits[::-1] + seq_bits[::-1]
        self.step = 0

    def next_steps(self):
        least = self.width >> len(self.bits)
        steps, shapes = [], []
        for order, (start, stop) in zip(self.orders, self.cuts):
            left = [bit for bit in self.bits if bit not in order[: self.step]]
            above = left.index(order[self.step])
            inner = least << (len(left) - above - 1)
            steps.append((*order[self.step], inner))
            shapes += 2 * [shaped(1 << above, inner, stop - start)]
        return tuple(steps), tuple(shapes)

    def send(self, halves):
        self.kept = halves[0::2]
        self.got = [
            swap(half, order[self.step][0], 1 << order[self.step][1])
            for half, order in zip(halves[1::2], self.orders)
        ]
        self.step += 1

    def stage(self, deps=()):
        steps, shapes = self.next_steps()
        loaded = self.step == 1
        scratch = [pltpu.VMEM((self.width >> self.step, self.columns), F32)]
        if loaded:
            scratch += [pltpu.VMEM(half.shape, BF16) for half in self.kept]
            scratch += [pltpu.SemaphoreType.DMA((self.parts,))]
        *halves, token = call(
            "stage", 2, functools.partial(stage_kernel, steps, loaded),
            "s" + ("h" if loaded else "v") * self.parts + "v" * self.parts, shapes,
            "v" * len(shapes), scratch,
        )(self.place, *self.kept, *self.got, deps=deps)
        self.send(halves)
        return token

    def last_stage(self, deps=()):
        while self.step < len(self.bits) - 1:
            self.stage()
        bit = self.orders[0][-1][1]
        rows = self.width >> (len(self.bits) + 1)
        near, near_other, far, far_other, token = call(
            "last_stage", 1, functools.partial(last_stage_kernel, bit, self.cuts),
            "s" + "v" * (2 * self.parts), (shaped(rows, 2 * self.width),) * 4, "vvvv",
            [pltpu.VMEM((4 * rows, self.columns), F32)],
        )(self.place, *self.kept, *self.got, deps=deps)
        self.sums = (
            near, swap(far, "seq", 1 << bit), swap(near_other, "seq", 1),
            swap(far_other, "seq", (1 << bit) | 1),
        )
        return token

    def finish(self, deps=()):
        rows = self.sums[0].shape[0]
        return call(
            "assemble", 1, assemble_kernel, "svvvv",
            (shaped(rows, 3 * self.width), shaped(rows, self.width)), "vv",
        )(self.place, *self.sums, deps=deps)


def shards(frames_in, modulation, spatial_qkv, spatial_out, temporal_qkv, temporal_out, cotangent):
    n = lax.axis_size("seq")
    videos, frames, patches, width = frames_in.shape
    all_frames = frames * n
    tokens = frames * patches
    own_patches = patches // n
    rows = frames * own_patches
    padded = -(-rows // 8) * 8
    time_block = 6 * all_frames if own_patches % 6 == 0 else 3 * all_frames
    core = jnp.stack([lax.axis_index("dp"), lax.axis_index("seq")]).astype(jnp.int32)

    joint_padded = -(-videos * rows // 8) * 8
    to_pieces = np.zeros((n * padded, tokens), np.float32)
    to_joint = np.zeros((videos, n * joint_padded, tokens), np.float32)
    by_patch = np.zeros((tokens, n * padded), np.float32)
    joint_by_patch = np.zeros((videos, tokens, n * joint_padded), np.float32)
    for device in range(n):
        for f in range(frames):
            for p in range(own_patches):
                inside = f * own_patches + p
                before = f * patches + device * own_patches + p
                after = p * all_frames + device * frames + f
                to_pieces[device * padded + inside, before] = 1
                by_patch[after, device * padded + inside] = 1
                for v in range(videos):
                    place = device * joint_padded + v * rows + inside
                    to_joint[v, place, before] = 1
                    joint_by_patch[v, after, place] = 1
    from_joint = jnp.asarray(np.concatenate(list(to_joint), 1).T, BF16)
    to_pieces, from_pieces = jnp.asarray(to_pieces, BF16), jnp.asarray(to_pieces.T, BF16)
    to_joint = [jnp.asarray(m, BF16) for m in to_joint]
    by_patch, from_patch = jnp.asarray(by_patch, BF16), jnp.asarray(by_patch.T, BF16)
    joint_from_patch = [jnp.asarray(m.T, BF16) for m in joint_by_patch]
    joint_by_patch = [jnp.asarray(m, BF16) for m in joint_by_patch]

    def exchange(pieces):
        return lax.all_to_all(pieces, "seq", split_axis=0, concat_axis=0, tiled=True)

    piece = shaped(n, padded, width)
    joint_piece = shaped(n, joint_padded, width)
    row = shaped(tokens, width)
    two, three, four = [shaped(tokens, count * width) for count in (2, 3, 4)]
    all_rows = shaped(videos, tokens, width)
    weights_shape = (frames * (HEADS // 2), patches, 2 * patches)

    def vmem(*shape, dtype=BF16):
        return pltpu.VMEM(shape, dtype)

    def sems(count):
        return pltpu.SemaphoreType.DMA((count,))

    weight_refs = [vmem(width, 3 * width), vmem(width, width)]
    x = frames_in.reshape(videos, tokens, width)
    cot = cotangent.reshape(videos, tokens, width)

    def exchange_units(units):
        return swap(units, "seq", 1)

    cot_sent, token = call("split", 3, functools.partial(split_kernel, n), "vv", (piece,), "v")(
        cot, to_pieces
    )
    cot_pieces = exchange(cot_sent)
    deps = [token]
    saved, arrived = [], []
    for v in range(videos):
        sent, *keep, token = call(
            "space_forward", 14, functools.partial(space_forward_kernel, n, patches, v),
            "aavaavv",
            (joint_piece if v else piece, three, two, shaped(*weights_shape)),
            "vaaa",
            [
                vmem(tokens, width), vmem(tokens, width), vmem(tokens, 2 * width),
                vmem(tokens, 3 * width), vmem(*weights_shape), *weight_refs,
                vmem(HEADS // 2, patches, 2 * patches, dtype=F32), sems(9),
            ],
        )(
            x, cot, modulation, spatial_qkv, spatial_out, to_joint[0] if v else to_pieces,
            to_joint[1], deps=deps,
        )
        deps = [token, cot_pieces]
        arrived.append(exchange(sent))
        saved.append((*keep, exchange_units(keep[1])))

    returned, time_units, out_sent = [], [], core
    for v in range(videos):
        d_middle, out_sent, left, sent, right, token = call(
            "time", 25, functools.partial(time_kernel, n, time_block, all_frames, v),
            "svvvaavvvv" + ("v" if v else "a"),
            (piece, joint_piece, two, two, four),
            "vvaaa",
            [
                vmem(tokens, width, dtype=F32), vmem(tokens, width), vmem(tokens, width),
                vmem(tokens, 2 * width), vmem(tokens, 3 * width), vmem(tokens, width),
                vmem(tokens, 4 * width), *weight_refs,
                *[vmem(HEADS // 2, time_block, 2 * time_block, dtype=d) for d in (F32, F32, BF16, BF16)],
                sems(9),
            ],
        )(
            core, arrived[v], arrived[v] if v else cot_pieces, modulation, temporal_qkv,
            temporal_out, joint_by_patch[0] if v else by_patch,
            joint_by_patch[1] if v else by_patch, from_patch, joint_from_patch[v], out_sent,
            deps=deps,
        )
        deps = [token]
        returned.append(exchange(d_middle))
        time_units.append((left, exchange_units(left), right, exchange_units(sent)))

    grad_scale = (videos * lax.axis_size("dp") * all_frames * patches) ** (-0.5)

    def weights(units, late, deps=()):
        reduction = Reduction(core, width, late)
        steps, shapes = reduction.next_steps()
        operands = [one for kind in zip(*units) for one in kind]
        *halves, token = call(
            "weights", 10,
            functools.partial(weight_kernel, videos, reduction.cuts, steps, grad_scale),
            "s" + "a" * (4 * videos), shapes, "a" * len(shapes),
            [vmem(*half.shape) for half in shapes] + [
                vmem(2 * videos * tokens, 2 * width), vmem(2 * videos * tokens, 2 * width),
                vmem(width, reduction.columns, dtype=F32), sems(8 * videos + len(shapes)),
            ],
        )(core, *operands, deps=deps)
        reduction.send(halves)
        return reduction, token

    def grad_of(video, units, d_middle, deps=()):
        return call(
            "grad_input", 8, functools.partial(grad_input_kernel, video), "avvva", (row,), "v",
            [vmem(tokens, 3 * width), vmem(width, 3 * width), sems(6)],
        )(units[2], d_middle, x, modulation, spatial_qkv, deps=deps)

    d_middles, space_units = [], []
    for v in range(videos):
        packed, left, weights_saved, left_got = saved[v]
        d_middle, sent, right, token = call(
            "space_backward", 15, functools.partial(space_backward_kernel, patches, v),
            "svvavav",
            (row, two, four),
            "vaa",
            [
                vmem(tokens, width), vmem(tokens, 4 * width), vmem(tokens, 3 * width),
                vmem(width, width),
                *[vmem(HEADS // 2, patches, 2 * patches, dtype=d) for d in (F32, BF16)], sems(4),
            ],
        )(
            core, returned[v], modulation, spatial_out, from_pieces, packed, weights_saved,
            deps=[*deps, left_got],
        )
        if v == 0:
            time_sum, began = weights(time_units, False, deps=[token])
            deps = [began]
            out_back = exchange(out_sent)
        d_middles.append(d_middle)
        space_units.append((left, left_got, right, exchange_units(sent)))
    first_grad, token = grad_of(0, space_units[0], d_middles[0], deps=[token])
    grad_input = [first_grad]
    token = time_sum.stage(deps=[token])
    space_sum, token = weights(space_units, True, deps=[token])
    token = time_sum.stage(deps=[token, out_back])
    for v in range(1, videos):
        one_grad, token = grad_of(v, space_units[v], d_middles[v], deps=[token])
        grad_input.append(one_grad)
    token = time_sum.last_stage(deps=[token])
    token = space_sum.stage(deps=[token])
    block_out, grad_input, token = call(
        "join", 4, join_kernel, "vv" + "a" * videos, (all_rows, all_rows), "va", [sems(videos)]
    )(out_back, from_joint, *grad_input, deps=[token])
    token = space_sum.stage(deps=[token])
    *grad_time, token = time_sum.finish(deps=[token])
    space_sum.last_stage(deps=[token])
    *grad_space, _ = space_sum.finish()
    return (
        block_out.reshape(frames_in.shape), grad_input.reshape(frames_in.shape),
        *grad_space, *grad_time,
    )


def solution(mesh):
    return jax.shard_map(
        shards,
        mesh=mesh,
        in_specs=(
            P("dp", "seq", None, None),
            P("dp", None, None),
            P(),
            P(),
            P(),
            P(),
            P("dp", "seq", None, None),
        ),
        out_specs=(
            P("dp", "seq", None, None),
            P("dp", "seq", None, None),
            P(("dp", "seq"), None),
            P(("dp", "seq"), None),
            P(("dp", "seq"), None),
            P(("dp", "seq"), None),
        ),
        check_vma=False,
    )
```

```python
import functools

import jax
import jax.numpy as jnp
import numpy as np
from jax import lax
from jax.experimental import pallas as pl
from jax.experimental.pallas import tpu as pltpu
from jax.sharding import PartitionSpec as P

HEADS = 16
NORM_EPSILON = 1e-06
MASKED = -1e30
TOKEN = jax.ShapeDtypeStruct((8, 128), jnp.float32)
LOG2_E = 1.4426950408889634
MIB = 1024 * 1024
F32 = jnp.float32
BF16 = jnp.bfloat16

NN = (((1,), (0,)), ((), ()))
NT = (((1,), (1,)), ((), ()))
TN = (((0,), (0,)), ((), ()))


def dot(left, right, dims=NN):
    return lax.dot_general(left, right, dims, preferred_element_type=F32)


ROOM = {
    "split": 56, "space_forward": 56, "time": 56, "weights": 56, "space_backward": 56,
    "grad_input": 56, "stage": 24, "last_stage": 16, "assemble": 16, "join": 56,
}
SPACES = {"v": pltpu.VMEM, "s": pltpu.SMEM, "a": pl.ANY}


def call(name, us, body, ins, out_shape, outs, scratch=()):
    def run(*operands, deps=()):
        before = len(operands) + len(deps) + len(out_shape)

        def with_token(*refs):
            refs[before][...] = jnp.zeros(TOKEN.shape, TOKEN.dtype)
            body(*refs[:before], *refs[before + 1 :])

        return pl.pallas_call(
            with_token,
            out_shape=(*out_shape, TOKEN),
            in_specs=[pl.BlockSpec(memory_space=SPACES[s]) for s in ins + "a" * len(deps)],
            out_specs=tuple(pl.BlockSpec(memory_space=SPACES[s]) for s in outs + "v"),
            scratch_shapes=list(scratch),
            compiler_params=pltpu.CompilerParams(vmem_limit_bytes=ROOM[name] * MIB),
            cost_estimate=pl.CostEstimate(
                flops=int(us * 1e9), transcendentals=0, bytes_accessed=int(us * 1e6)
            ),
            name=name,
        )(*operands, *deps)

    return run


def shaped(*shape, dtype=BF16):
    return jax.ShapeDtypeStruct(shape, dtype)


def norm_stats(values):
    mean = jnp.mean(values, -1, keepdims=True)
    centred = values - mean
    inverse = lax.rsqrt(jnp.mean(centred * centred, -1, keepdims=True) + NORM_EPSILON)
    return centred * inverse, inverse


def norm_backward(d_modded, normed, inverse, scale):
    e = d_modded * (1.0 + scale)
    return inverse * (
        e
        - jnp.mean(e, -1, keepdims=True)
        - normed * jnp.mean(e * normed, -1, keepdims=True)
    )


def pair_windows(width):
    size = 2 * width // HEADS
    found = []
    for pair in range(HEADS // 2):
        start = pair * size // 128 * 128
        offset = pair * size - start
        found.append((start, 128 * pl.cdiv(offset + size, 128), offset))
    return found


def pair_masks(rows, span, offset, size):
    lane = lax.broadcasted_iota(jnp.int32, (rows, span), 1)
    first = (lane >= offset) & (lane < offset + size)
    both = (lane >= offset) & (lane < offset + 2 * size)
    return first, both


def two_heads(values, first, both):
    zero = jnp.zeros_like(values)
    return jnp.concatenate(
        [jnp.where(first, values, zero), jnp.where(both & ~first, values, zero)], 0
    )


def per_query(by_key, other, first):
    out = dot(by_key, other, TN)
    rows = out.shape[0] // 2
    return jnp.where(first, out[:rows], out[rows:])


def softmax_by_key(scores, factor, keep):
    if keep is not None:
        scores = jnp.where(keep, scores, MASKED)
    raised = jnp.exp2((scores - jnp.max(scores, 0, keepdims=True)) * (factor * LOG2_E))
    return raised * (1.0 / jnp.sum(raised, 0, keepdims=True))


def put(ref, rows, start, both, value):
    at = (pl.ds(rows, both.shape[0]), pl.ds(start, both.shape[1]))
    ref[at] = jnp.where(both, value.astype(BF16), ref[at])


def frame_rows(pieces):
    n, rows, width = pieces.shape
    return pieces.astype(F32).reshape(n * rows, width).astype(BF16)


def piece_rows(values, n):
    return values.reshape(n, values.shape[0] // n, values.shape[1]).astype(BF16)


def same_video(rows, frames):
    left = lax.broadcasted_iota(jnp.int32, (rows, 2 * rows), 0) // frames
    column = lax.broadcasted_iota(jnp.int32, (rows, 2 * rows), 1)
    right = jnp.where(column >= rows, column - rows, column) // frames
    return left == right


class Copies:
    def __init__(self, sems):
        self.sems, self.used = sems, 0

    def start(self, source, target):
        copy = pltpu.make_async_copy(source, target, self.sems.at[self.used])
        self.used += 1
        copy.start()
        return copy


def qkv_loads(copies, wqkv_ref, wqkv, width):
    parts = [pl.ds(part * width, width) for part in range(3)]
    return [copies.start(wqkv_ref.at[:, at], wqkv.at[:, at]) for at in parts]


def project_qkv(modded, wqkv, loads, packed, width):
    for part, load in enumerate(loads):
        load.wait()
        at = pl.ds(part * width, width)
        packed[:, at] = dot(modded, wqkv[:, at]).astype(BF16)


def split_kernel(n, x_ref, scatter_ref, out_ref):
    out_ref[...] = piece_rows(dot(scatter_ref[...], x_ref[0]), n)


def join_kernel(pieces_ref, gather_ref, *refs):
    *grads, out_ref, grad_out = refs
    for video in range(grad_out.shape[0]):
        grad_out[video] = grads[video][...]
    rows = dot(gather_ref[...], frame_rows(pieces_ref[...])).astype(BF16)
    out_ref[...] = rows.reshape(out_ref.shape)


def space_forward_kernel(
    n, block, video, x_ref, cot_ref, mod_ref, wqkv_ref, wout_ref, scatter_ref, scatter_cot_ref, *refs
):
    sent_ref, packed_out, left_out, weights_out = refs[-13:-9]
    x, cot, left, packed, weights, wqkv, wout, scores_ref, sems = refs[-9:]
    width = x.shape[1]
    size = width // HEADS
    factor = size ** (-0.5)
    copies = Copies(sems)
    load_x = copies.start(x_ref.at[video], x)
    load_qkv = qkv_loads(copies, wqkv_ref, wqkv, width)
    load_out = copies.start(wout_ref, wout)
    if video:
        load_cot = copies.start(cot_ref.at[video], cot)
    load_x.wait()
    normed, _ = norm_stats(x[...].astype(F32))
    left[:, 0:width] = (
        normed * (1.0 + mod_ref[video, 1:2, :]) + mod_ref[video, 0:1, :]
    ).astype(BF16)
    project_qkv(left[:, 0:width], wqkv, load_qkv, packed, width)
    stores = [copies.start(packed, packed_out)]
    pairs = pair_windows(width)

    def one_block(g, carry):
        rows = pl.multiple_of(g * block, 16)
        at = pl.ds(rows, block)
        for pair, (start, span, offset) in enumerate(pairs):
            first, both = pair_masks(block, span, offset, size)
            query = two_heads(packed[at, pl.ds(start, span)], first, both)
            scores_ref[pair] = dot(packed[at, pl.ds(width + start, span)], query, NT)
        for pair in range(len(pairs)):
            probs = softmax_by_key(scores_ref[pair], factor, None)
            weights[g * len(pairs) + pair] = probs.astype(BF16)
        for pair, (start, span, offset) in enumerate(pairs):
            first, both = pair_masks(block, span, offset, size)
            value = packed[at, pl.ds(2 * width + start, span)]
            attended = per_query(weights[g * len(pairs) + pair], value, first)
            put(left, rows, width + start, both, attended)
        return carry

    lax.fori_loop(0, x.shape[0] // block, one_block, 0)
    stores.append(copies.start(left, left_out))
    stores.append(copies.start(weights, weights_out))
    load_out.wait()
    projected = dot(left[:, width:], wout[...])
    middle = (x[...].astype(F32) + mod_ref[video, 2:3, :] * projected).astype(BF16)
    pieces = dot(scatter_ref[...], middle)
    if video:
        load_cot.wait()
        pieces += dot(scatter_cot_ref[...], cot[...])
    sent_ref[...] = piece_rows(pieces, n)
    for store in stores:
        store.wait()


def unit_stores(copies, core, width, right, outs):
    sent_out, right_out = outs
    other = pl.multiple_of((1 - core) * (2 * width), 128)
    return [
        copies.start(right.at[:, pl.ds(other, 2 * width)], sent_out), copies.start(right, right_out)
    ]


def time_kernel(
    n, block, frames, video, core_ref, middle_ref, cot_ref, mod_ref, wqkv_ref, wout_ref,
    gather_ref, gather_cot_ref, scatter_ref, scatter_out_ref, others_ref, *refs
):
    (d_middle_ref, block_out_ref, left_out, *unit_outs), scratch = refs[-19:-14], refs[-14:]
    normed, x, up, left, packed, d_out, right, wqkv, wout = scratch[:9]
    scores_ref, d_probs_ref, weights_ref, d_scores_ref, sems = scratch[9:]
    width = x.shape[1]
    size = width // HEADS
    factor = size ** (-0.5)
    copies = Copies(sems)
    load_qkv = qkv_loads(copies, wqkv_ref, wqkv, width)
    load_out = copies.start(wout_ref, wout)
    x[...] = dot(gather_ref[...], frame_rows(middle_ref[...])).astype(BF16)
    up[...] = dot(gather_cot_ref[...], frame_rows(cot_ref[...])).astype(BF16)
    normed_now, inverse = norm_stats(x[...].astype(F32))
    normed[...] = normed_now
    left[:, 0:width] = (
        normed_now * (1.0 + mod_ref[video, 4:5, :]) + mod_ref[video, 3:4, :]
    ).astype(BF16)
    right[:, 3 * width :] = (mod_ref[video, 5:6, :] * up[...].astype(F32)).astype(BF16)
    project_qkv(left[:, 0:width], wqkv, load_qkv, packed, width)
    load_out.wait()
    d_out[...] = dot(right[:, 3 * width :], wout[...], NT).astype(BF16)
    keep = same_video(block, frames)

    pairs = pair_windows(width)

    def one_block(g, carry):
        rows = pl.multiple_of(g * block, 16)
        at = pl.ds(rows, block)

        def parts(pair):
            start, span, offset = pairs[pair]
            first, both = pair_masks(block, span, offset, size)
            query = two_heads(packed[at, pl.ds(start, span)], first, both)
            key = packed[at, pl.ds(width + start, span)]
            value = packed[at, pl.ds(2 * width + start, span)]
            d_rows = two_heads(d_out[at, pl.ds(start, span)], first, both)
            return start, first, both, query, key, value, d_rows

        for pair in range(len(pairs)):
            _, _, _, query, key, value, d_rows = parts(pair)
            scores_ref[pair] = dot(key, query, NT)
            d_probs_ref[pair] = dot(value, d_rows, NT)
        for pair in range(len(pairs)):
            probs = softmax_by_key(scores_ref[pair], factor, keep)
            d_probs = d_probs_ref[pair]
            total = jnp.sum(probs * d_probs, 0, keepdims=True)
            weights_ref[pair] = probs.astype(BF16)
            d_scores_ref[pair] = (probs * (d_probs - total) * factor).astype(BF16)
        for pair in range(len(pairs)):
            start, first, both, query, key, value, d_rows = parts(pair)
            weights, d_scores = weights_ref[pair], d_scores_ref[pair]
            put(left, rows, width + start, both, per_query(weights, value, first))
            put(right, rows, start, both, per_query(d_scores, key, first))
            put(right, rows, width + start, both, dot(d_scores, query))
            put(right, rows, 2 * width + start, both, dot(weights, d_rows))
        return carry

    lax.fori_loop(0, x.shape[0] // block, one_block, 0)
    stores = [copies.start(left, left_out)]
    stores += unit_stores(copies, core_ref[1] & 1, width, right, unit_outs)
    d_modded = dot(right[:, 0 : 3 * width], wqkv[...], NT)
    d_middle = up[...].astype(F32) + norm_backward(
        d_modded, normed[...], inverse, mod_ref[video, 4:5, :]
    )
    d_middle_ref[...] = piece_rows(dot(scatter_ref[...], d_middle.astype(BF16)), n)
    projected = dot(left[:, width:], wout[...])
    out = (x[...].astype(F32) + mod_ref[video, 5:6, :] * projected).astype(BF16)
    pieces = dot(scatter_out_ref[...], out)
    if video:
        pieces += others_ref[...].astype(F32).reshape(pieces.shape)
    block_out_ref[...] = piece_rows(pieces, n)
    for store in stores:
        store.wait()


def space_backward_kernel(
    block, video, core_ref, up_ref, mod_ref, wout_ref, gather_ref, packed_ref, weights_ref, *refs
):
    d_middle_ref, *unit_outs = refs[-10:-7]
    d_out, right, packed, wout, d_probs_ref, d_scores_ref, sems = refs[-7:]
    width = wout.shape[0]
    size = width // HEADS
    factor = size ** (-0.5)
    copies = Copies(sems)
    load_out = copies.start(wout_ref, wout)
    load_packed = copies.start(packed_ref, packed)
    up = dot(gather_ref[...], frame_rows(up_ref[...]))
    d_middle_ref[...] = up.astype(BF16)
    right[:, 3 * width :] = (mod_ref[video, 2:3, :] * up).astype(BF16)
    load_out.wait()
    d_out[...] = dot(right[:, 3 * width :], wout[...], NT).astype(BF16)
    load_packed.wait()
    pairs = pair_windows(width)

    def one_block(g, carry):
        rows = pl.multiple_of(g * block, 16)
        at = pl.ds(rows, block)
        for pair, (start, span, offset) in enumerate(pairs):
            first, both = pair_masks(block, span, offset, size)
            d_rows = two_heads(d_out[at, pl.ds(start, span)], first, both)
            d_probs_ref[pair] = dot(packed[at, pl.ds(2 * width + start, span)], d_rows, NT)
        for pair in range(len(pairs)):
            probs = weights_ref[g * len(pairs) + pair].astype(F32)
            d_probs = d_probs_ref[pair]
            total = jnp.sum(probs * d_probs, 0, keepdims=True) / jnp.sum(probs, 0, keepdims=True)
            d_scores_ref[pair] = (probs * (d_probs - total) * factor).astype(BF16)
        for pair, (start, span, offset) in enumerate(pairs):
            first, both = pair_masks(block, span, offset, size)
            query = two_heads(packed[at, pl.ds(start, span)], first, both)
            key = packed[at, pl.ds(width + start, span)]
            d_rows = two_heads(d_out[at, pl.ds(start, span)], first, both)
            weights, d_scores = weights_ref[g * len(pairs) + pair], d_scores_ref[pair]
            put(right, rows, start, both, per_query(d_scores, key, first))
            put(right, rows, width + start, both, dot(d_scores, query))
            put(right, rows, 2 * width + start, both, dot(weights, d_rows))
        return carry

    lax.fori_loop(0, d_out.shape[0] // block, one_block, 0)
    for store in unit_stores(copies, core_ref[1] & 1, width, right, unit_outs):
        store.wait()


def grad_input_kernel(video, right_ref, d_middle_ref, x_ref, mod_ref, wqkv_ref, *refs):
    out_ref, d_packed, wqkv, sems = refs[-4:]
    width = out_ref.shape[1]
    copies = Copies(sems)
    parts = [pl.ds(part * width, width) for part in range(3)]
    loads = [
        (copies.start(right_ref.at[:, at], d_packed.at[:, at]),
         copies.start(wqkv_ref.at[:, at], wqkv.at[:, at]))
        for at in parts
    ]
    normed, inverse = norm_stats(x_ref[video].astype(F32))
    d_modded = 0.0
    for at, load in zip(parts, loads):
        for one in load:
            one.wait()
        d_modded += dot(d_packed[:, at], wqkv[:, at], NT)
    d_tokens = norm_backward(d_modded, normed, inverse, mod_ref[video, 1:2, :])
    out_ref[...] = (d_middle_ref[...].astype(F32) + d_tokens).astype(BF16)


def bit_of(place_ref, axis, bit):
    return (place_ref[0 if axis == "dp" else 1] >> bit) & 1


def emit_halves(rows, inner, mine, kept_ref, sent_ref):
    columns = kept_ref.shape[2]
    for outer in range(kept_ref.shape[0]):
        low = rows[2 * outer * inner : (2 * outer + 1) * inner, :columns]
        high = rows[(2 * outer + 1) * inner : (2 * outer + 2) * inner, :columns]
        kept_ref[outer] = jnp.where(mine == 0, low, high).astype(BF16)
        sent_ref[outer] = jnp.where(mine == 0, high, low).astype(BF16)


def weight_kernel(videos, cuts, steps, grad_scale, place_ref, *refs):
    left_own, left_got, right_own, right_got = [
        refs[at * videos : (at + 1) * videos] for at in range(4)
    ]
    count = 2 * len(cuts)
    outs, scratch = refs[-4 - 2 * count : -4 - count], refs[-4 - count : -4]
    left_rows, right_rows, total, sems = refs[-4:]
    width = left_rows.shape[1] // 2
    tokens = left_own[0].shape[0]
    copies = Copies(sems)
    core = place_ref[1] & 1
    own = pl.multiple_of(core * (2 * width), 128)

    def load(unit):
        now = []
        at = pl.ds(unit * width, width)
        mine = pl.ds(pl.multiple_of(own + unit * width, 128), width)
        for video in range(videos):
            for place, (left, right, columns) in enumerate(
                (
                    (left_own[video], right_own[video], mine),
                    (left_got[video], right_got[video], at),
                )
            ):
                rows = pl.ds((2 * video + place) * tokens, tokens)
                now.append(copies.start(left.at[:, at], left_rows.at[rows, at]))
                now.append(copies.start(right.at[:, columns], right_rows.at[rows, at]))
        return now

    waits = [load(0), load(1)]
    done, stores = 0, []
    for part, ((low, high), (axis, bit, inner)) in enumerate(zip(cuts, steps)):
        for unit in range(2):
            start, stop = max(low, unit * width), min(high, (unit + 1) * width)
            if start >= stop:
                continue
            while done <= unit:
                for wait in waits[done]:
                    wait.wait()
                done += 1
            column = pl.multiple_of(core * width, 128) if unit else 0
            left = left_rows[:, pl.ds(column, width)]
            total[:, start - low : stop - low] = (
                dot(left, right_rows[:, start:stop], TN) * grad_scale
            )
        pair = slice(2 * part, 2 * part + 2)
        emit_halves(total, inner, bit_of(place_ref, axis, bit), *scratch[pair])
        stores += [copies.start(a, b) for a, b in zip(scratch[pair], outs[pair])]
    for store in stores:
        store.wait()


def add_got(total, kept, got):
    each, columns = kept.shape[1:]
    for outer in range(kept.shape[0]):
        total[outer * each : (outer + 1) * each, :columns] = kept[outer].astype(F32) + got[
            outer
        ].astype(F32)


def stage_kernel(steps, place_ref, *refs):
    count = len(steps)
    total, outs = refs[-1], refs[-1 - 2 * count : -1]
    for part, (axis, bit, inner) in enumerate(steps):
        add_got(total, refs[part], refs[count + part])
        emit_halves(
            total, inner, bit_of(place_ref, axis, bit), outs[2 * part], outs[2 * part + 1]
        )


def last_stage_kernel(bit, cuts, place_ref, *refs):
    count = len(cuts)
    outs, total = refs[-5:-1], refs[-1]
    rows = outs[0].shape[0]
    mine, core = bit_of(place_ref, "seq", bit) == 0, (place_ref[1] & 1) == 0
    for part, (start, stop) in enumerate(cuts):
        add_got(total, refs[part], refs[count + part])
        low, high = total[: 2 * rows, : stop - start], total[2 * rows : 4 * rows, : stop - start]
        near, far = jnp.where(mine, low, high), jnp.where(mine, high, low)
        for place, half in enumerate((near, far)):
            first, second = half[:rows], half[rows:]
            same, other = jnp.where(core, first, second), jnp.where(core, second, first)
            outs[2 * place][:, start:stop] = same.astype(BF16)
            outs[2 * place + 1][:, start:stop] = other.astype(BF16)


def assemble_kernel(place_ref, *refs):
    near, far, near_other, far_other = [ref[...].astype(F32) for ref in refs[:4]]
    qkv_ref, out_ref = refs[-2:]
    width = out_ref.shape[1]
    core = (place_ref[1] & 1) == 0
    mine, others = near + far, near_other + far_other
    low = jnp.where(core, mine, others).astype(BF16)
    high = jnp.where(core, others, mine).astype(BF16)
    qkv_ref[:, : 2 * width] = low
    qkv_ref[:, 2 * width :] = high[:, :width]
    out_ref[...] = high[:, width:]


def swap(x, axis, mask):
    size = lax.axis_size(axis)
    return lax.ppermute(x, axis, [(i, i ^ mask) for i in range(size)])


class Reduction:
    def __init__(self, place, width, late):
        dp_bits = [("dp", bit) for bit in range(lax.axis_size("dp").bit_length() - 1)]
        seq_bits = [("seq", bit) for bit in range(1, lax.axis_size("seq").bit_length() - 1)]
        if late:
            self.orders = (
                dp_bits + seq_bits,
                dp_bits[-1:] + seq_bits[:1] + dp_bits[:-1] + seq_bits[1:],
                seq_bits[:1] + dp_bits + seq_bits[1:],
            )
        else:
            self.orders = (dp_bits + seq_bits, dp_bits[::-1] + seq_bits)
        tiles = 2 * width // 128
        ends = [0, (tiles - tiles // 6) * 64, (tiles - tiles // 6) * 128] if late else [0, width]
        self.cuts = tuple(zip(ends, ends[1:] + [2 * width]))
        self.parts = len(self.orders)
        self.place, self.width = place, width
        self.columns = max(stop - start for start, stop in self.cuts)
        self.bits = dp_bits[::-1] + seq_bits[::-1]
        self.step = 0

    def next_steps(self):
        least = self.width >> len(self.bits)
        steps, shapes = [], []
        for order, (start, stop) in zip(self.orders, self.cuts):
            left = [bit for bit in self.bits if bit not in order[: self.step]]
            above = left.index(order[self.step])
            inner = least << (len(left) - above - 1)
            steps.append((*order[self.step], inner))
            shapes += 2 * [shaped(1 << above, inner, stop - start)]
        return tuple(steps), tuple(shapes)

    def send(self, halves):
        self.kept = halves[0::2]
        self.got = [
            swap(half, order[self.step][0], 1 << order[self.step][1])
            for half, order in zip(halves[1::2], self.orders)
        ]
        self.step += 1

    def stage(self, deps=()):
        steps, shapes = self.next_steps()
        *halves, token = call(
            "stage", 2, functools.partial(stage_kernel, steps), "s" + "v" * (2 * self.parts),
            shapes, "v" * len(shapes),
            [pltpu.VMEM((self.width >> self.step, self.columns), F32)],
        )(self.place, *self.kept, *self.got, deps=deps)
        self.send(halves)
        return token

    def last_stage(self, deps=()):
        while self.step < len(self.bits) - 1:
            self.stage()
        bit = self.orders[0][-1][1]
        rows = self.width >> (len(self.bits) + 1)
        near, near_other, far, far_other, token = call(
            "last_stage", 1, functools.partial(last_stage_kernel, bit, self.cuts),
            "s" + "v" * (2 * self.parts), (shaped(rows, 2 * self.width),) * 4, "vvvv",
            [pltpu.VMEM((4 * rows, self.columns), F32)],
        )(self.place, *self.kept, *self.got, deps=deps)
        self.sums = (
            near, swap(far, "seq", 1 << bit), swap(near_other, "seq", 1),
            swap(far_other, "seq", (1 << bit) | 1),
        )
        return token

    def finish(self, deps=()):
        rows = self.sums[0].shape[0]
        return call(
            "assemble", 1, assemble_kernel, "svvvv",
            (shaped(rows, 3 * self.width), shaped(rows, self.width)), "vv",
        )(self.place, *self.sums, deps=deps)


def shards(frames_in, modulation, spatial_qkv, spatial_out, temporal_qkv, temporal_out, cotangent):
    n = lax.axis_size("seq")
    videos, frames, patches, width = frames_in.shape
    all_frames = frames * n
    tokens = frames * patches
    own_patches = patches // n
    rows = frames * own_patches
    padded = -(-rows // 8) * 8
    time_block = 6 * all_frames if own_patches % 6 == 0 else 3 * all_frames
    core = jnp.stack([lax.axis_index("dp"), lax.axis_index("seq")]).astype(jnp.int32)

    joint_padded = -(-videos * rows // 8) * 8
    to_pieces = np.zeros((n * padded, tokens), np.float32)
    to_joint = np.zeros((videos, n * joint_padded, tokens), np.float32)
    by_patch = np.zeros((tokens, n * padded), np.float32)
    joint_by_patch = np.zeros((videos, tokens, n * joint_padded), np.float32)
    for device in range(n):
        for f in range(frames):
            for p in range(own_patches):
                inside = f * own_patches + p
                before = f * patches + device * own_patches + p
                after = p * all_frames + device * frames + f
                to_pieces[device * padded + inside, before] = 1
                by_patch[after, device * padded + inside] = 1
                for v in range(videos):
                    place = device * joint_padded + v * rows + inside
                    to_joint[v, place, before] = 1
                    joint_by_patch[v, after, place] = 1
    from_joint = jnp.asarray(np.concatenate(list(to_joint), 1).T, BF16)
    to_pieces, from_pieces = jnp.asarray(to_pieces, BF16), jnp.asarray(to_pieces.T, BF16)
    to_joint = [jnp.asarray(m, BF16) for m in to_joint]
    by_patch, from_patch = jnp.asarray(by_patch, BF16), jnp.asarray(by_patch.T, BF16)
    joint_from_patch = [jnp.asarray(m.T, BF16) for m in joint_by_patch]
    joint_by_patch = [jnp.asarray(m, BF16) for m in joint_by_patch]

    def exchange(pieces):
        return lax.all_to_all(pieces, "seq", split_axis=0, concat_axis=0, tiled=True)

    piece = shaped(n, padded, width)
    joint_piece = shaped(n, joint_padded, width)
    row = shaped(tokens, width)
    two, three, four = [shaped(tokens, count * width) for count in (2, 3, 4)]
    all_rows = shaped(videos, tokens, width)
    weights_shape = (frames * (HEADS // 2), patches, 2 * patches)

    def vmem(*shape, dtype=BF16):
        return pltpu.VMEM(shape, dtype)

    def sems(count):
        return pltpu.SemaphoreType.DMA((count,))

    weight_refs = [vmem(width, 3 * width), vmem(width, width)]
    x = frames_in.reshape(videos, tokens, width)
    cot = cotangent.reshape(videos, tokens, width)

    def exchange_units(units):
        return swap(units, "seq", 1)

    cot_sent, token = call("split", 3, functools.partial(split_kernel, n), "vv", (piece,), "v")(
        cot, to_pieces
    )
    cot_pieces = exchange(cot_sent)
    deps = [token]
    saved, arrived = [], []
    for v in range(videos):
        sent, *keep, token = call(
            "space_forward", 14, functools.partial(space_forward_kernel, n, patches, v),
            "aavaavv",
            (joint_piece if v else piece, three, two, shaped(*weights_shape)),
            "vaaa",
            [
                vmem(tokens, width), vmem(tokens, width), vmem(tokens, 2 * width),
                vmem(tokens, 3 * width), vmem(*weights_shape), *weight_refs,
                vmem(HEADS // 2, patches, 2 * patches, dtype=F32), sems(9),
            ],
        )(
            x, cot, modulation, spatial_qkv, spatial_out, to_joint[0] if v else to_pieces,
            to_joint[1], deps=deps,
        )
        deps = [token, cot_pieces]
        arrived.append(exchange(sent))
        saved.append((*keep, exchange_units(keep[1])))

    returned, time_units, out_sent = [], [], core
    for v in range(videos):
        d_middle, out_sent, left, sent, right, token = call(
            "time", 25, functools.partial(time_kernel, n, time_block, all_frames, v),
            "svvvaavvvv" + ("v" if v else "a"),
            (piece, joint_piece, two, two, four),
            "vvaaa",
            [
                vmem(tokens, width, dtype=F32), vmem(tokens, width), vmem(tokens, width),
                vmem(tokens, 2 * width), vmem(tokens, 3 * width), vmem(tokens, width),
                vmem(tokens, 4 * width), *weight_refs,
                *[vmem(HEADS // 2, time_block, 2 * time_block, dtype=d) for d in (F32, F32, BF16, BF16)],
                sems(9),
            ],
        )(
            core, arrived[v], arrived[v] if v else cot_pieces, modulation, temporal_qkv,
            temporal_out, joint_by_patch[0] if v else by_patch,
            joint_by_patch[1] if v else by_patch, from_patch, joint_from_patch[v], out_sent,
            deps=deps,
        )
        deps = [token]
        returned.append(exchange(d_middle))
        time_units.append((left, exchange_units(left), right, exchange_units(sent)))

    grad_scale = (videos * lax.axis_size("dp") * all_frames * patches) ** (-0.5)

    def weights(units, late, deps=()):
        reduction = Reduction(core, width, late)
        steps, shapes = reduction.next_steps()
        operands = [one for kind in zip(*units) for one in kind]
        *halves, token = call(
            "weights", 10,
            functools.partial(weight_kernel, videos, reduction.cuts, steps, grad_scale),
            "s" + "a" * (4 * videos), shapes, "a" * len(shapes),
            [vmem(*half.shape) for half in shapes] + [
                vmem(2 * videos * tokens, 2 * width), vmem(2 * videos * tokens, 2 * width),
                vmem(width, reduction.columns, dtype=F32), sems(8 * videos + len(shapes)),
            ],
        )(core, *operands, deps=deps)
        reduction.send(halves)
        return reduction, token

    def grad_of(video, units, d_middle, deps=()):
        return call(
            "grad_input", 8, functools.partial(grad_input_kernel, video), "avvva", (row,), "v",
            [vmem(tokens, 3 * width), vmem(width, 3 * width), sems(6)],
        )(units[2], d_middle, x, modulation, spatial_qkv, deps=deps)

    d_middles, space_units = [], []
    for v in range(videos):
        packed, left, weights_saved, left_got = saved[v]
        d_middle, sent, right, token = call(
            "space_backward", 15, functools.partial(space_backward_kernel, patches, v),
            "svvavav",
            (row, two, four),
            "vaa",
            [
                vmem(tokens, width), vmem(tokens, 4 * width), vmem(tokens, 3 * width),
                vmem(width, width),
                *[vmem(HEADS // 2, patches, 2 * patches, dtype=d) for d in (F32, BF16)], sems(4),
            ],
        )(
            core, returned[v], modulation, spatial_out, from_pieces, packed, weights_saved,
            deps=[*deps, left_got],
        )
        if v == 0:
            time_sum, began = weights(time_units, False, deps=[token])
            deps = [began]
            out_back = exchange(out_sent)
        d_middles.append(d_middle)
        space_units.append((left, left_got, right, exchange_units(sent)))
    token = time_sum.stage(deps=[token])
    space_sum, token = weights(space_units, True, deps=[token])
    token = time_sum.stage(deps=[token])
    grad_input = []
    for v in range(videos):
        one_grad, token = grad_of(
            v, space_units[v], d_middles[v], deps=[token, out_back] if v else [token]
        )
        grad_input.append(one_grad)
    token = time_sum.last_stage(deps=[token])
    token = space_sum.stage(deps=[token])
    block_out, grad_input, token = call(
        "join", 4, join_kernel, "vv" + "v" * videos, (all_rows, all_rows), "vv"
    )(out_back, from_joint, *grad_input, deps=[token])
    token = space_sum.stage(deps=[token])
    token = space_sum.last_stage(deps=[token])
    *grad_time, token = time_sum.finish(deps=[token])
    *grad_space, _ = space_sum.finish(deps=[token])
    return (
        block_out.reshape(frames_in.shape), grad_input.reshape(frames_in.shape),
        *grad_space, *grad_time,
    )


def solution(mesh):
    return jax.shard_map(
        shards,
        mesh=mesh,
        in_specs=(
            P("dp", "seq", None, None),
            P("dp", None, None),
            P(),
            P(),
            P(),
            P(),
            P("dp", "seq", None, None),
        ),
        out_specs=(
            P("dp", "seq", None, None),
            P("dp", "seq", None, None),
            P(("dp", "seq"), None),
            P(("dp", "seq"), None),
            P(("dp", "seq"), None),
            P(("dp", "seq"), None),
        ),
        check_vma=False,
    )
```

```python
import functools

import jax
import jax.numpy as jnp
import numpy as np
from jax import lax
from jax.experimental import pallas as pl
from jax.experimental.pallas import tpu as pltpu
from jax.sharding import PartitionSpec as P

HEADS = 16
NORM_EPSILON = 1e-06
MASKED = -1e30
TOKEN = jax.ShapeDtypeStruct((8, 128), jnp.float32)
LOG2_E = 1.4426950408889634
MIB = 1024 * 1024
F32 = jnp.float32
BF16 = jnp.bfloat16

NN = (((1,), (0,)), ((), ()))
NT = (((1,), (1,)), ((), ()))
TN = (((0,), (0,)), ((), ()))


def dot(left, right, dims=NN):
    return lax.dot_general(left, right, dims, preferred_element_type=F32)


ROOM = {
    "split": 56, "space_forward": 56, "time": 56, "weights": 56, "space_backward": 56,
    "grad_input": 56, "stage": 24, "last_stage": 16, "assemble": 16, "join": 56,
}
SPACES = {"v": pltpu.VMEM, "s": pltpu.SMEM, "a": pl.ANY}


def call(name, us, body, ins, out_shape, outs, scratch=()):
    def run(*operands, deps=()):
        before = len(operands) + len(deps) + len(out_shape)

        def with_token(*refs):
            refs[before][...] = jnp.zeros(TOKEN.shape, TOKEN.dtype)
            body(*refs[:before], *refs[before + 1 :])

        return pl.pallas_call(
            with_token,
            out_shape=(*out_shape, TOKEN),
            in_specs=[pl.BlockSpec(memory_space=SPACES[s]) for s in ins + "a" * len(deps)],
            out_specs=tuple(pl.BlockSpec(memory_space=SPACES[s]) for s in outs + "v"),
            scratch_shapes=list(scratch),
            compiler_params=pltpu.CompilerParams(vmem_limit_bytes=ROOM[name] * MIB),
            cost_estimate=pl.CostEstimate(
                flops=int(us * 1e9), transcendentals=0, bytes_accessed=int(us * 1e6)
            ),
            name=name,
        )(*operands, *deps)

    return run


def shaped(*shape, dtype=BF16):
    return jax.ShapeDtypeStruct(shape, dtype)


def norm_stats(values):
    mean = jnp.mean(values, -1, keepdims=True)
    centred = values - mean
    inverse = lax.rsqrt(jnp.mean(centred * centred, -1, keepdims=True) + NORM_EPSILON)
    return centred * inverse, inverse


def norm_backward(d_modded, normed, inverse, scale):
    e = d_modded * (1.0 + scale)
    return inverse * (
        e
        - jnp.mean(e, -1, keepdims=True)
        - normed * jnp.mean(e * normed, -1, keepdims=True)
    )


def pair_windows(width):
    size = 2 * width // HEADS
    found = []
    for pair in range(HEADS // 2):
        start = pair * size // 128 * 128
        offset = pair * size - start
        found.append((start, 128 * pl.cdiv(offset + size, 128), offset))
    return found


def pair_masks(rows, span, offset, size):
    lane = lax.broadcasted_iota(jnp.int32, (rows, span), 1)
    first = (lane >= offset) & (lane < offset + size)
    both = (lane >= offset) & (lane < offset + 2 * size)
    return first, both


def two_heads(values, first, both):
    zero = jnp.zeros_like(values)
    return jnp.concatenate(
        [jnp.where(first, values, zero), jnp.where(both & ~first, values, zero)], 0
    )


def per_query(by_key, other, first):
    out = dot(by_key, other, TN)
    rows = out.shape[0] // 2
    return jnp.where(first, out[:rows], out[rows:])


def softmax_by_key(scores, factor, keep):
    if keep is not None:
        scores = jnp.where(keep, scores, MASKED)
    raised = jnp.exp2((scores - jnp.max(scores, 0, keepdims=True)) * (factor * LOG2_E))
    return raised * (1.0 / jnp.sum(raised, 0, keepdims=True))


def put(ref, rows, start, both, value):
    at = (pl.ds(rows, both.shape[0]), pl.ds(start, both.shape[1]))
    ref[at] = jnp.where(both, value.astype(BF16), ref[at])


def frame_rows(pieces):
    n, rows, width = pieces.shape
    return pieces.astype(F32).reshape(n * rows, width).astype(BF16)


def piece_rows(values, n):
    return values.reshape(n, values.shape[0] // n, values.shape[1]).astype(BF16)


def same_video(rows, frames):
    left = lax.broadcasted_iota(jnp.int32, (rows, 2 * rows), 0) // frames
    column = lax.broadcasted_iota(jnp.int32, (rows, 2 * rows), 1)
    right = jnp.where(column >= rows, column - rows, column) // frames
    return left == right


class Copies:
    def __init__(self, sems):
        self.sems, self.used = sems, 0

    def start(self, source, target):
        copy = pltpu.make_async_copy(source, target, self.sems.at[self.used])
        self.used += 1
        copy.start()
        return copy


def qkv_loads(copies, wqkv_ref, wqkv, width):
    parts = [pl.ds(part * width, width) for part in range(3)]
    return [copies.start(wqkv_ref.at[:, at], wqkv.at[:, at]) for at in parts]


def project_qkv(modded, wqkv, loads, packed, width):
    for part, load in enumerate(loads):
        load.wait()
        at = pl.ds(part * width, width)
        packed[:, at] = dot(modded, wqkv[:, at]).astype(BF16)


def split_kernel(n, x_ref, scatter_ref, out_ref):
    out_ref[...] = piece_rows(dot(scatter_ref[...], x_ref[0]), n)


def join_kernel(pieces_ref, gather_ref, *refs):
    *grads, out_ref, grad_out = refs
    for video in range(grad_out.shape[0]):
        grad_out[video] = grads[video][...]
    rows = dot(gather_ref[...], frame_rows(pieces_ref[...])).astype(BF16)
    out_ref[...] = rows.reshape(out_ref.shape)


def space_forward_kernel(
    n, block, video, x_ref, cot_ref, mod_ref, wqkv_ref, wout_ref, scatter_ref, scatter_cot_ref, *refs
):
    sent_ref, packed_out, left_out, weights_out = refs[-13:-9]
    x, cot, left, packed, weights, wqkv, wout, scores_ref, sems = refs[-9:]
    width = x.shape[1]
    size = width // HEADS
    factor = size ** (-0.5)
    copies = Copies(sems)
    load_x = copies.start(x_ref.at[video], x)
    load_qkv = qkv_loads(copies, wqkv_ref, wqkv, width)
    load_out = copies.start(wout_ref, wout)
    if video:
        load_cot = copies.start(cot_ref.at[video], cot)
    load_x.wait()
    normed, _ = norm_stats(x[...].astype(F32))
    left[:, 0:width] = (
        normed * (1.0 + mod_ref[video, 1:2, :]) + mod_ref[video, 0:1, :]
    ).astype(BF16)
    project_qkv(left[:, 0:width], wqkv, load_qkv, packed, width)
    stores = [copies.start(packed, packed_out)]
    pairs = pair_windows(width)

    def one_block(g, carry):
        rows = pl.multiple_of(g * block, 16)
        at = pl.ds(rows, block)
        for pair, (start, span, offset) in enumerate(pairs):
            first, both = pair_masks(block, span, offset, size)
            query = two_heads(packed[at, pl.ds(start, span)], first, both)
            scores_ref[pair] = dot(packed[at, pl.ds(width + start, span)], query, NT)
        for pair in range(len(pairs)):
            probs = softmax_by_key(scores_ref[pair], factor, None)
            weights[g * len(pairs) + pair] = probs.astype(BF16)
        for pair, (start, span, offset) in enumerate(pairs):
            first, both = pair_masks(block, span, offset, size)
            value = packed[at, pl.ds(2 * width + start, span)]
            attended = per_query(weights[g * len(pairs) + pair], value, first)
            put(left, rows, width + start, both, attended)
        return carry

    lax.fori_loop(0, x.shape[0] // block, one_block, 0)
    stores.append(copies.start(left, left_out))
    stores.append(copies.start(weights, weights_out))
    load_out.wait()
    projected = dot(left[:, width:], wout[...])
    middle = (x[...].astype(F32) + mod_ref[video, 2:3, :] * projected).astype(BF16)
    pieces = dot(scatter_ref[...], middle)
    if video:
        load_cot.wait()
        pieces += dot(scatter_cot_ref[...], cot[...])
    sent_ref[...] = piece_rows(pieces, n)
    for store in stores:
        store.wait()


def unit_stores(copies, core, width, right, outs):
    sent_out, right_out = outs
    other = pl.multiple_of((1 - core) * (2 * width), 128)
    return [
        copies.start(right.at[:, pl.ds(other, 2 * width)], sent_out), copies.start(right, right_out)
    ]


def time_kernel(
    n, block, frames, video, core_ref, middle_ref, cot_ref, mod_ref, wqkv_ref, wout_ref,
    gather_ref, gather_cot_ref, scatter_ref, scatter_out_ref, others_ref, *refs
):
    (d_middle_ref, block_out_ref, left_out, *unit_outs), scratch = refs[-19:-14], refs[-14:]
    normed, x, up, left, packed, d_out, right, wqkv, wout = scratch[:9]
    scores_ref, d_probs_ref, weights_ref, d_scores_ref, sems = scratch[9:]
    width = x.shape[1]
    size = width // HEADS
    factor = size ** (-0.5)
    copies = Copies(sems)
    load_qkv = qkv_loads(copies, wqkv_ref, wqkv, width)
    load_out = copies.start(wout_ref, wout)
    x[...] = dot(gather_ref[...], frame_rows(middle_ref[...])).astype(BF16)
    up[...] = dot(gather_cot_ref[...], frame_rows(cot_ref[...])).astype(BF16)
    normed_now, inverse = norm_stats(x[...].astype(F32))
    normed[...] = normed_now
    left[:, 0:width] = (
        normed_now * (1.0 + mod_ref[video, 4:5, :]) + mod_ref[video, 3:4, :]
    ).astype(BF16)
    right[:, 3 * width :] = (mod_ref[video, 5:6, :] * up[...].astype(F32)).astype(BF16)
    project_qkv(left[:, 0:width], wqkv, load_qkv, packed, width)
    load_out.wait()
    d_out[...] = dot(right[:, 3 * width :], wout[...], NT).astype(BF16)
    keep = same_video(block, frames)

    pairs = pair_windows(width)

    def one_block(g, carry):
        rows = pl.multiple_of(g * block, 16)
        at = pl.ds(rows, block)

        def parts(pair):
            start, span, offset = pairs[pair]
            first, both = pair_masks(block, span, offset, size)
            query = two_heads(packed[at, pl.ds(start, span)], first, both)
            key = packed[at, pl.ds(width + start, span)]
            value = packed[at, pl.ds(2 * width + start, span)]
            d_rows = two_heads(d_out[at, pl.ds(start, span)], first, both)
            return start, first, both, query, key, value, d_rows

        for pair in range(len(pairs)):
            _, _, _, query, key, value, d_rows = parts(pair)
            scores_ref[pair] = dot(key, query, NT)
            d_probs_ref[pair] = dot(value, d_rows, NT)
        for pair in range(len(pairs)):
            probs = softmax_by_key(scores_ref[pair], factor, keep)
            d_probs = d_probs_ref[pair]
            total = jnp.sum(probs * d_probs, 0, keepdims=True)
            weights_ref[pair] = probs.astype(BF16)
            d_scores_ref[pair] = (probs * (d_probs - total) * factor).astype(BF16)
        for pair in range(len(pairs)):
            start, first, both, query, key, value, d_rows = parts(pair)
            weights, d_scores = weights_ref[pair], d_scores_ref[pair]
            put(left, rows, width + start, both, per_query(weights, value, first))
            put(right, rows, start, both, per_query(d_scores, key, first))
            put(right, rows, width + start, both, dot(d_scores, query))
            put(right, rows, 2 * width + start, both, dot(weights, d_rows))
        return carry

    lax.fori_loop(0, x.shape[0] // block, one_block, 0)
    stores = [copies.start(left, left_out)]
    stores += unit_stores(copies, core_ref[1] & 1, width, right, unit_outs)
    d_modded = dot(right[:, 0 : 3 * width], wqkv[...], NT)
    d_middle = up[...].astype(F32) + norm_backward(
        d_modded, normed[...], inverse, mod_ref[video, 4:5, :]
    )
    d_middle_ref[...] = piece_rows(dot(scatter_ref[...], d_middle.astype(BF16)), n)
    projected = dot(left[:, width:], wout[...])
    out = (x[...].astype(F32) + mod_ref[video, 5:6, :] * projected).astype(BF16)
    pieces = dot(scatter_out_ref[...], out)
    if video:
        pieces += others_ref[...].astype(F32).reshape(pieces.shape)
    block_out_ref[...] = piece_rows(pieces, n)
    for store in stores:
        store.wait()


def space_backward_kernel(
    block, video, core_ref, up_ref, mod_ref, wout_ref, gather_ref, packed_ref, weights_ref, *refs
):
    d_middle_ref, *unit_outs = refs[-10:-7]
    d_out, right, packed, wout, d_probs_ref, d_scores_ref, sems = refs[-7:]
    width = wout.shape[0]
    size = width // HEADS
    factor = size ** (-0.5)
    copies = Copies(sems)
    load_out = copies.start(wout_ref, wout)
    load_packed = copies.start(packed_ref, packed)
    up = dot(gather_ref[...], frame_rows(up_ref[...]))
    d_middle_ref[...] = up.astype(BF16)
    right[:, 3 * width :] = (mod_ref[video, 2:3, :] * up).astype(BF16)
    load_out.wait()
    d_out[...] = dot(right[:, 3 * width :], wout[...], NT).astype(BF16)
    load_packed.wait()
    pairs = pair_windows(width)

    def one_block(g, carry):
        rows = pl.multiple_of(g * block, 16)
        at = pl.ds(rows, block)
        for pair, (start, span, offset) in enumerate(pairs):
            first, both = pair_masks(block, span, offset, size)
            d_rows = two_heads(d_out[at, pl.ds(start, span)], first, both)
            d_probs_ref[pair] = dot(packed[at, pl.ds(2 * width + start, span)], d_rows, NT)
        for pair in range(len(pairs)):
            probs = weights_ref[g * len(pairs) + pair].astype(F32)
            d_probs = d_probs_ref[pair]
            total = jnp.sum(probs * d_probs, 0, keepdims=True) / jnp.sum(probs, 0, keepdims=True)
            d_scores_ref[pair] = (probs * (d_probs - total) * factor).astype(BF16)
        for pair, (start, span, offset) in enumerate(pairs):
            first, both = pair_masks(block, span, offset, size)
            query = two_heads(packed[at, pl.ds(start, span)], first, both)
            key = packed[at, pl.ds(width + start, span)]
            d_rows = two_heads(d_out[at, pl.ds(start, span)], first, both)
            weights, d_scores = weights_ref[g * len(pairs) + pair], d_scores_ref[pair]
            put(right, rows, start, both, per_query(d_scores, key, first))
            put(right, rows, width + start, both, dot(d_scores, query))
            put(right, rows, 2 * width + start, both, dot(weights, d_rows))
        return carry

    lax.fori_loop(0, d_out.shape[0] // block, one_block, 0)
    for store in unit_stores(copies, core_ref[1] & 1, width, right, unit_outs):
        store.wait()


def grad_input_kernel(video, right_ref, d_middle_ref, x_ref, mod_ref, wqkv_ref, *refs):
    out_ref, d_packed, wqkv, sems = refs[-4:]
    width = out_ref.shape[1]
    copies = Copies(sems)
    parts = [pl.ds(part * width, width) for part in range(3)]
    loads = [
        (copies.start(right_ref.at[:, at], d_packed.at[:, at]),
         copies.start(wqkv_ref.at[:, at], wqkv.at[:, at]))
        for at in parts
    ]
    normed, inverse = norm_stats(x_ref[video].astype(F32))
    d_modded = 0.0
    for at, load in zip(parts, loads):
        for one in load:
            one.wait()
        d_modded += dot(d_packed[:, at], wqkv[:, at], NT)
    d_tokens = norm_backward(d_modded, normed, inverse, mod_ref[video, 1:2, :])
    out_ref[...] = (d_middle_ref[...].astype(F32) + d_tokens).astype(BF16)


def bit_of(place_ref, axis, bit):
    return (place_ref[0 if axis == "dp" else 1] >> bit) & 1


def emit_halves(rows, inner, mine, kept_ref, sent_ref):
    columns = kept_ref.shape[2]
    for outer in range(kept_ref.shape[0]):
        low = rows[2 * outer * inner : (2 * outer + 1) * inner, :columns]
        high = rows[(2 * outer + 1) * inner : (2 * outer + 2) * inner, :columns]
        kept_ref[outer] = jnp.where(mine == 0, low, high).astype(BF16)
        sent_ref[outer] = jnp.where(mine == 0, high, low).astype(BF16)


def weight_kernel(videos, cuts, steps, grad_scale, place_ref, *refs):
    left_own, left_got, right_own, right_got = [
        refs[at * videos : (at + 1) * videos] for at in range(4)
    ]
    count = 2 * len(cuts)
    outs, scratch = refs[-4 - 2 * count : -4 - count], refs[-4 - count : -4]
    left_rows, right_rows, total, sems = refs[-4:]
    width = left_rows.shape[1] // 2
    tokens = left_own[0].shape[0]
    copies = Copies(sems)
    core = place_ref[1] & 1
    own = pl.multiple_of(core * (2 * width), 128)

    def load(unit):
        now = []
        at = pl.ds(unit * width, width)
        mine = pl.ds(pl.multiple_of(own + unit * width, 128), width)
        for video in range(videos):
            for place, (left, right, columns) in enumerate(
                (
                    (left_own[video], right_own[video], mine),
                    (left_got[video], right_got[video], at),
                )
            ):
                rows = pl.ds((2 * video + place) * tokens, tokens)
                now.append(copies.start(left.at[:, at], left_rows.at[rows, at]))
                now.append(copies.start(right.at[:, columns], right_rows.at[rows, at]))
        return now

    waits = [load(0), load(1)]
    done, stores = 0, []
    for part, ((low, high), (axis, bit, inner)) in enumerate(zip(cuts, steps)):
        for unit in range(2):
            start, stop = max(low, unit * width), min(high, (unit + 1) * width)
            if start >= stop:
                continue
            while done <= unit:
                for wait in waits[done]:
                    wait.wait()
                done += 1
            column = pl.multiple_of(core * width, 128) if unit else 0
            left = left_rows[:, pl.ds(column, width)]
            total[:, start - low : stop - low] = (
                dot(left, right_rows[:, start:stop], TN) * grad_scale
            )
        pair = slice(2 * part, 2 * part + 2)
        emit_halves(total, inner, bit_of(place_ref, axis, bit), *scratch[pair])
        stores += [copies.start(a, b) for a, b in zip(scratch[pair], outs[pair])]
    for store in stores:
        store.wait()


def add_got(total, kept, got):
    each, columns = kept.shape[1:]
    for outer in range(kept.shape[0]):
        total[outer * each : (outer + 1) * each, :columns] = kept[outer].astype(F32) + got[
            outer
        ].astype(F32)


def stage_kernel(steps, place_ref, *refs):
    count = len(steps)
    total, outs = refs[-1], refs[-1 - 2 * count : -1]
    for part, (axis, bit, inner) in enumerate(steps):
        add_got(total, refs[part], refs[count + part])
        emit_halves(
            total, inner, bit_of(place_ref, axis, bit), outs[2 * part], outs[2 * part + 1]
        )


def last_stage_kernel(bit, cuts, place_ref, *refs):
    count = len(cuts)
    outs, total = refs[-5:-1], refs[-1]
    rows = outs[0].shape[0]
    mine, core = bit_of(place_ref, "seq", bit) == 0, (place_ref[1] & 1) == 0
    for part, (start, stop) in enumerate(cuts):
        add_got(total, refs[part], refs[count + part])
        low, high = total[: 2 * rows, : stop - start], total[2 * rows : 4 * rows, : stop - start]
        near, far = jnp.where(mine, low, high), jnp.where(mine, high, low)
        for place, half in enumerate((near, far)):
            first, second = half[:rows], half[rows:]
            same, other = jnp.where(core, first, second), jnp.where(core, second, first)
            outs[2 * place][:, start:stop] = same.astype(BF16)
            outs[2 * place + 1][:, start:stop] = other.astype(BF16)


def assemble_kernel(place_ref, *refs):
    near, far, near_other, far_other = [ref[...].astype(F32) for ref in refs[:4]]
    qkv_ref, out_ref = refs[-2:]
    width = out_ref.shape[1]
    core = (place_ref[1] & 1) == 0
    mine, others = near + far, near_other + far_other
    low = jnp.where(core, mine, others).astype(BF16)
    high = jnp.where(core, others, mine).astype(BF16)
    qkv_ref[:, : 2 * width] = low
    qkv_ref[:, 2 * width :] = high[:, :width]
    out_ref[...] = high[:, width:]


def swap(x, axis, mask):
    size = lax.axis_size(axis)
    return lax.ppermute(x, axis, [(i, i ^ mask) for i in range(size)])


class Reduction:
    def __init__(self, place, width, late):
        dp_bits = [("dp", bit) for bit in range(lax.axis_size("dp").bit_length() - 1)]
        seq_bits = [("seq", bit) for bit in range(1, lax.axis_size("seq").bit_length() - 1)]
        if late:
            self.orders = (
                dp_bits + seq_bits,
                dp_bits[-1:] + seq_bits[:1] + dp_bits[:-1] + seq_bits[1:],
                seq_bits[:1] + dp_bits + seq_bits[1:],
            )
        else:
            self.orders = (dp_bits + seq_bits, dp_bits[::-1] + seq_bits)
        tiles = 2 * width // 128
        ends = [0, (tiles - tiles // 6) * 64, (tiles - tiles // 6) * 128] if late else [0, width]
        self.cuts = tuple(zip(ends, ends[1:] + [2 * width]))
        self.parts = len(self.orders)
        self.place, self.width = place, width
        self.columns = max(stop - start for start, stop in self.cuts)
        self.bits = dp_bits[::-1] + seq_bits[::-1]
        self.step = 0

    def next_steps(self):
        least = self.width >> len(self.bits)
        steps, shapes = [], []
        for order, (start, stop) in zip(self.orders, self.cuts):
            left = [bit for bit in self.bits if bit not in order[: self.step]]
            above = left.index(order[self.step])
            inner = least << (len(left) - above - 1)
            steps.append((*order[self.step], inner))
            shapes += 2 * [shaped(1 << above, inner, stop - start)]
        return tuple(steps), tuple(shapes)

    def send(self, halves):
        self.kept = halves[0::2]
        self.got = [
            swap(half, order[self.step][0], 1 << order[self.step][1])
            for half, order in zip(halves[1::2], self.orders)
        ]
        self.step += 1

    def stage(self, deps=()):
        steps, shapes = self.next_steps()
        *halves, token = call(
            "stage", 2, functools.partial(stage_kernel, steps), "s" + "v" * (2 * self.parts),
            shapes, "v" * len(shapes),
            [pltpu.VMEM((self.width >> self.step, self.columns), F32)],
        )(self.place, *self.kept, *self.got, deps=deps)
        self.send(halves)
        return token

    def last_stage(self, deps=()):
        while self.step < len(self.bits) - 1:
            self.stage()
        bit = self.orders[0][-1][1]
        rows = self.width >> (len(self.bits) + 1)
        near, near_other, far, far_other, token = call(
            "last_stage", 1, functools.partial(last_stage_kernel, bit, self.cuts),
            "s" + "v" * (2 * self.parts), (shaped(rows, 2 * self.width),) * 4, "vvvv",
            [pltpu.VMEM((4 * rows, self.columns), F32)],
        )(self.place, *self.kept, *self.got, deps=deps)
        self.sums = (
            near, swap(far, "seq", 1 << bit), swap(near_other, "seq", 1),
            swap(far_other, "seq", (1 << bit) | 1),
        )
        return token

    def finish(self, deps=()):
        rows = self.sums[0].shape[0]
        return call(
            "assemble", 1, assemble_kernel, "svvvv",
            (shaped(rows, 3 * self.width), shaped(rows, self.width)), "vv",
        )(self.place, *self.sums, deps=deps)


def shards(frames_in, modulation, spatial_qkv, spatial_out, temporal_qkv, temporal_out, cotangent):
    n = lax.axis_size("seq")
    videos, frames, patches, width = frames_in.shape
    all_frames = frames * n
    tokens = frames * patches
    own_patches = patches // n
    rows = frames * own_patches
    padded = -(-rows // 8) * 8
    time_block = 6 * all_frames if own_patches % 6 == 0 else 3 * all_frames
    core = jnp.stack([lax.axis_index("dp"), lax.axis_index("seq")]).astype(jnp.int32)

    joint_padded = -(-videos * rows // 8) * 8
    to_pieces = np.zeros((n * padded, tokens), np.float32)
    to_joint = np.zeros((videos, n * joint_padded, tokens), np.float32)
    by_patch = np.zeros((tokens, n * padded), np.float32)
    joint_by_patch = np.zeros((videos, tokens, n * joint_padded), np.float32)
    for device in range(n):
        for f in range(frames):
            for p in range(own_patches):
                inside = f * own_patches + p
                before = f * patches + device * own_patches + p
                after = p * all_frames + device * frames + f
                to_pieces[device * padded + inside, before] = 1
                by_patch[after, device * padded + inside] = 1
                for v in range(videos):
                    place = device * joint_padded + v * rows + inside
                    to_joint[v, place, before] = 1
                    joint_by_patch[v, after, place] = 1
    from_joint = jnp.asarray(np.concatenate(list(to_joint), 1).T, BF16)
    to_pieces, from_pieces = jnp.asarray(to_pieces, BF16), jnp.asarray(to_pieces.T, BF16)
    to_joint = [jnp.asarray(m, BF16) for m in to_joint]
    by_patch, from_patch = jnp.asarray(by_patch, BF16), jnp.asarray(by_patch.T, BF16)
    joint_from_patch = [jnp.asarray(m.T, BF16) for m in joint_by_patch]
    joint_by_patch = [jnp.asarray(m, BF16) for m in joint_by_patch]

    def exchange(pieces):
        return lax.all_to_all(pieces, "seq", split_axis=0, concat_axis=0, tiled=True)

    piece = shaped(n, padded, width)
    joint_piece = shaped(n, joint_padded, width)
    row = shaped(tokens, width)
    two, three, four = [shaped(tokens, count * width) for count in (2, 3, 4)]
    all_rows = shaped(videos, tokens, width)
    weights_shape = (frames * (HEADS // 2), patches, 2 * patches)

    def vmem(*shape, dtype=BF16):
        return pltpu.VMEM(shape, dtype)

    def sems(count):
        return pltpu.SemaphoreType.DMA((count,))

    weight_refs = [vmem(width, 3 * width), vmem(width, width)]
    x = frames_in.reshape(videos, tokens, width)
    cot = cotangent.reshape(videos, tokens, width)

    def exchange_units(units):
        return swap(units, "seq", 1)

    cot_sent, token = call("split", 3, functools.partial(split_kernel, n), "vv", (piece,), "v")(
        cot, to_pieces
    )
    cot_pieces = exchange(cot_sent)
    deps = [token]
    saved, arrived = [], []
    for v in range(videos):
        sent, *keep, token = call(
            "space_forward", 14, functools.partial(space_forward_kernel, n, patches, v),
            "aavaavv",
            (joint_piece if v else piece, three, two, shaped(*weights_shape)),
            "vaaa",
            [
                vmem(tokens, width), vmem(tokens, width), vmem(tokens, 2 * width),
                vmem(tokens, 3 * width), vmem(*weights_shape), *weight_refs,
                vmem(HEADS // 2, patches, 2 * patches, dtype=F32), sems(9),
            ],
        )(
            x, cot, modulation, spatial_qkv, spatial_out, to_joint[0] if v else to_pieces,
            to_joint[1], deps=deps,
        )
        deps = [token, cot_pieces]
        arrived.append(exchange(sent))
        saved.append((*keep, exchange_units(keep[1])))

    returned, time_units, out_sent = [], [], core
    for v in range(videos):
        d_middle, out_sent, left, sent, right, token = call(
            "time", 25, functools.partial(time_kernel, n, time_block, all_frames, v),
            "svvvaavvvv" + ("v" if v else "a"),
            (piece, joint_piece, two, two, four),
            "vvaaa",
            [
                vmem(tokens, width, dtype=F32), vmem(tokens, width), vmem(tokens, width),
                vmem(tokens, 2 * width), vmem(tokens, 3 * width), vmem(tokens, width),
                vmem(tokens, 4 * width), *weight_refs,
                *[vmem(HEADS // 2, time_block, 2 * time_block, dtype=d) for d in (F32, F32, BF16, BF16)],
                sems(9),
            ],
        )(
            core, arrived[v], arrived[v] if v else cot_pieces, modulation, temporal_qkv,
            temporal_out, joint_by_patch[0] if v else by_patch,
            joint_by_patch[1] if v else by_patch, from_patch, joint_from_patch[v], out_sent,
            deps=deps,
        )
        deps = [token]
        returned.append(exchange(d_middle))
        time_units.append((left, exchange_units(left), right, exchange_units(sent)))

    grad_scale = (videos * lax.axis_size("dp") * all_frames * patches) ** (-0.5)

    def weights(units, late, deps=()):
        reduction = Reduction(core, width, late)
        steps, shapes = reduction.next_steps()
        operands = [one for kind in zip(*units) for one in kind]
        *halves, token = call(
            "weights", 10,
            functools.partial(weight_kernel, videos, reduction.cuts, steps, grad_scale),
            "s" + "a" * (4 * videos), shapes, "a" * len(shapes),
            [vmem(*half.shape) for half in shapes] + [
                vmem(2 * videos * tokens, 2 * width), vmem(2 * videos * tokens, 2 * width),
                vmem(width, reduction.columns, dtype=F32), sems(8 * videos + len(shapes)),
            ],
        )(core, *operands, deps=deps)
        reduction.send(halves)
        return reduction, token

    def grad_of(video, units, d_middle, deps=()):
        return call(
            "grad_input", 8, functools.partial(grad_input_kernel, video), "avvva", (row,), "v",
            [vmem(tokens, 3 * width), vmem(width, 3 * width), sems(6)],
        )(units[2], d_middle, x, modulation, spatial_qkv, deps=deps)

    d_middles, space_units = [], []
    for v in range(videos):
        packed, left, weights_saved, left_got = saved[v]
        d_middle, sent, right, token = call(
            "space_backward", 15, functools.partial(space_backward_kernel, patches, v),
            "svvavav",
            (row, two, four),
            "vaa",
            [
                vmem(tokens, width), vmem(tokens, 4 * width), vmem(tokens, 3 * width),
                vmem(width, width),
                *[vmem(HEADS // 2, patches, 2 * patches, dtype=d) for d in (F32, BF16)], sems(4),
            ],
        )(
            core, returned[v], modulation, spatial_out, from_pieces, packed, weights_saved,
            deps=[*deps, left_got],
        )
        if v == 0:
            time_sum, began = weights(time_units, False, deps=[token])
            deps = [began]
            out_back = exchange(out_sent)
        d_middles.append(d_middle)
        space_units.append((left, left_got, right, exchange_units(sent)))
    grad_input = []

    def next_grad(deps):
        v = len(grad_input)
        one_grad, token = grad_of(v, space_units[v], d_middles[v], deps=deps)
        grad_input.append(one_grad)
        return token

    token = next_grad([token])
    token = time_sum.stage(deps=[token])
    space_sum, token = weights(space_units, True, deps=[token])
    token = time_sum.stage(deps=[token])
    while len(grad_input) < videos:
        token = next_grad([token, out_back])
    token = time_sum.last_stage(deps=[token])
    token = space_sum.stage(deps=[token])
    block_out, grad_input, token = call(
        "join", 4, join_kernel, "vv" + "v" * videos, (all_rows, all_rows), "vv"
    )(out_back, from_joint, *grad_input, deps=[token])
    *grad_time, token = time_sum.finish(deps=[token])
    token = space_sum.stage(deps=[token])
    space_sum.last_stage(deps=[token])
    *grad_space, _ = space_sum.finish()
    return (
        block_out.reshape(frames_in.shape), grad_input.reshape(frames_in.shape),
        *grad_space, *grad_time,
    )


def solution(mesh):
    return jax.shard_map(
        shards,
        mesh=mesh,
        in_specs=(
            P("dp", "seq", None, None),
            P("dp", None, None),
            P(),
            P(),
            P(),
            P(),
            P("dp", "seq", None, None),
        ),
        out_specs=(
            P("dp", "seq", None, None),
            P("dp", "seq", None, None),
            P(("dp", "seq"), None),
            P(("dp", "seq"), None),
            P(("dp", "seq"), None),
            P(("dp", "seq"), None),
        ),
        check_vma=False,
    )
```

```python
import functools

import jax
import jax.numpy as jnp
import numpy as np
from jax import lax
from jax.experimental import pallas as pl
from jax.experimental.pallas import tpu as pltpu
from jax.sharding import PartitionSpec as P

HEADS = 16
NORM_EPSILON = 1e-06
MASKED = -1e30
TOKEN = jax.ShapeDtypeStruct((8, 128), jnp.float32)
LOG2_E = 1.4426950408889634
MIB = 1024 * 1024
F32 = jnp.float32
BF16 = jnp.bfloat16

NN = (((1,), (0,)), ((), ()))
NT = (((1,), (1,)), ((), ()))
TN = (((0,), (0,)), ((), ()))


def dot(left, right, dims=NN):
    return lax.dot_general(left, right, dims, preferred_element_type=F32)


ROOM = {
    "split": 56, "space_forward": 56, "time": 56, "weights": 56, "space_backward": 56,
    "grad_input": 56, "stage": 24, "last_stage": 16, "core_stage": 16, "assemble": 16, "join": 56,
}
SPACES = {"v": pltpu.VMEM, "s": pltpu.SMEM, "a": pl.ANY}


def call(name, us, body, ins, out_shape, outs, scratch=()):
    def run(*operands, deps=()):
        before = len(operands) + len(deps) + len(out_shape)

        def with_token(*refs):
            refs[before][...] = jnp.zeros(TOKEN.shape, TOKEN.dtype)
            body(*refs[:before], *refs[before + 1 :])

        return pl.pallas_call(
            with_token,
            out_shape=(*out_shape, TOKEN),
            in_specs=[pl.BlockSpec(memory_space=SPACES[s]) for s in ins + "a" * len(deps)],
            out_specs=tuple(pl.BlockSpec(memory_space=SPACES[s]) for s in outs + "v"),
            scratch_shapes=list(scratch),
            compiler_params=pltpu.CompilerParams(vmem_limit_bytes=ROOM[name] * MIB),
            cost_estimate=pl.CostEstimate(
                flops=int(us * 1e9), transcendentals=0, bytes_accessed=int(us * 1e6)
            ),
            name=name,
        )(*operands, *deps)

    return run


def shaped(*shape, dtype=BF16):
    return jax.ShapeDtypeStruct(shape, dtype)


def norm_stats(values):
    mean = jnp.mean(values, -1, keepdims=True)
    centred = values - mean
    inverse = lax.rsqrt(jnp.mean(centred * centred, -1, keepdims=True) + NORM_EPSILON)
    return centred * inverse, inverse


def norm_backward(d_modded, normed, inverse, scale):
    e = d_modded * (1.0 + scale)
    return inverse * (
        e
        - jnp.mean(e, -1, keepdims=True)
        - normed * jnp.mean(e * normed, -1, keepdims=True)
    )


def pair_windows(width):
    size = 2 * width // HEADS
    found = []
    for pair in range(HEADS // 2):
        start = pair * size // 128 * 128
        offset = pair * size - start
        found.append((start, 128 * pl.cdiv(offset + size, 128), offset))
    return found


def pair_masks(rows, span, offset, size):
    lane = lax.broadcasted_iota(jnp.int32, (rows, span), 1)
    first = (lane >= offset) & (lane < offset + size)
    both = (lane >= offset) & (lane < offset + 2 * size)
    return first, both


def two_heads(values, first, both):
    zero = jnp.zeros_like(values)
    return jnp.concatenate(
        [jnp.where(first, values, zero), jnp.where(both & ~first, values, zero)], 0
    )


def per_query(by_key, other, first):
    out = dot(by_key, other, TN)
    rows = out.shape[0] // 2
    return jnp.where(first, out[:rows], out[rows:])


def softmax_by_key(scores, factor, keep):
    if keep is not None:
        scores = jnp.where(keep, scores, MASKED)
    raised = jnp.exp2((scores - jnp.max(scores, 0, keepdims=True)) * (factor * LOG2_E))
    return raised * (1.0 / jnp.sum(raised, 0, keepdims=True))


def put(ref, rows, start, both, value):
    at = (pl.ds(rows, both.shape[0]), pl.ds(start, both.shape[1]))
    ref[at] = jnp.where(both, value.astype(BF16), ref[at])


def frame_rows(pieces):
    n, rows, width = pieces.shape
    return pieces.astype(F32).reshape(n * rows, width).astype(BF16)


def piece_rows(values, n):
    return values.reshape(n, values.shape[0] // n, values.shape[1]).astype(BF16)


def same_video(rows, frames):
    left = lax.broadcasted_iota(jnp.int32, (rows, 2 * rows), 0) // frames
    column = lax.broadcasted_iota(jnp.int32, (rows, 2 * rows), 1)
    right = jnp.where(column >= rows, column - rows, column) // frames
    return left == right


class Copies:
    def __init__(self, sems):
        self.sems, self.used = sems, 0

    def start(self, source, target):
        copy = pltpu.make_async_copy(source, target, self.sems.at[self.used])
        self.used += 1
        copy.start()
        return copy


def qkv_loads(copies, wqkv_ref, wqkv, width):
    parts = [pl.ds(part * width, width) for part in range(3)]
    return [copies.start(wqkv_ref.at[:, at], wqkv.at[:, at]) for at in parts]


def project_qkv(modded, wqkv, loads, packed, width):
    for part, load in enumerate(loads):
        load.wait()
        at = pl.ds(part * width, width)
        packed[:, at] = dot(modded, wqkv[:, at]).astype(BF16)


def split_kernel(n, x_ref, scatter_ref, out_ref):
    out_ref[...] = piece_rows(dot(scatter_ref[...], x_ref[0]), n)


def join_kernel(pieces_ref, gather_ref, *refs):
    *grads, out_ref, grad_out = refs
    for video in range(grad_out.shape[0]):
        grad_out[video] = grads[video][...]
    rows = dot(gather_ref[...], frame_rows(pieces_ref[...])).astype(BF16)
    out_ref[...] = rows.reshape(out_ref.shape)


def space_forward_kernel(
    n, block, video, x_ref, cot_ref, mod_ref, wqkv_ref, wout_ref, scatter_ref, scatter_cot_ref, *refs
):
    sent_ref, packed_out, left_out, weights_out = refs[-13:-9]
    x, cot, left, packed, weights, wqkv, wout, scores_ref, sems = refs[-9:]
    width = x.shape[1]
    size = width // HEADS
    factor = size ** (-0.5)
    copies = Copies(sems)
    load_x = copies.start(x_ref.at[video], x)
    load_qkv = qkv_loads(copies, wqkv_ref, wqkv, width)
    load_out = copies.start(wout_ref, wout)
    if video:
        load_cot = copies.start(cot_ref.at[video], cot)
    load_x.wait()
    normed, _ = norm_stats(x[...].astype(F32))
    left[:, 0:width] = (
        normed * (1.0 + mod_ref[video, 1:2, :]) + mod_ref[video, 0:1, :]
    ).astype(BF16)
    project_qkv(left[:, 0:width], wqkv, load_qkv, packed, width)
    stores = [copies.start(packed, packed_out)]
    pairs = pair_windows(width)

    def one_block(g, carry):
        rows = pl.multiple_of(g * block, 16)
        at = pl.ds(rows, block)
        for pair, (start, span, offset) in enumerate(pairs):
            first, both = pair_masks(block, span, offset, size)
            query = two_heads(packed[at, pl.ds(start, span)], first, both)
            scores_ref[pair] = dot(packed[at, pl.ds(width + start, span)], query, NT)
        for pair in range(len(pairs)):
            probs = softmax_by_key(scores_ref[pair], factor, None)
            weights[g * len(pairs) + pair] = probs.astype(BF16)
        for pair, (start, span, offset) in enumerate(pairs):
            first, both = pair_masks(block, span, offset, size)
            value = packed[at, pl.ds(2 * width + start, span)]
            attended = per_query(weights[g * len(pairs) + pair], value, first)
            put(left, rows, width + start, both, attended)
        return carry

    lax.fori_loop(0, x.shape[0] // block, one_block, 0)
    stores.append(copies.start(left, left_out))
    stores.append(copies.start(weights, weights_out))
    load_out.wait()
    projected = dot(left[:, width:], wout[...])
    middle = (x[...].astype(F32) + mod_ref[video, 2:3, :] * projected).astype(BF16)
    pieces = dot(scatter_ref[...], middle)
    if video:
        load_cot.wait()
        pieces += dot(scatter_cot_ref[...], cot[...])
    sent_ref[...] = piece_rows(pieces, n)
    for store in stores:
        store.wait()


def unit_stores(copies, core, width, right, outs):
    sent_out, right_out = outs
    other = pl.multiple_of((1 - core) * (2 * width), 128)
    return [
        copies.start(right.at[:, pl.ds(other, 2 * width)], sent_out), copies.start(right, right_out)
    ]


def time_kernel(
    n, block, frames, video, core_ref, middle_ref, cot_ref, mod_ref, wqkv_ref, wout_ref,
    gather_ref, gather_cot_ref, scatter_ref, scatter_out_ref, others_ref, *refs
):
    (d_middle_ref, block_out_ref, left_out, *unit_outs), scratch = refs[-19:-14], refs[-14:]
    normed, x, up, left, packed, d_out, right, wqkv, wout = scratch[:9]
    scores_ref, d_probs_ref, weights_ref, d_scores_ref, sems = scratch[9:]
    width = x.shape[1]
    size = width // HEADS
    factor = size ** (-0.5)
    copies = Copies(sems)
    load_qkv = qkv_loads(copies, wqkv_ref, wqkv, width)
    load_out = copies.start(wout_ref, wout)
    x[...] = dot(gather_ref[...], frame_rows(middle_ref[...])).astype(BF16)
    up[...] = dot(gather_cot_ref[...], frame_rows(cot_ref[...])).astype(BF16)
    normed_now, inverse = norm_stats(x[...].astype(F32))
    normed[...] = normed_now
    left[:, 0:width] = (
        normed_now * (1.0 + mod_ref[video, 4:5, :]) + mod_ref[video, 3:4, :]
    ).astype(BF16)
    right[:, 3 * width :] = (mod_ref[video, 5:6, :] * up[...].astype(F32)).astype(BF16)
    project_qkv(left[:, 0:width], wqkv, load_qkv, packed, width)
    load_out.wait()
    d_out[...] = dot(right[:, 3 * width :], wout[...], NT).astype(BF16)
    keep = same_video(block, frames)

    pairs = pair_windows(width)

    def one_block(g, carry):
        rows = pl.multiple_of(g * block, 16)
        at = pl.ds(rows, block)

        def parts(pair):
            start, span, offset = pairs[pair]
            first, both = pair_masks(block, span, offset, size)
            query = two_heads(packed[at, pl.ds(start, span)], first, both)
            key = packed[at, pl.ds(width + start, span)]
            value = packed[at, pl.ds(2 * width + start, span)]
            d_rows = two_heads(d_out[at, pl.ds(start, span)], first, both)
            return start, first, both, query, key, value, d_rows

        for pair in range(len(pairs)):
            _, _, _, query, key, value, d_rows = parts(pair)
            scores_ref[pair] = dot(key, query, NT)
            d_probs_ref[pair] = dot(value, d_rows, NT)
        for pair in range(len(pairs)):
            probs = softmax_by_key(scores_ref[pair], factor, keep)
            d_probs = d_probs_ref[pair]
            total = jnp.sum(probs * d_probs, 0, keepdims=True)
            weights_ref[pair] = probs.astype(BF16)
            d_scores_ref[pair] = (probs * (d_probs - total) * factor).astype(BF16)
        for pair in range(len(pairs)):
            start, first, both, query, key, value, d_rows = parts(pair)
            weights, d_scores = weights_ref[pair], d_scores_ref[pair]
            put(left, rows, width + start, both, per_query(weights, value, first))
            put(right, rows, start, both, per_query(d_scores, key, first))
            put(right, rows, width + start, both, dot(d_scores, query))
            put(right, rows, 2 * width + start, both, dot(weights, d_rows))
        return carry

    lax.fori_loop(0, x.shape[0] // block, one_block, 0)
    stores = [copies.start(left, left_out)]
    stores += unit_stores(copies, core_ref[1] & 1, width, right, unit_outs)
    d_modded = dot(right[:, 0 : 3 * width], wqkv[...], NT)
    d_middle = up[...].astype(F32) + norm_backward(
        d_modded, normed[...], inverse, mod_ref[video, 4:5, :]
    )
    d_middle_ref[...] = piece_rows(dot(scatter_ref[...], d_middle.astype(BF16)), n)
    projected = dot(left[:, width:], wout[...])
    out = (x[...].astype(F32) + mod_ref[video, 5:6, :] * projected).astype(BF16)
    pieces = dot(scatter_out_ref[...], out)
    if video:
        pieces += others_ref[...].astype(F32).reshape(pieces.shape)
    block_out_ref[...] = piece_rows(pieces, n)
    for store in stores:
        store.wait()


def space_backward_kernel(
    block, video, core_ref, up_ref, mod_ref, wout_ref, gather_ref, packed_ref, weights_ref, *refs
):
    d_middle_ref, *unit_outs = refs[-10:-7]
    d_out, right, packed, wout, d_probs_ref, d_scores_ref, sems = refs[-7:]
    width = wout.shape[0]
    size = width // HEADS
    factor = size ** (-0.5)
    copies = Copies(sems)
    load_out = copies.start(wout_ref, wout)
    load_packed = copies.start(packed_ref, packed)
    up = dot(gather_ref[...], frame_rows(up_ref[...]))
    d_middle_ref[...] = up.astype(BF16)
    right[:, 3 * width :] = (mod_ref[video, 2:3, :] * up).astype(BF16)
    load_out.wait()
    d_out[...] = dot(right[:, 3 * width :], wout[...], NT).astype(BF16)
    load_packed.wait()
    pairs = pair_windows(width)

    def one_block(g, carry):
        rows = pl.multiple_of(g * block, 16)
        at = pl.ds(rows, block)
        for pair, (start, span, offset) in enumerate(pairs):
            first, both = pair_masks(block, span, offset, size)
            d_rows = two_heads(d_out[at, pl.ds(start, span)], first, both)
            d_probs_ref[pair] = dot(packed[at, pl.ds(2 * width + start, span)], d_rows, NT)
        for pair in range(len(pairs)):
            probs = weights_ref[g * len(pairs) + pair].astype(F32)
            d_probs = d_probs_ref[pair]
            total = jnp.sum(probs * d_probs, 0, keepdims=True) / jnp.sum(probs, 0, keepdims=True)
            d_scores_ref[pair] = (probs * (d_probs - total) * factor).astype(BF16)
        for pair, (start, span, offset) in enumerate(pairs):
            first, both = pair_masks(block, span, offset, size)
            query = two_heads(packed[at, pl.ds(start, span)], first, both)
            key = packed[at, pl.ds(width + start, span)]
            d_rows = two_heads(d_out[at, pl.ds(start, span)], first, both)
            weights, d_scores = weights_ref[g * len(pairs) + pair], d_scores_ref[pair]
            put(right, rows, start, both, per_query(d_scores, key, first))
            put(right, rows, width + start, both, dot(d_scores, query))
            put(right, rows, 2 * width + start, both, dot(weights, d_rows))
        return carry

    lax.fori_loop(0, d_out.shape[0] // block, one_block, 0)
    for store in unit_stores(copies, core_ref[1] & 1, width, right, unit_outs):
        store.wait()


def grad_input_kernel(video, right_ref, d_middle_ref, x_ref, mod_ref, wqkv_ref, *refs):
    out_ref, d_packed, wqkv, sems = refs[-4:]
    width = out_ref.shape[1]
    copies = Copies(sems)
    parts = [pl.ds(part * width, width) for part in range(3)]
    loads = [
        (copies.start(right_ref.at[:, at], d_packed.at[:, at]),
         copies.start(wqkv_ref.at[:, at], wqkv.at[:, at]))
        for at in parts
    ]
    normed, inverse = norm_stats(x_ref[video].astype(F32))
    d_modded = 0.0
    for at, load in zip(parts, loads):
        for one in load:
            one.wait()
        d_modded += dot(d_packed[:, at], wqkv[:, at], NT)
    d_tokens = norm_backward(d_modded, normed, inverse, mod_ref[video, 1:2, :])
    out_ref[...] = (d_middle_ref[...].astype(F32) + d_tokens).astype(BF16)


def bit_of(place_ref, axis, bit):
    return (place_ref[0 if axis == "dp" else 1] >> bit) & 1


def emit_halves(rows, inner, mine, kept_ref, sent_ref):
    columns = kept_ref.shape[2]
    for outer in range(kept_ref.shape[0]):
        low = rows[2 * outer * inner : (2 * outer + 1) * inner, :columns]
        high = rows[(2 * outer + 1) * inner : (2 * outer + 2) * inner, :columns]
        kept_ref[outer] = jnp.where(mine == 0, low, high).astype(BF16)
        sent_ref[outer] = jnp.where(mine == 0, high, low).astype(BF16)


def weight_kernel(videos, cuts, steps, grad_scale, place_ref, *refs):
    left_own, left_got, right_own, right_got = [
        refs[at * videos : (at + 1) * videos] for at in range(4)
    ]
    count = 2 * len(cuts)
    outs, scratch = refs[-4 - 2 * count : -4 - count], refs[-4 - count : -4]
    left_rows, right_rows, total, sems = refs[-4:]
    width = left_rows.shape[1] // 2
    tokens = left_own[0].shape[0]
    copies = Copies(sems)
    core = place_ref[1] & 1
    own = pl.multiple_of(core * (2 * width), 128)

    def load(unit):
        now = []
        at = pl.ds(unit * width, width)
        mine = pl.ds(pl.multiple_of(own + unit * width, 128), width)
        for video in range(videos):
            for place, (left, right, columns) in enumerate(
                (
                    (left_own[video], right_own[video], mine),
                    (left_got[video], right_got[video], at),
                )
            ):
                rows = pl.ds((2 * video + place) * tokens, tokens)
                now.append(copies.start(left.at[:, at], left_rows.at[rows, at]))
                now.append(copies.start(right.at[:, columns], right_rows.at[rows, at]))
        return now

    waits = [load(0), load(1)]
    done, stores = 0, []
    for part, ((low, high), (axis, bit, inner)) in enumerate(zip(cuts, steps)):
        for unit in range(2):
            start, stop = max(low, unit * width), min(high, (unit + 1) * width)
            if start >= stop:
                continue
            while done <= unit:
                for wait in waits[done]:
                    wait.wait()
                done += 1
            column = pl.multiple_of(core * width, 128) if unit else 0
            left = left_rows[:, pl.ds(column, width)]
            total[:, start - low : stop - low] = (
                dot(left, right_rows[:, start:stop], TN) * grad_scale
            )
        pair = slice(2 * part, 2 * part + 2)
        emit_halves(total, inner, bit_of(place_ref, axis, bit), *scratch[pair])
        stores += [copies.start(a, b) for a, b in zip(scratch[pair], outs[pair])]
    for store in stores:
        store.wait()


def add_got(total, kept, got):
    each, columns = kept.shape[1:]
    for outer in range(kept.shape[0]):
        total[outer * each : (outer + 1) * each, :columns] = kept[outer].astype(F32) + got[
            outer
        ].astype(F32)


def stage_kernel(steps, place_ref, *refs):
    count = len(steps)
    total, outs = refs[-1], refs[-1 - 2 * count : -1]
    for part, (axis, bit, inner) in enumerate(steps):
        add_got(total, refs[part], refs[count + part])
        emit_halves(
            total, inner, bit_of(place_ref, axis, bit), outs[2 * part], outs[2 * part + 1]
        )


def last_stage_kernel(bit, cuts, place_ref, *refs):
    count = len(cuts)
    outs, total = refs[-5:-1], refs[-1]
    rows = outs[0].shape[0]
    mine, core = bit_of(place_ref, "seq", bit) == 0, (place_ref[1] & 1) == 0
    for part, (start, stop) in enumerate(cuts):
        add_got(total, refs[part], refs[count + part])
        low, high = total[: 2 * rows, : stop - start], total[2 * rows : 4 * rows, : stop - start]
        near, far = jnp.where(mine, low, high), jnp.where(mine, high, low)
        for place, half in enumerate((near, far)):
            first, second = half[:rows], half[rows:]
            same, other = jnp.where(core, first, second), jnp.where(core, second, first)
            outs[2 * place][:, start:stop] = same.astype(BF16)
            outs[2 * place + 1][:, start:stop] = other.astype(BF16)


def far_stage_kernel(bit, cuts, place_ref, *refs):
    count = len(cuts)
    (near_out, far_out), total = refs[-3:-1], refs[-1]
    rows = near_out.shape[0]
    mine = bit_of(place_ref, "seq", bit) == 0
    for part, (start, stop) in enumerate(cuts):
        add_got(total, refs[part], refs[count + part])
        low, high = total[:rows, : stop - start], total[rows : 2 * rows, : stop - start]
        near_out[:, start:stop] = jnp.where(mine, low, high).astype(BF16)
        far_out[:, start:stop] = jnp.where(mine, high, low).astype(BF16)


def core_stage_kernel(place_ref, near_ref, got_ref, *refs):
    kept_out, sent_out = refs[-2:]
    rows = kept_out.shape[0]
    core = (place_ref[1] & 1) == 0
    total = near_ref[...].astype(F32) + got_ref[...].astype(F32)
    low, high = total[:rows], total[rows:]
    kept_out[...] = jnp.where(core, low, high).astype(BF16)
    sent_out[...] = jnp.where(core, high, low).astype(BF16)


def assemble_two_kernel(place_ref, kept_ref, got_ref, *refs):
    qkv_ref, out_ref = refs[-2:]
    width = out_ref.shape[1]
    core = (place_ref[1] & 1) == 0
    kept, got = kept_ref[...].astype(F32), got_ref[...].astype(F32)
    low = jnp.where(core, kept, got).astype(BF16)
    high = jnp.where(core, got, kept).astype(BF16)
    qkv_ref[:, : 2 * width] = low
    qkv_ref[:, 2 * width :] = high[:, :width]
    out_ref[...] = high[:, width:]


def assemble_kernel(place_ref, *refs):
    near, far, near_other, far_other = [ref[...].astype(F32) for ref in refs[:4]]
    qkv_ref, out_ref = refs[-2:]
    width = out_ref.shape[1]
    core = (place_ref[1] & 1) == 0
    mine, others = near + far, near_other + far_other
    low = jnp.where(core, mine, others).astype(BF16)
    high = jnp.where(core, others, mine).astype(BF16)
    qkv_ref[:, : 2 * width] = low
    qkv_ref[:, 2 * width :] = high[:, :width]
    out_ref[...] = high[:, width:]


def swap(x, axis, mask):
    size = lax.axis_size(axis)
    return lax.ppermute(x, axis, [(i, i ^ mask) for i in range(size)])


class Reduction:
    def __init__(self, place, width, late):
        dp_bits = [("dp", bit) for bit in range(lax.axis_size("dp").bit_length() - 1)]
        seq_bits = [("seq", bit) for bit in range(1, lax.axis_size("seq").bit_length() - 1)]
        if late:
            self.orders = (
                dp_bits + seq_bits,
                dp_bits[-1:] + seq_bits[:1] + dp_bits[:-1] + seq_bits[1:],
                seq_bits[:1] + dp_bits + seq_bits[1:],
            )
        else:
            self.orders = (dp_bits + seq_bits, dp_bits[::-1] + seq_bits)
        tiles = 2 * width // 128
        ends = [0, (tiles - tiles // 6) * 64, (tiles - tiles // 6) * 128] if late else [0, width]
        self.cuts = tuple(zip(ends, ends[1:] + [2 * width]))
        self.parts = len(self.orders)
        self.place, self.width = place, width
        self.columns = max(stop - start for start, stop in self.cuts)
        self.bits = dp_bits[::-1] + seq_bits[::-1]
        self.step = 0

    def next_steps(self):
        least = self.width >> len(self.bits)
        steps, shapes = [], []
        for order, (start, stop) in zip(self.orders, self.cuts):
            left = [bit for bit in self.bits if bit not in order[: self.step]]
            above = left.index(order[self.step])
            inner = least << (len(left) - above - 1)
            steps.append((*order[self.step], inner))
            shapes += 2 * [shaped(1 << above, inner, stop - start)]
        return tuple(steps), tuple(shapes)

    def send(self, halves):
        self.kept = halves[0::2]
        self.got = [
            swap(half, order[self.step][0], 1 << order[self.step][1])
            for half, order in zip(halves[1::2], self.orders)
        ]
        self.step += 1

    def stage(self, deps=()):
        steps, shapes = self.next_steps()
        *halves, token = call(
            "stage", 2, functools.partial(stage_kernel, steps), "s" + "v" * (2 * self.parts),
            shapes, "v" * len(shapes),
            [pltpu.VMEM((self.width >> self.step, self.columns), F32)],
        )(self.place, *self.kept, *self.got, deps=deps)
        self.send(halves)
        return token

    def last_stage(self, deps=()):
        while self.step < len(self.bits) - 1:
            self.stage()
        bit = self.orders[0][-1][1]
        rows = self.width >> (len(self.bits) + 1)
        near, near_other, far, far_other, token = call(
            "last_stage", 1, functools.partial(last_stage_kernel, bit, self.cuts),
            "s" + "v" * (2 * self.parts), (shaped(rows, 2 * self.width),) * 4, "vvvv",
            [pltpu.VMEM((4 * rows, self.columns), F32)],
        )(self.place, *self.kept, *self.got, deps=deps)
        self.sums = (
            near, swap(far, "seq", 1 << bit), swap(near_other, "seq", 1),
            swap(far_other, "seq", (1 << bit) | 1),
        )
        return token

    def far_stage(self, deps=()):
        while self.step < len(self.bits) - 1:
            self.stage()
        bit = self.orders[0][-1][1]
        rows = self.width >> len(self.bits)
        near, far, token = call(
            "last_stage", 1, functools.partial(far_stage_kernel, bit, self.cuts),
            "s" + "v" * (2 * self.parts), (shaped(rows, 2 * self.width),) * 2, "vv",
            [pltpu.VMEM((2 * rows, self.columns), F32)],
        )(self.place, *self.kept, *self.got, deps=deps)
        self.sums = (near, swap(far, "seq", 1 << bit))
        return token

    def core_stage(self, deps=()):
        rows = self.width >> (len(self.bits) + 1)
        kept, sent, token = call(
            "core_stage", 1, core_stage_kernel, "svv", (shaped(rows, 2 * self.width),) * 2, "vv"
        )(self.place, *self.sums, deps=deps)
        self.sums = (kept, swap(sent, "seq", 1))
        return token

    def finish(self, deps=()):
        rows = self.sums[0].shape[0]
        return call(
            "assemble", 1, assemble_kernel if len(self.sums) == 4 else assemble_two_kernel,
            "s" + "v" * len(self.sums),
            (shaped(rows, 3 * self.width), shaped(rows, self.width)), "vv",
        )(self.place, *self.sums, deps=deps)


def shards(frames_in, modulation, spatial_qkv, spatial_out, temporal_qkv, temporal_out, cotangent):
    n = lax.axis_size("seq")
    videos, frames, patches, width = frames_in.shape
    all_frames = frames * n
    tokens = frames * patches
    own_patches = patches // n
    rows = frames * own_patches
    padded = -(-rows // 8) * 8
    time_block = 6 * all_frames if own_patches % 6 == 0 else 3 * all_frames
    core = jnp.stack([lax.axis_index("dp"), lax.axis_index("seq")]).astype(jnp.int32)

    joint_padded = -(-videos * rows // 8) * 8
    to_pieces = np.zeros((n * padded, tokens), np.float32)
    to_joint = np.zeros((videos, n * joint_padded, tokens), np.float32)
    by_patch = np.zeros((tokens, n * padded), np.float32)
    joint_by_patch = np.zeros((videos, tokens, n * joint_padded), np.float32)
    for device in range(n):
        for f in range(frames):
            for p in range(own_patches):
                inside = f * own_patches + p
                before = f * patches + device * own_patches + p
                after = p * all_frames + device * frames + f
                to_pieces[device * padded + inside, before] = 1
                by_patch[after, device * padded + inside] = 1
                for v in range(videos):
                    place = device * joint_padded + v * rows + inside
                    to_joint[v, place, before] = 1
                    joint_by_patch[v, after, place] = 1
    from_joint = jnp.asarray(np.concatenate(list(to_joint), 1).T, BF16)
    to_pieces, from_pieces = jnp.asarray(to_pieces, BF16), jnp.asarray(to_pieces.T, BF16)
    to_joint = [jnp.asarray(m, BF16) for m in to_joint]
    by_patch, from_patch = jnp.asarray(by_patch, BF16), jnp.asarray(by_patch.T, BF16)
    joint_from_patch = [jnp.asarray(m.T, BF16) for m in joint_by_patch]
    joint_by_patch = [jnp.asarray(m, BF16) for m in joint_by_patch]

    def exchange(pieces):
        return lax.all_to_all(pieces, "seq", split_axis=0, concat_axis=0, tiled=True)

    piece = shaped(n, padded, width)
    joint_piece = shaped(n, joint_padded, width)
    row = shaped(tokens, width)
    two, three, four = [shaped(tokens, count * width) for count in (2, 3, 4)]
    all_rows = shaped(videos, tokens, width)
    weights_shape = (frames * (HEADS // 2), patches, 2 * patches)

    def vmem(*shape, dtype=BF16):
        return pltpu.VMEM(shape, dtype)

    def sems(count):
        return pltpu.SemaphoreType.DMA((count,))

    weight_refs = [vmem(width, 3 * width), vmem(width, width)]
    x = frames_in.reshape(videos, tokens, width)
    cot = cotangent.reshape(videos, tokens, width)

    def exchange_units(units):
        return swap(units, "seq", 1)

    cot_sent, token = call("split", 3, functools.partial(split_kernel, n), "vv", (piece,), "v")(
        cot, to_pieces
    )
    cot_pieces = exchange(cot_sent)
    deps = [token]
    saved, arrived = [], []
    for v in range(videos):
        sent, *keep, token = call(
            "space_forward", 14, functools.partial(space_forward_kernel, n, patches, v),
            "aavaavv",
            (joint_piece if v else piece, three, two, shaped(*weights_shape)),
            "vaaa",
            [
                vmem(tokens, width), vmem(tokens, width), vmem(tokens, 2 * width),
                vmem(tokens, 3 * width), vmem(*weights_shape), *weight_refs,
                vmem(HEADS // 2, patches, 2 * patches, dtype=F32), sems(9),
            ],
        )(
            x, cot, modulation, spatial_qkv, spatial_out, to_joint[0] if v else to_pieces,
            to_joint[1], deps=deps,
        )
        deps = [token, cot_pieces]
        arrived.append(exchange(sent))
        saved.append((*keep, exchange_units(keep[1])))

    returned, time_units, out_sent = [], [], core
    for v in range(videos):
        d_middle, out_sent, left, sent, right, token = call(
            "time", 25, functools.partial(time_kernel, n, time_block, all_frames, v),
            "svvvaavvvv" + ("v" if v else "a"),
            (piece, joint_piece, two, two, four),
            "vvaaa",
            [
                vmem(tokens, width, dtype=F32), vmem(tokens, width), vmem(tokens, width),
                vmem(tokens, 2 * width), vmem(tokens, 3 * width), vmem(tokens, width),
                vmem(tokens, 4 * width), *weight_refs,
                *[vmem(HEADS // 2, time_block, 2 * time_block, dtype=d) for d in (F32, F32, BF16, BF16)],
                sems(9),
            ],
        )(
            core, arrived[v], arrived[v] if v else cot_pieces, modulation, temporal_qkv,
            temporal_out, joint_by_patch[0] if v else by_patch,
            joint_by_patch[1] if v else by_patch, from_patch, joint_from_patch[v], out_sent,
            deps=deps,
        )
        deps = [token]
        returned.append(exchange(d_middle))
        time_units.append((left, exchange_units(left), right, exchange_units(sent)))

    grad_scale = (videos * lax.axis_size("dp") * all_frames * patches) ** (-0.5)

    def weights(units, late, deps=()):
        reduction = Reduction(core, width, late)
        steps, shapes = reduction.next_steps()
        operands = [one for kind in zip(*units) for one in kind]
        *halves, token = call(
            "weights", 10,
            functools.partial(weight_kernel, videos, reduction.cuts, steps, grad_scale),
            "s" + "a" * (4 * videos), shapes, "a" * len(shapes),
            [vmem(*half.shape) for half in shapes] + [
                vmem(2 * videos * tokens, 2 * width), vmem(2 * videos * tokens, 2 * width),
                vmem(width, reduction.columns, dtype=F32), sems(8 * videos + len(shapes)),
            ],
        )(core, *operands, deps=deps)
        reduction.send(halves)
        return reduction, token

    def grad_of(video, units, d_middle, deps=()):
        return call(
            "grad_input", 8, functools.partial(grad_input_kernel, video), "avvva", (row,), "v",
            [vmem(tokens, 3 * width), vmem(width, 3 * width), sems(6)],
        )(units[2], d_middle, x, modulation, spatial_qkv, deps=deps)

    d_middles, space_units = [], []
    for v in range(videos):
        packed, left, weights_saved, left_got = saved[v]
        d_middle, sent, right, token = call(
            "space_backward", 15, functools.partial(space_backward_kernel, patches, v),
            "svvavav",
            (row, two, four),
            "vaa",
            [
                vmem(tokens, width), vmem(tokens, 4 * width), vmem(tokens, 3 * width),
                vmem(width, width),
                *[vmem(HEADS // 2, patches, 2 * patches, dtype=d) for d in (F32, BF16)], sems(4),
            ],
        )(
            core, returned[v], modulation, spatial_out, from_pieces, packed, weights_saved,
            deps=[*deps, left_got],
        )
        if v == 0:
            time_sum, began = weights(time_units, False, deps=[token])
            deps = [began]
            out_back = exchange(out_sent)
        d_middles.append(d_middle)
        space_units.append((left, left_got, right, exchange_units(sent)))
    token = time_sum.stage(deps=[token])
    space_sum, token = weights(space_units, True, deps=[token])
    token = time_sum.stage(deps=[token])
    grad_input = []
    for v in range(videos):
        one_grad, token = grad_of(
            v, space_units[v], d_middles[v], deps=[token, out_back] if v else [token]
        )
        grad_input.append(one_grad)
    token = time_sum.far_stage(deps=[token])
    token = space_sum.stage(deps=[token])
    block_out, grad_input, token = call(
        "join", 4, join_kernel, "vv" + "v" * videos, (all_rows, all_rows), "vv"
    )(out_back, from_joint, *grad_input, deps=[token])
    token = space_sum.stage(deps=[token])
    token = time_sum.core_stage(deps=[token])
    token = space_sum.last_stage(deps=[token])
    *grad_time, token = time_sum.finish(deps=[token])
    *grad_space, _ = space_sum.finish(deps=[token])
    return (
        block_out.reshape(frames_in.shape), grad_input.reshape(frames_in.shape),
        *grad_space, *grad_time,
    )


def solution(mesh):
    return jax.shard_map(
        shards,
        mesh=mesh,
        in_specs=(
            P("dp", "seq", None, None),
            P("dp", None, None),
            P(),
            P(),
            P(),
            P(),
            P("dp", "seq", None, None),
        ),
        out_specs=(
            P("dp", "seq", None, None),
            P("dp", "seq", None, None),
            P(("dp", "seq"), None),
            P(("dp", "seq"), None),
            P(("dp", "seq"), None),
            P(("dp", "seq"), None),
        ),
        check_vma=False,
    )
```

```python
import functools

import jax
import jax.numpy as jnp
import numpy as np
from jax import lax
from jax.experimental import pallas as pl
from jax.experimental.pallas import tpu as pltpu
from jax.sharding import PartitionSpec as P

HEADS = 16
NORM_EPSILON = 1e-06
MASKED = -1e30
TOKEN = jax.ShapeDtypeStruct((8, 128), jnp.float32)
LOG2_E = 1.4426950408889634
MIB = 1024 * 1024
F32 = jnp.float32
BF16 = jnp.bfloat16

NN = (((1,), (0,)), ((), ()))
NT = (((1,), (1,)), ((), ()))
TN = (((0,), (0,)), ((), ()))


def dot(left, right, dims=NN):
    return lax.dot_general(left, right, dims, preferred_element_type=F32)


ROOM = {
    "split": 56, "space_forward": 56, "time": 56, "weights": 56, "space_backward": 56,
    "grad_input": 56, "early_stage": 60, "stage": 24, "last_stage": 16, "core_stage": 16, "assemble": 16, "join": 56,
}
SPACES = {"v": pltpu.VMEM, "s": pltpu.SMEM, "a": pl.ANY}


def call(name, us, body, ins, out_shape, outs, scratch=()):
    def run(*operands, deps=()):
        before = len(operands) + len(deps) + len(out_shape)

        def with_token(*refs):
            refs[before][...] = jnp.zeros(TOKEN.shape, TOKEN.dtype)
            body(*refs[:before], *refs[before + 1 :])

        return pl.pallas_call(
            with_token,
            out_shape=(*out_shape, TOKEN),
            in_specs=[pl.BlockSpec(memory_space=SPACES[s]) for s in ins + "a" * len(deps)],
            out_specs=tuple(pl.BlockSpec(memory_space=SPACES[s]) for s in outs + "v"),
            scratch_shapes=list(scratch),
            compiler_params=pltpu.CompilerParams(vmem_limit_bytes=ROOM[name] * MIB),
            cost_estimate=pl.CostEstimate(
                flops=int(us * 1e9), transcendentals=0, bytes_accessed=int(us * 1e6)
            ),
            name=name,
        )(*operands, *deps)

    return run


def shaped(*shape, dtype=BF16):
    return jax.ShapeDtypeStruct(shape, dtype)


def norm_stats(values):
    mean = jnp.mean(values, -1, keepdims=True)
    centred = values - mean
    inverse = lax.rsqrt(jnp.mean(centred * centred, -1, keepdims=True) + NORM_EPSILON)
    return centred * inverse, inverse


def norm_backward(d_modded, normed, inverse, scale):
    e = d_modded * (1.0 + scale)
    return inverse * (
        e
        - jnp.mean(e, -1, keepdims=True)
        - normed * jnp.mean(e * normed, -1, keepdims=True)
    )


def pair_windows(width):
    size = 2 * width // HEADS
    found = []
    for pair in range(HEADS // 2):
        start = pair * size // 128 * 128
        offset = pair * size - start
        found.append((start, 128 * pl.cdiv(offset + size, 128), offset))
    return found


def pair_masks(rows, span, offset, size):
    lane = lax.broadcasted_iota(jnp.int32, (rows, span), 1)
    first = (lane >= offset) & (lane < offset + size)
    both = (lane >= offset) & (lane < offset + 2 * size)
    return first, both


def two_heads(values, first, both):
    zero = jnp.zeros_like(values)
    return jnp.concatenate(
        [jnp.where(first, values, zero), jnp.where(both & ~first, values, zero)], 0
    )


def per_query(by_key, other, first):
    out = dot(by_key, other, TN)
    rows = out.shape[0] // 2
    return jnp.where(first, out[:rows], out[rows:])


def softmax_by_key(scores, factor, keep):
    if keep is not None:
        scores = jnp.where(keep, scores, MASKED)
    raised = jnp.exp2((scores - jnp.max(scores, 0, keepdims=True)) * (factor * LOG2_E))
    return raised * (1.0 / jnp.sum(raised, 0, keepdims=True))


def put(ref, rows, start, both, value):
    at = (pl.ds(rows, both.shape[0]), pl.ds(start, both.shape[1]))
    ref[at] = jnp.where(both, value.astype(BF16), ref[at])


def frame_rows(pieces):
    n, rows, width = pieces.shape
    return pieces.astype(F32).reshape(n * rows, width).astype(BF16)


def piece_rows(values, n):
    return values.reshape(n, values.shape[0] // n, values.shape[1]).astype(BF16)


def same_video(rows, frames):
    left = lax.broadcasted_iota(jnp.int32, (rows, 2 * rows), 0) // frames
    column = lax.broadcasted_iota(jnp.int32, (rows, 2 * rows), 1)
    right = jnp.where(column >= rows, column - rows, column) // frames
    return left == right


class Copies:
    def __init__(self, sems):
        self.sems, self.used = sems, 0

    def start(self, source, target):
        copy = pltpu.make_async_copy(source, target, self.sems.at[self.used])
        self.used += 1
        copy.start()
        return copy


def qkv_loads(copies, wqkv_ref, wqkv, width):
    parts = [pl.ds(part * width, width) for part in range(3)]
    return [copies.start(wqkv_ref.at[:, at], wqkv.at[:, at]) for at in parts]


def project_qkv(modded, wqkv, loads, packed, width):
    for part, load in enumerate(loads):
        load.wait()
        at = pl.ds(part * width, width)
        packed[:, at] = dot(modded, wqkv[:, at]).astype(BF16)


def split_kernel(n, x_ref, scatter_ref, out_ref):
    out_ref[...] = piece_rows(dot(scatter_ref[...], x_ref[0]), n)


def join_kernel(pieces_ref, gather_ref, *refs):
    *grads, out_ref, grad_out = refs
    for video in range(grad_out.shape[0]):
        grad_out[video] = grads[video][...]
    rows = dot(gather_ref[...], frame_rows(pieces_ref[...])).astype(BF16)
    out_ref[...] = rows.reshape(out_ref.shape)


def space_forward_kernel(
    n, block, video, x_ref, cot_ref, mod_ref, wqkv_ref, wout_ref, scatter_ref, scatter_cot_ref, *refs
):
    sent_ref, packed_out, left_out, weights_out = refs[-13:-9]
    x, cot, left, packed, weights, wqkv, wout, scores_ref, sems = refs[-9:]
    width = x.shape[1]
    size = width // HEADS
    factor = size ** (-0.5)
    copies = Copies(sems)
    load_x = copies.start(x_ref.at[video], x)
    load_qkv = qkv_loads(copies, wqkv_ref, wqkv, width)
    load_out = copies.start(wout_ref, wout)
    if video:
        load_cot = copies.start(cot_ref.at[video], cot)
    load_x.wait()
    normed, _ = norm_stats(x[...].astype(F32))
    left[:, 0:width] = (
        normed * (1.0 + mod_ref[video, 1:2, :]) + mod_ref[video, 0:1, :]
    ).astype(BF16)
    project_qkv(left[:, 0:width], wqkv, load_qkv, packed, width)
    stores = [copies.start(packed, packed_out)]
    pairs = pair_windows(width)

    def one_block(g, carry):
        rows = pl.multiple_of(g * block, 16)
        at = pl.ds(rows, block)
        for pair, (start, span, offset) in enumerate(pairs):
            first, both = pair_masks(block, span, offset, size)
            query = two_heads(packed[at, pl.ds(start, span)], first, both)
            scores_ref[pair] = dot(packed[at, pl.ds(width + start, span)], query, NT)
        for pair in range(len(pairs)):
            probs = softmax_by_key(scores_ref[pair], factor, None)
            weights[g * len(pairs) + pair] = probs.astype(BF16)
        for pair, (start, span, offset) in enumerate(pairs):
            first, both = pair_masks(block, span, offset, size)
            value = packed[at, pl.ds(2 * width + start, span)]
            attended = per_query(weights[g * len(pairs) + pair], value, first)
            put(left, rows, width + start, both, attended)
        return carry

    lax.fori_loop(0, x.shape[0] // block, one_block, 0)
    stores.append(copies.start(left, left_out))
    stores.append(copies.start(weights, weights_out))
    load_out.wait()
    projected = dot(left[:, width:], wout[...])
    middle = (x[...].astype(F32) + mod_ref[video, 2:3, :] * projected).astype(BF16)
    pieces = dot(scatter_ref[...], middle)
    if video:
        load_cot.wait()
        pieces += dot(scatter_cot_ref[...], cot[...])
    sent_ref[...] = piece_rows(pieces, n)
    for store in stores:
        store.wait()


def unit_stores(copies, core, width, right, outs):
    sent_out, right_out = outs
    other = pl.multiple_of((1 - core) * (2 * width), 128)
    return [
        copies.start(right.at[:, pl.ds(other, 2 * width)], sent_out), copies.start(right, right_out)
    ]


def time_kernel(
    n, block, frames, video, core_ref, middle_ref, cot_ref, mod_ref, wqkv_ref, wout_ref,
    gather_ref, gather_cot_ref, scatter_ref, scatter_out_ref, others_ref, *refs
):
    (d_middle_ref, block_out_ref, left_out, *unit_outs), scratch = refs[-19:-14], refs[-14:]
    normed, x, up, left, packed, d_out, right, wqkv, wout = scratch[:9]
    scores_ref, d_probs_ref, weights_ref, d_scores_ref, sems = scratch[9:]
    width = x.shape[1]
    size = width // HEADS
    factor = size ** (-0.5)
    copies = Copies(sems)
    load_qkv = qkv_loads(copies, wqkv_ref, wqkv, width)
    load_out = copies.start(wout_ref, wout)
    x[...] = dot(gather_ref[...], frame_rows(middle_ref[...])).astype(BF16)
    up[...] = dot(gather_cot_ref[...], frame_rows(cot_ref[...])).astype(BF16)
    normed_now, inverse = norm_stats(x[...].astype(F32))
    normed[...] = normed_now
    left[:, 0:width] = (
        normed_now * (1.0 + mod_ref[video, 4:5, :]) + mod_ref[video, 3:4, :]
    ).astype(BF16)
    right[:, 3 * width :] = (mod_ref[video, 5:6, :] * up[...].astype(F32)).astype(BF16)
    project_qkv(left[:, 0:width], wqkv, load_qkv, packed, width)
    load_out.wait()
    d_out[...] = dot(right[:, 3 * width :], wout[...], NT).astype(BF16)
    keep = same_video(block, frames)

    pairs = pair_windows(width)

    def one_block(g, carry):
        rows = pl.multiple_of(g * block, 16)
        at = pl.ds(rows, block)

        def parts(pair):
            start, span, offset = pairs[pair]
            first, both = pair_masks(block, span, offset, size)
            query = two_heads(packed[at, pl.ds(start, span)], first, both)
            key = packed[at, pl.ds(width + start, span)]
            value = packed[at, pl.ds(2 * width + start, span)]
            d_rows = two_heads(d_out[at, pl.ds(start, span)], first, both)
            return start, first, both, query, key, value, d_rows

        for pair in range(len(pairs)):
            _, _, _, query, key, value, d_rows = parts(pair)
            scores_ref[pair] = dot(key, query, NT)
            d_probs_ref[pair] = dot(value, d_rows, NT)
        for pair in range(len(pairs)):
            probs = softmax_by_key(scores_ref[pair], factor, keep)
            d_probs = d_probs_ref[pair]
            total = jnp.sum(probs * d_probs, 0, keepdims=True)
            weights_ref[pair] = probs.astype(BF16)
            d_scores_ref[pair] = (probs * (d_probs - total) * factor).astype(BF16)
        for pair in range(len(pairs)):
            start, first, both, query, key, value, d_rows = parts(pair)
            weights, d_scores = weights_ref[pair], d_scores_ref[pair]
            put(left, rows, width + start, both, per_query(weights, value, first))
            put(right, rows, start, both, per_query(d_scores, key, first))
            put(right, rows, width + start, both, dot(d_scores, query))
            put(right, rows, 2 * width + start, both, dot(weights, d_rows))
        return carry

    lax.fori_loop(0, x.shape[0] // block, one_block, 0)
    stores = [copies.start(left, left_out)]
    stores += unit_stores(copies, core_ref[1] & 1, width, right, unit_outs)
    d_modded = dot(right[:, 0 : 3 * width], wqkv[...], NT)
    d_middle = up[...].astype(F32) + norm_backward(
        d_modded, normed[...], inverse, mod_ref[video, 4:5, :]
    )
    d_middle_ref[...] = piece_rows(dot(scatter_ref[...], d_middle.astype(BF16)), n)
    projected = dot(left[:, width:], wout[...])
    out = (x[...].astype(F32) + mod_ref[video, 5:6, :] * projected).astype(BF16)
    pieces = dot(scatter_out_ref[...], out)
    if video:
        pieces += others_ref[...].astype(F32).reshape(pieces.shape)
    block_out_ref[...] = piece_rows(pieces, n)
    for store in stores:
        store.wait()


def space_backward_kernel(
    block, video, core_ref, up_ref, mod_ref, wout_ref, gather_ref, packed_ref, weights_ref, *refs
):
    d_middle_ref, *unit_outs = refs[-10:-7]
    d_out, right, packed, wout, d_probs_ref, d_scores_ref, sems = refs[-7:]
    width = wout.shape[0]
    size = width // HEADS
    factor = size ** (-0.5)
    copies = Copies(sems)
    load_out = copies.start(wout_ref, wout)
    load_packed = copies.start(packed_ref, packed)
    up = dot(gather_ref[...], frame_rows(up_ref[...]))
    d_middle_ref[...] = up.astype(BF16)
    right[:, 3 * width :] = (mod_ref[video, 2:3, :] * up).astype(BF16)
    load_out.wait()
    d_out[...] = dot(right[:, 3 * width :], wout[...], NT).astype(BF16)
    load_packed.wait()
    pairs = pair_windows(width)

    def one_block(g, carry):
        rows = pl.multiple_of(g * block, 16)
        at = pl.ds(rows, block)
        for pair, (start, span, offset) in enumerate(pairs):
            first, both = pair_masks(block, span, offset, size)
            d_rows = two_heads(d_out[at, pl.ds(start, span)], first, both)
            d_probs_ref[pair] = dot(packed[at, pl.ds(2 * width + start, span)], d_rows, NT)
        for pair in range(len(pairs)):
            probs = weights_ref[g * len(pairs) + pair].astype(F32)
            d_probs = d_probs_ref[pair]
            total = jnp.sum(probs * d_probs, 0, keepdims=True) / jnp.sum(probs, 0, keepdims=True)
            d_scores_ref[pair] = (probs * (d_probs - total) * factor).astype(BF16)
        for pair, (start, span, offset) in enumerate(pairs):
            first, both = pair_masks(block, span, offset, size)
            query = two_heads(packed[at, pl.ds(start, span)], first, both)
            key = packed[at, pl.ds(width + start, span)]
            d_rows = two_heads(d_out[at, pl.ds(start, span)], first, both)
            weights, d_scores = weights_ref[g * len(pairs) + pair], d_scores_ref[pair]
            put(right, rows, start, both, per_query(d_scores, key, first))
            put(right, rows, width + start, both, dot(d_scores, query))
            put(right, rows, 2 * width + start, both, dot(weights, d_rows))
        return carry

    lax.fori_loop(0, d_out.shape[0] // block, one_block, 0)
    for store in unit_stores(copies, core_ref[1] & 1, width, right, unit_outs):
        store.wait()


def grad_input_kernel(video, right_ref, d_middle_ref, x_ref, mod_ref, wqkv_ref, *refs):
    out_ref, d_packed, wqkv, sems = refs[-4:]
    width = out_ref.shape[1]
    copies = Copies(sems)
    parts = [pl.ds(part * width, width) for part in range(3)]
    loads = [
        (copies.start(right_ref.at[:, at], d_packed.at[:, at]),
         copies.start(wqkv_ref.at[:, at], wqkv.at[:, at]))
        for at in parts
    ]
    normed, inverse = norm_stats(x_ref[video].astype(F32))
    d_modded = 0.0
    for at, load in zip(parts, loads):
        for one in load:
            one.wait()
        d_modded += dot(d_packed[:, at], wqkv[:, at], NT)
    d_tokens = norm_backward(d_modded, normed, inverse, mod_ref[video, 1:2, :])
    out_ref[...] = (d_middle_ref[...].astype(F32) + d_tokens).astype(BF16)


def bit_of(place_ref, axis, bit):
    return (place_ref[0 if axis == "dp" else 1] >> bit) & 1


def emit_halves(rows, inner, mine, kept_ref, sent_ref):
    columns = kept_ref.shape[2]
    for outer in range(kept_ref.shape[0]):
        low = rows[2 * outer * inner : (2 * outer + 1) * inner, :columns]
        high = rows[(2 * outer + 1) * inner : (2 * outer + 2) * inner, :columns]
        kept_ref[outer] = jnp.where(mine == 0, low, high).astype(BF16)
        sent_ref[outer] = jnp.where(mine == 0, high, low).astype(BF16)


def weight_kernel(videos, cuts, steps, grad_scale, place_ref, *refs):
    left_own, left_got, right_own, right_got = [
        refs[at * videos : (at + 1) * videos] for at in range(4)
    ]
    count = 2 * len(cuts)
    outs, scratch = refs[-4 - 2 * count : -4 - count], refs[-4 - count : -4]
    left_rows, right_rows, total, sems = refs[-4:]
    width = left_rows.shape[1] // 2
    tokens = left_own[0].shape[0]
    copies = Copies(sems)
    core = place_ref[1] & 1
    own = pl.multiple_of(core * (2 * width), 128)

    def load(unit):
        now = []
        at = pl.ds(unit * width, width)
        mine = pl.ds(pl.multiple_of(own + unit * width, 128), width)
        for video in range(videos):
            for place, (left, right, columns) in enumerate(
                (
                    (left_own[video], right_own[video], mine),
                    (left_got[video], right_got[video], at),
                )
            ):
                rows = pl.ds((2 * video + place) * tokens, tokens)
                now.append(copies.start(left.at[:, at], left_rows.at[rows, at]))
                now.append(copies.start(right.at[:, columns], right_rows.at[rows, at]))
        return now

    waits = [load(0), load(1)]
    done, stores = 0, []
    for part, ((low, high), (axis, bit, inner)) in enumerate(zip(cuts, steps)):
        for unit in range(2):
            start, stop = max(low, unit * width), min(high, (unit + 1) * width)
            if start >= stop:
                continue
            while done <= unit:
                for wait in waits[done]:
                    wait.wait()
                done += 1
            column = pl.multiple_of(core * width, 128) if unit else 0
            left = left_rows[:, pl.ds(column, width)]
            total[:, start - low : stop - low] = (
                dot(left, right_rows[:, start:stop], TN) * grad_scale
            )
        pair = slice(2 * part, 2 * part + 2)
        emit_halves(total, inner, bit_of(place_ref, axis, bit), *scratch[pair])
        stores += [copies.start(a, b) for a, b in zip(scratch[pair], outs[pair])]
    for store in stores:
        store.wait()


def add_got(total, kept, got):
    each, columns = kept.shape[1:]
    for outer in range(kept.shape[0]):
        total[outer * each : (outer + 1) * each, :columns] = kept[outer].astype(F32) + got[
            outer
        ].astype(F32)


def stage_kernel(steps, place_ref, *refs):
    count = len(steps)
    total, outs = refs[-1], refs[-1 - 2 * count : -1]
    for part, (axis, bit, inner) in enumerate(steps):
        add_got(total, refs[part], refs[count + part])
        emit_halves(
            total, inner, bit_of(place_ref, axis, bit), outs[2 * part], outs[2 * part + 1]
        )


def last_stage_kernel(bit, cuts, place_ref, *refs):
    count = len(cuts)
    outs, total = refs[-5:-1], refs[-1]
    rows = outs[0].shape[0]
    mine, core = bit_of(place_ref, "seq", bit) == 0, (place_ref[1] & 1) == 0
    for part, (start, stop) in enumerate(cuts):
        add_got(total, refs[part], refs[count + part])
        low, high = total[: 2 * rows, : stop - start], total[2 * rows : 4 * rows, : stop - start]
        near, far = jnp.where(mine, low, high), jnp.where(mine, high, low)
        for place, half in enumerate((near, far)):
            first, second = half[:rows], half[rows:]
            same, other = jnp.where(core, first, second), jnp.where(core, second, first)
            outs[2 * place][:, start:stop] = same.astype(BF16)
            outs[2 * place + 1][:, start:stop] = other.astype(BF16)


def far_stage_kernel(bit, cuts, place_ref, *refs):
    count = len(cuts)
    (near_out, far_out), total = refs[-3:-1], refs[-1]
    rows = near_out.shape[0]
    mine = bit_of(place_ref, "seq", bit) == 0
    for part, (start, stop) in enumerate(cuts):
        add_got(total, refs[part], refs[count + part])
        low, high = total[:rows, : stop - start], total[rows : 2 * rows, : stop - start]
        near_out[:, start:stop] = jnp.where(mine, low, high).astype(BF16)
        far_out[:, start:stop] = jnp.where(mine, high, low).astype(BF16)


def core_stage_kernel(place_ref, near_ref, got_ref, *refs):
    kept_out, sent_out = refs[-2:]
    rows = kept_out.shape[0]
    core = (place_ref[1] & 1) == 0
    total = near_ref[...].astype(F32) + got_ref[...].astype(F32)
    low, high = total[:rows], total[rows:]
    kept_out[...] = jnp.where(core, low, high).astype(BF16)
    sent_out[...] = jnp.where(core, high, low).astype(BF16)


def assemble_two_kernel(place_ref, kept_ref, got_ref, *refs):
    qkv_ref, out_ref = refs[-2:]
    width = out_ref.shape[1]
    core = (place_ref[1] & 1) == 0
    kept, got = kept_ref[...].astype(F32), got_ref[...].astype(F32)
    low = jnp.where(core, kept, got).astype(BF16)
    high = jnp.where(core, got, kept).astype(BF16)
    qkv_ref[:, : 2 * width] = low
    qkv_ref[:, 2 * width :] = high[:, :width]
    out_ref[...] = high[:, width:]


def assemble_kernel(place_ref, *refs):
    near, far, near_other, far_other = [ref[...].astype(F32) for ref in refs[:4]]
    qkv_ref, out_ref = refs[-2:]
    width = out_ref.shape[1]
    core = (place_ref[1] & 1) == 0
    mine, others = near + far, near_other + far_other
    low = jnp.where(core, mine, others).astype(BF16)
    high = jnp.where(core, others, mine).astype(BF16)
    qkv_ref[:, : 2 * width] = low
    qkv_ref[:, 2 * width :] = high[:, :width]
    out_ref[...] = high[:, width:]


def swap(x, axis, mask):
    size = lax.axis_size(axis)
    return lax.ppermute(x, axis, [(i, i ^ mask) for i in range(size)])


class Reduction:
    def __init__(self, place, width, late):
        dp_bits = [("dp", bit) for bit in range(lax.axis_size("dp").bit_length() - 1)]
        seq_bits = [("seq", bit) for bit in range(1, lax.axis_size("seq").bit_length() - 1)]
        if late:
            self.orders = (
                dp_bits + seq_bits,
                dp_bits[-1:] + seq_bits[:1] + dp_bits[:-1] + seq_bits[1:],
                seq_bits[:1] + dp_bits + seq_bits[1:],
            )
        else:
            self.orders = (dp_bits + seq_bits, dp_bits[::-1] + seq_bits)
        tiles = 2 * width // 128
        ends = [0, (tiles - tiles // 6) * 64, (tiles - tiles // 6) * 128] if late else [0, width]
        self.cuts = tuple(zip(ends, ends[1:] + [2 * width]))
        self.parts = len(self.orders)
        self.place, self.width, self.late = place, width, late
        self.columns = max(stop - start for start, stop in self.cuts)
        self.bits = dp_bits[::-1] + seq_bits[::-1]
        self.step = 0

    def next_steps(self):
        least = self.width >> len(self.bits)
        steps, shapes = [], []
        for order, (start, stop) in zip(self.orders, self.cuts):
            left = [bit for bit in self.bits if bit not in order[: self.step]]
            above = left.index(order[self.step])
            inner = least << (len(left) - above - 1)
            steps.append((*order[self.step], inner))
            shapes += 2 * [shaped(1 << above, inner, stop - start)]
        return tuple(steps), tuple(shapes)

    def send(self, halves):
        self.kept = halves[0::2]
        self.got = [
            swap(half, order[self.step][0], 1 << order[self.step][1])
            for half, order in zip(halves[1::2], self.orders)
        ]
        self.step += 1

    def stage(self, deps=()):
        steps, shapes = self.next_steps()
        *halves, token = call(
            "stage" if self.late else "early_stage", 2, functools.partial(stage_kernel, steps),
            "s" + "v" * (2 * self.parts), shapes, "v" * len(shapes),
            [pltpu.VMEM((self.width >> self.step, self.columns), F32)],
        )(self.place, *self.kept, *self.got, deps=deps)
        self.send(halves)
        return token

    def last_stage(self, deps=()):
        while self.step < len(self.bits) - 1:
            self.stage()
        bit = self.orders[0][-1][1]
        rows = self.width >> (len(self.bits) + 1)
        near, near_other, far, far_other, token = call(
            "last_stage", 1, functools.partial(last_stage_kernel, bit, self.cuts),
            "s" + "v" * (2 * self.parts), (shaped(rows, 2 * self.width),) * 4, "vvvv",
            [pltpu.VMEM((4 * rows, self.columns), F32)],
        )(self.place, *self.kept, *self.got, deps=deps)
        self.sums = (
            near, swap(far, "seq", 1 << bit), swap(near_other, "seq", 1),
            swap(far_other, "seq", (1 << bit) | 1),
        )
        return token

    def far_stage(self, deps=()):
        while self.step < len(self.bits) - 1:
            self.stage()
        bit = self.orders[0][-1][1]
        rows = self.width >> len(self.bits)
        near, far, token = call(
            "last_stage", 1, functools.partial(far_stage_kernel, bit, self.cuts),
            "s" + "v" * (2 * self.parts), (shaped(rows, 2 * self.width),) * 2, "vv",
            [pltpu.VMEM((2 * rows, self.columns), F32)],
        )(self.place, *self.kept, *self.got, deps=deps)
        self.sums = (near, swap(far, "seq", 1 << bit))
        return token

    def core_stage(self, deps=()):
        rows = self.width >> (len(self.bits) + 1)
        kept, sent, token = call(
            "core_stage", 1, core_stage_kernel, "svv", (shaped(rows, 2 * self.width),) * 2, "vv"
        )(self.place, *self.sums, deps=deps)
        self.sums = (kept, swap(sent, "seq", 1))
        return token

    def finish(self, deps=()):
        rows = self.sums[0].shape[0]
        return call(
            "assemble", 1, assemble_kernel if len(self.sums) == 4 else assemble_two_kernel,
            "s" + "v" * len(self.sums),
            (shaped(rows, 3 * self.width), shaped(rows, self.width)), "vv",
        )(self.place, *self.sums, deps=deps)


def shards(frames_in, modulation, spatial_qkv, spatial_out, temporal_qkv, temporal_out, cotangent):
    n = lax.axis_size("seq")
    videos, frames, patches, width = frames_in.shape
    all_frames = frames * n
    tokens = frames * patches
    own_patches = patches // n
    rows = frames * own_patches
    padded = -(-rows // 8) * 8
    time_block = 6 * all_frames if own_patches % 6 == 0 else 3 * all_frames
    core = jnp.stack([lax.axis_index("dp"), lax.axis_index("seq")]).astype(jnp.int32)

    joint_padded = -(-videos * rows // 8) * 8
    to_pieces = np.zeros((n * padded, tokens), np.float32)
    to_joint = np.zeros((videos, n * joint_padded, tokens), np.float32)
    by_patch = np.zeros((tokens, n * padded), np.float32)
    joint_by_patch = np.zeros((videos, tokens, n * joint_padded), np.float32)
    for device in range(n):
        for f in range(frames):
            for p in range(own_patches):
                inside = f * own_patches + p
                before = f * patches + device * own_patches + p
                after = p * all_frames + device * frames + f
                to_pieces[device * padded + inside, before] = 1
                by_patch[after, device * padded + inside] = 1
                for v in range(videos):
                    place = device * joint_padded + v * rows + inside
                    to_joint[v, place, before] = 1
                    joint_by_patch[v, after, place] = 1
    from_joint = jnp.asarray(np.concatenate(list(to_joint), 1).T, BF16)
    to_pieces, from_pieces = jnp.asarray(to_pieces, BF16), jnp.asarray(to_pieces.T, BF16)
    to_joint = [jnp.asarray(m, BF16) for m in to_joint]
    by_patch, from_patch = jnp.asarray(by_patch, BF16), jnp.asarray(by_patch.T, BF16)
    joint_from_patch = [jnp.asarray(m.T, BF16) for m in joint_by_patch]
    joint_by_patch = [jnp.asarray(m, BF16) for m in joint_by_patch]

    def exchange(pieces):
        return lax.all_to_all(pieces, "seq", split_axis=0, concat_axis=0, tiled=True)

    piece = shaped(n, padded, width)
    joint_piece = shaped(n, joint_padded, width)
    row = shaped(tokens, width)
    two, three, four = [shaped(tokens, count * width) for count in (2, 3, 4)]
    all_rows = shaped(videos, tokens, width)
    weights_shape = (frames * (HEADS // 2), patches, 2 * patches)

    def vmem(*shape, dtype=BF16):
        return pltpu.VMEM(shape, dtype)

    def sems(count):
        return pltpu.SemaphoreType.DMA((count,))

    weight_refs = [vmem(width, 3 * width), vmem(width, width)]
    x = frames_in.reshape(videos, tokens, width)
    cot = cotangent.reshape(videos, tokens, width)

    def exchange_units(units):
        return swap(units, "seq", 1)

    cot_sent, token = call("split", 3, functools.partial(split_kernel, n), "vv", (piece,), "v")(
        cot, to_pieces
    )
    cot_pieces = exchange(cot_sent)
    deps = [token]
    saved, arrived = [], []
    for v in range(videos):
        sent, *keep, token = call(
            "space_forward", 14, functools.partial(space_forward_kernel, n, patches, v),
            "aavaavv",
            (joint_piece if v else piece, three, two, shaped(*weights_shape)),
            "vaaa",
            [
                vmem(tokens, width), vmem(tokens, width), vmem(tokens, 2 * width),
                vmem(tokens, 3 * width), vmem(*weights_shape), *weight_refs,
                vmem(HEADS // 2, patches, 2 * patches, dtype=F32), sems(9),
            ],
        )(
            x, cot, modulation, spatial_qkv, spatial_out, to_joint[0] if v else to_pieces,
            to_joint[1], deps=deps,
        )
        deps = [token, cot_pieces]
        arrived.append(exchange(sent))
        saved.append((*keep, exchange_units(keep[1])))

    returned, time_units, out_sent = [], [], core
    for v in range(videos):
        d_middle, out_sent, left, sent, right, token = call(
            "time", 25, functools.partial(time_kernel, n, time_block, all_frames, v),
            "svvvaavvvv" + ("v" if v else "a"),
            (piece, joint_piece, two, two, four),
            "vvaaa",
            [
                vmem(tokens, width, dtype=F32), vmem(tokens, width), vmem(tokens, width),
                vmem(tokens, 2 * width), vmem(tokens, 3 * width), vmem(tokens, width),
                vmem(tokens, 4 * width), *weight_refs,
                *[vmem(HEADS // 2, time_block, 2 * time_block, dtype=d) for d in (F32, F32, BF16, BF16)],
                sems(9),
            ],
        )(
            core, arrived[v], arrived[v] if v else cot_pieces, modulation, temporal_qkv,
            temporal_out, joint_by_patch[0] if v else by_patch,
            joint_by_patch[1] if v else by_patch, from_patch, joint_from_patch[v], out_sent,
            deps=deps,
        )
        deps = [token]
        returned.append(exchange(d_middle))
        time_units.append((left, exchange_units(left), right, exchange_units(sent)))

    grad_scale = (videos * lax.axis_size("dp") * all_frames * patches) ** (-0.5)

    def weights(units, late, deps=()):
        reduction = Reduction(core, width, late)
        steps, shapes = reduction.next_steps()
        operands = [one for kind in zip(*units) for one in kind]
        *halves, token = call(
            "weights", 10,
            functools.partial(weight_kernel, videos, reduction.cuts, steps, grad_scale),
            "s" + "a" * (4 * videos), shapes, "a" * len(shapes),
            [vmem(*half.shape) for half in shapes] + [
                vmem(2 * videos * tokens, 2 * width), vmem(2 * videos * tokens, 2 * width),
                vmem(width, reduction.columns, dtype=F32), sems(8 * videos + len(shapes)),
            ],
        )(core, *operands, deps=deps)
        reduction.send(halves)
        return reduction, token

    def grad_of(video, units, d_middle, deps=()):
        return call(
            "grad_input", 8, functools.partial(grad_input_kernel, video), "avvva", (row,), "v",
            [vmem(tokens, 3 * width), vmem(width, 3 * width), sems(6)],
        )(units[2], d_middle, x, modulation, spatial_qkv, deps=deps)

    d_middles, space_units = [], []
    for v in range(videos):
        packed, left, weights_saved, left_got = saved[v]
        d_middle, sent, right, token = call(
            "space_backward", 15, functools.partial(space_backward_kernel, patches, v),
            "svvavav",
            (row, two, four),
            "vaa",
            [
                vmem(tokens, width), vmem(tokens, 4 * width), vmem(tokens, 3 * width),
                vmem(width, width),
                *[vmem(HEADS // 2, patches, 2 * patches, dtype=d) for d in (F32, BF16)], sems(4),
            ],
        )(
            core, returned[v], modulation, spatial_out, from_pieces, packed, weights_saved,
            deps=[*deps, left_got],
        )
        if v == 0:
            time_sum, began = weights(time_units, False, deps=[token])
            deps = [began]
            out_back = exchange(out_sent)
        d_middles.append(d_middle)
        space_units.append((left, left_got, right, exchange_units(sent)))
    token = time_sum.stage(deps=[token])
    space_sum, token = weights(space_units, True, deps=[token])
    token = time_sum.stage(deps=[token])
    grad_input = []
    for v in range(videos):
        one_grad, token = grad_of(
            v, space_units[v], d_middles[v], deps=[token, out_back] if v else [token]
        )
        grad_input.append(one_grad)
    token = time_sum.far_stage(deps=[token])
    token = space_sum.stage(deps=[token])
    block_out, grad_input, token = call(
        "join", 4, join_kernel, "vv" + "v" * videos, (all_rows, all_rows), "vv"
    )(out_back, from_joint, *grad_input, deps=[token])
    token = space_sum.stage(deps=[token])
    token = time_sum.core_stage(deps=[token])
    token = space_sum.last_stage(deps=[token])
    *grad_time, token = time_sum.finish(deps=[token])
    *grad_space, _ = space_sum.finish(deps=[token])
    return (
        block_out.reshape(frames_in.shape), grad_input.reshape(frames_in.shape),
        *grad_space, *grad_time,
    )


def solution(mesh):
    return jax.shard_map(
        shards,
        mesh=mesh,
        in_specs=(
            P("dp", "seq", None, None),
            P("dp", None, None),
            P(),
            P(),
            P(),
            P(),
            P("dp", "seq", None, None),
        ),
        out_specs=(
            P("dp", "seq", None, None),
            P("dp", "seq", None, None),
            P(("dp", "seq"), None),
            P(("dp", "seq"), None),
            P(("dp", "seq"), None),
            P(("dp", "seq"), None),
        ),
        check_vma=False,
    )
```
